128 devices in a mesh: grp: 8 (over x, core), dev: 16 (over y, z).
Axes of the slice: x: 4, y: 4, z: 4, core: 2. Of those that a mesh axis runs over, the one named last changes fastest.
Arguments:
- emission: float32 [64, 524288], P(None, ('grp', 'dev')), may hold values from 0.2 to 2
- positions: float32 [3, 524288], P(None, ('grp', 'dev')), may hold values from -5 to 5
- normals: float32 [3, 524288], P(None, ('grp', 'dev')), may hold values from -3 to 3
- areas: float32 [524288], P(('grp', 'dev')), may hold values from 0.5 to 4
- material: int32 [524288], P(('grp', 'dev')), may hold values from 0 to 15
- reflect: float32 [64, 16], replicated, may hold values from 0.2 to 0.8
- pair_local: int32 [16384], P(('grp', 'dev')), may hold values from 0 to 31
- pair_device: int32 [16384, 1], P(('grp', 'dev')), may hold values from 0 to 127; in each aligned block of 128 rows (0 to 127, 128 to 255, ...) at most 2 rows name the same one
- pair_block: int32 [16384], P(('grp', 'dev')), may hold values from 0 to 31
Outputs:
- radiosity: float32 [64, 524288], P(None, ('grp', 'dev'))
The draws below stay inside these ranges and needn't reach their ends.
Inputs may be any that keep to these rules, and one draw needn't show every extreme that they name: `pair_device`: among the 128 pairs of one device, at most 2 name the same device; some device's pairs name one device exactly 2 times.
All inputs are finite; a program needn't handle non-finite values.
Results may differ from the reference program's by a relative error of at most 0.00055.
Values may be sent and summed in bfloat16 or wider, within the bound.
A program may use at most 128 MiB of HBM per device.

```python
import math
import jax
import jax.numpy as jnp
import numpy as np
from jax import lax

NB = 64
BLK = 128
NCLASS = 16
SWEEPS = 2
BLK_DEV = 32
PAIRS_DEV = 128
CAP = 2
NBLOCKS = 4096
P_SIZE = 524288
PAIRS = 16384
DEVICES = 128


def touch_ends(drawn, key, least, top_value):
    longest = drawn.shape.index(max(drawn.shape))
    spots = []
    for shift in (0, 1):
        where = [jax.random.randint(jax.random.fold_in(key, axis), (), 0, length) for axis, length in enumerate(drawn.shape)]
        where[longest] = (where[longest] + shift) % drawn.shape[longest]
        spots.append(tuple(where))
    return drawn.at[spots[0]].set(least).at[spots[1]].set(top_value)


def levels(rng, dims, cuts, smallest, top_value):
    level = 1.0
    for dim, parts in cuts:
        steps = jax.random.uniform(jax.random.fold_in(jax.random.fold_in(rng, 6), dim), (parts,), jnp.float32, smallest / len(cuts), top_value / len(cuts))
        level = level * jnp.repeat(jnp.exp(steps), dims[dim] // parts).reshape((-1,) + (1,) * (len(dims) - 1 - dim))
    return level


def routed_block(key, own, number, rows, amount, top, reach, skew):
    sequence = jax.random.permutation(key, amount)
    packed, common = shares(amount, rows * top, reach, skew, True), shares(amount, rows * top, reach, skew, False)
    places = jnp.arange(amount)

    def named(lengths, rotation):
        used = int((lengths > 0).sum())
        fixed = max(1, used // 4)
        passed = fixed + (places - fixed + rotation * (used - fixed)) % max(1, amount - fixed)
        return jnp.zeros((amount,), jnp.int32).at[sequence[jnp.where(places < fixed, places, passed)]].set(jnp.asarray(lengths, jnp.int32))

    lengths = jnp.where(number % 4 == 0, named(packed, number // 4), named(common, number - number // 4 - 1))
    mixed = jax.random.permutation(jax.random.fold_in(own, 3), amount)
    donor, sink = mixed[0:amount // 2 * 2:2], mixed[1:amount // 2 * 2:2]
    slack = jnp.minimum(lengths[donor] - 1, reach - lengths[sink]) // 2
    slack = jnp.where((donor == sequence[0]) | (sink == sequence[0]) | (lengths[sink] == 0), 0, jnp.maximum(slack, 0))
    passed = jax.random.randint(jax.random.fold_in(own, 4), (amount // 2,), 0, 1 << 20) % (slack + 1)
    lengths = lengths.at[donor].add(-passed).at[sink].add(passed)
    labels = jnp.searchsorted(jnp.cumsum(lengths), jnp.arange(rows * top), side="right").astype(jnp.int32)
    table = labels.reshape(top, rows).T
    table = table[jax.random.permutation(jax.random.fold_in(own, 1), rows)]
    rotation = jax.random.randint(jax.random.fold_in(own, 2), (rows, 1), 0, top)
    return jnp.take_along_axis(table, (jnp.arange(top)[None, :] + rotation) % top, axis=1)


def shares(count, total, most, lean, full):
    portions = [(1 << 20) // math.isqrt(grade ** lean) + 1 for grade in range(1, count + 1)]
    largest = most if full else min(most, max(-(-total // count), total * portions[0] // sum(portions)))
    least = 1 if total - largest >= count - 1 else 0
    holding, surplus = [largest] + [least] * (count - 1), total - largest - least * (count - 1)
    while surplus > 0:
        movable = [i for i in range(1, count) if holding[i] < largest] or [i for i in range(1, count) if holding[i] < most]
        mass, left = sum([portions[i] for i in movable]), surplus
        for i in movable:
            more = min(most - holding[i], max(1, left * portions[i] // mass), surplus)
            holding[i] = holding[i] + more
            surplus = surplus - more
    return np.array(holding)


def noise(rng, dims, width, limit, cuts=(), kind=jnp.bfloat16):
    entries = jax.random.normal(rng, dims, jnp.float32) * width
    if len(cuts) > 0:
        entries = levels(rng, dims, cuts, -0.22, 0.18) * entries
    return jnp.clip(entries, min=-limit, max=limit).astype(kind)


def setup_inputs(seed: int = 0) -> dict:
    seeds = jax.random.split(jax.random.key(seed), 10)
    emission = jnp.clip(jnp.exp(math.log(2.0) - 2.3025851 * jax.random.uniform(seeds[0], (NB, P_SIZE), jnp.float32) ** levels(seeds[0], (NB, P_SIZE), ((1, 128),), -0.2, 0.2)), 0.2, 2.0)
    positions = noise(seeds[1], (3, P_SIZE), 1.0, 5.0, ((1, 128),), jnp.float32)
    normals = noise(seeds[2], (3, P_SIZE), 0.6, 3.0, ((1, 128),), jnp.float32)
    areas = jnp.clip(jnp.exp(math.log(4.0) - 2.0794415 * jax.random.uniform(seeds[3], (P_SIZE,), jnp.float32) ** levels(seeds[3], (P_SIZE,), ((0, 128),), -0.2, 0.2)), 0.5, 4.0)
    material = touch_ends(jax.random.randint(seeds[4], (P_SIZE,), 0, NCLASS), jax.random.fold_in(seeds[4], 1), 0, NCLASS - 1).astype(jnp.int32)
    reflect = jnp.clip(jax.random.uniform(seeds[5], (NB, NCLASS), jnp.float32, 0.2, 0.8), 0.2, 0.8)
    pair_local = touch_ends(jax.random.randint(seeds[6], (PAIRS,), 0, BLK_DEV), jax.random.fold_in(seeds[6], 1), 0, BLK_DEV - 1).astype(jnp.int32)
    pair_device_keys = jax.random.split(jax.random.fold_in(seeds[7], 1), PAIRS // PAIRS_DEV)
    pair_device_turns = jax.random.permutation(jax.random.fold_in(seeds[7], 3), PAIRS // PAIRS_DEV)
    pair_device = jax.vmap(lambda own, number: routed_block(jax.random.fold_in(seeds[7], 2), own, number, PAIRS_DEV, DEVICES, 1, CAP, 2))(pair_device_keys, pair_device_turns).reshape((PAIRS, 1))
    pair_block = touch_ends(jax.random.randint(seeds[8], (PAIRS,), 0, BLK_DEV), jax.random.fold_in(seeds[8], 1), 0, BLK_DEV - 1).astype(jnp.int32)
    return dict(emission=emission, positions=positions, normals=normals, areas=areas, material=material, reflect=reflect, pair_local=pair_local, pair_device=pair_device, pair_block=pair_block)


softening = 0.5


def view_tile(near, far):
    distance_sq = softening
    facing_near = 0.0
    facing_far = 0.0
    for axis_index in range(3):
        offset = far[:, axis_index, None, :] - near[:, axis_index, :, None]
        distance_sq = distance_sq + offset * offset
        facing_near = facing_near + near[:, 3 + axis_index, :, None] * offset
        facing_far = facing_far - far[:, 3 + axis_index, None, :] * offset
    return jnp.maximum(facing_near, 0.0) * jnp.maximum(facing_far, 0.0) / (math.pi * distance_sq * distance_sq)


def reference(emission, positions, normals, areas, material, reflect, pair_local, pair_device, pair_block):
    geometry = jnp.concatenate([positions, normals, areas[None, :]], 0)
    geometry = geometry.reshape(7, NBLOCKS, BLK).transpose(1, 0, 2)
    owner = jnp.arange(PAIRS, dtype=jnp.int32) // PAIRS_DEV
    near_block = (owner * BLK_DEV + pair_local).astype(jnp.int32)
    far_block = (pair_device[:, 0] * BLK_DEV + pair_block).astype(jnp.int32)
    near_rows = near_block.reshape(DEVICES, PAIRS_DEV)
    far_rows = far_block.reshape(DEVICES, PAIRS_DEV)
    class_hot = (jnp.arange(NCLASS, dtype=jnp.int32)[:, None] == material[None, :]).astype(jnp.float32)
    albedo = jnp.dot(reflect, class_hot, precision=lax.Precision.HIGHEST)
    albedo = albedo.reshape(NB, NBLOCKS, BLK).transpose(1, 0, 2)
    source = emission.reshape(NB, NBLOCKS, BLK).transpose(1, 0, 2)
    area_blocks = geometry[:, 6, :]
    current = source
    for sweep_index in range(SWEEPS):
        scaled = lax.optimization_barrier((current * area_blocks[:, None, :]).astype(jnp.bfloat16))

        def one_step(total, rows):
            near_index, far_index = rows
            kernel = view_tile(geometry[near_index], geometry[far_index]).astype(jnp.bfloat16)
            kernel = lax.optimization_barrier(kernel).astype(jnp.float32)
            to_near = jnp.einsum("pnj,pij->pni", scaled[far_index].astype(jnp.float32), kernel,
                                 precision=lax.Precision.HIGHEST)
            to_far = jnp.einsum("pni,pij->pnj", scaled[near_index].astype(jnp.float32), kernel,
                                precision=lax.Precision.HIGHEST)
            total = total.at[near_index].add(to_near).at[far_index].add(to_far)
            return total, None

        empty = jnp.zeros((NBLOCKS, NB, BLK), jnp.float32)
        gathered, _ = lax.scan(one_step, empty, (near_rows, far_rows))
        current = source + albedo * gathered
    return current.transpose(1, 0, 2).reshape(NB, P_SIZE)
```

```python
import math

import jax
import jax.numpy as jnp
from jax import lax
from jax.experimental import pallas as pl
from jax.experimental.pallas import tpu as pltpu
from jax.sharding import PartitionSpec as P

BLK = 128
SWEEPS = 2
AXES = ("grp", "dev")
GROUP = 8
softening = 0.5


def pack_kernel(index_ref, current_ref, areas_ref, out_ref, scaled_ref):
    blocks = scaled_ref.shape[0]

    @pl.when(pl.program_id(0) == 0)
    def _():
        for block in range(blocks):
            lanes = pl.ds(block * BLK, BLK)
            scaled_ref[block] = (current_ref[:, lanes] * areas_ref[:, lanes]).astype(jnp.bfloat16)

    base = pl.program_id(0) * out_ref.shape[0]
    for slot in range(out_ref.shape[0]):
        out_ref[slot] = scaled_ref[index_ref[base + slot]]


def pack(index, current, areas):
    slots = index.shape[0]
    bands, patches = current.shape
    step = min(slots, 32)
    return pl.pallas_call(
        pack_kernel,
        grid_spec=pltpu.PrefetchScalarGridSpec(
            num_scalar_prefetch=1,
            grid=(slots // step,),
            in_specs=[
                pl.BlockSpec((bands, patches), lambda i, index: (0, 0)),
                pl.BlockSpec((1, patches), lambda i, index: (0, 0)),
            ],
            out_specs=pl.BlockSpec((step, bands, BLK), lambda i, index: (i, 0, 0)),
            scratch_shapes=[pltpu.VMEM((patches // BLK, bands, BLK), jnp.bfloat16)],
        ),
        out_shape=jax.ShapeDtypeStruct((slots, bands, BLK), jnp.bfloat16),
        compiler_params=pltpu.CompilerParams(vmem_limit_bytes=32 << 20),
        cost_estimate=pl.CostEstimate(
            flops=0, bytes_accessed=slots * bands * BLK * 4, transcendentals=0
        ),
        name="pack",
    )(index, current, areas)


def tiles_kernel(mine_ref, other_ref, own_geometry_ref, geometry_ref, out_ref):
    base = pl.program_id(0) * out_ref.shape[0]
    for slot in range(out_ref.shape[0]):
        mine = mine_ref[base + slot]
        other = other_ref[base + slot]

        @pl.when(mine >= 0)
        def _():
            far = geometry_ref[other]
            far = jnp.concatenate([far, jnp.zeros((2, BLK), jnp.float32)], 0).T
            near = own_geometry_ref[mine]
            distance_sq = softening
            facing_near = 0.0
            facing_far = 0.0
            for axis_index in range(3):
                offset = far[:, axis_index : axis_index + 1] - near[axis_index : axis_index + 1]
                distance_sq = distance_sq + offset * offset
                facing_near = facing_near + near[3 + axis_index : 4 + axis_index] * offset
                facing_far = facing_far - far[:, 3 + axis_index : 4 + axis_index] * offset
            out_ref[slot] = (
                jnp.maximum(facing_near, 0.0)
                * jnp.maximum(facing_far, 0.0)
                / (math.pi * distance_sq * distance_sq)
            ).astype(jnp.bfloat16)


def tiles(mine, other, own_geometry, geometry):
    slots = mine.shape[0]
    step = GROUP
    return pl.pallas_call(
        tiles_kernel,
        grid_spec=pltpu.PrefetchScalarGridSpec(
            num_scalar_prefetch=2,
            grid=(slots // step,),
            in_specs=[
                pl.BlockSpec(own_geometry.shape, lambda i, mine, other: (0, 0, 0)),
                pl.BlockSpec(
                    geometry.shape, lambda i, mine, other: (0, 0, 0), pipeline_mode=pl.Buffered(1)
                ),
            ],
            out_specs=pl.BlockSpec((step, BLK, BLK), lambda i, mine, other: (i, 0, 0)),
        ),
        out_shape=jax.ShapeDtypeStruct((slots, BLK, BLK), jnp.bfloat16),
        compiler_params=pltpu.CompilerParams(vmem_limit_bytes=40 << 20),
        cost_estimate=pl.CostEstimate(
            flops=slots * BLK * BLK * 30, bytes_accessed=slots * BLK * BLK * 2, transcendentals=0
        ),
        name="tiles",
    )(mine, other, own_geometry, geometry)


def apply_kernel(mine_ref, values_ref, tiles_ref, start_ref, out_ref):
    @pl.when(pl.program_id(0) == 0)
    def _():
        out_ref[...] = start_ref[...]

    base = pl.program_id(0) * values_ref.shape[0]
    for slot in range(values_ref.shape[0]):
        mine = mine_ref[base + slot]

        @pl.when(mine >= 0)
        def _():
            lanes = pl.ds(pl.multiple_of(mine * BLK, BLK), BLK)
            out_ref[:, lanes] += jnp.dot(
                values_ref[slot], tiles_ref[slot], preferred_element_type=jnp.float32
            )


def apply(mine, values, kernel_tiles, start):
    slots, bands, _ = values.shape
    step = GROUP
    whole = pl.BlockSpec(start.shape, lambda i, mine: (0, 0))
    return pl.pallas_call(
        apply_kernel,
        grid_spec=pltpu.PrefetchScalarGridSpec(
            num_scalar_prefetch=1,
            grid=(slots // step,),
            in_specs=[
                pl.BlockSpec((step, bands, BLK), lambda i, mine: (i, 0, 0)),
                pl.BlockSpec((step, BLK, BLK), lambda i, mine: (i, 0, 0)),
                whole,
            ],
            out_specs=whole,
        ),
        out_shape=jax.ShapeDtypeStruct(start.shape, jnp.float32),
        compiler_params=pltpu.CompilerParams(vmem_limit_bytes=32 << 20),
        cost_estimate=pl.CostEstimate(
            flops=slots * bands * BLK * BLK * 2,
            bytes_accessed=slots * BLK * (bands + BLK) * 2,
            transcendentals=0,
        ),
        name="apply",
    )(mine, values, kernel_tiles, start)


def exchange(values):
    return lax.all_to_all(values, AXES, split_axis=0, concat_axis=0, tiled=True)


def on_device(
    emission, positions, normals, areas, material, reflect, pair_local, pair_device, pair_block
):
    bands, patches = emission.shape
    blocks = patches // BLK
    devices = lax.axis_size(AXES)
    me = lax.axis_index(AXES)
    pairs = pair_local.shape[0]
    areas = areas[None, :]

    target = pair_device[:, 0]
    order = jnp.arange(pairs, dtype=jnp.int32)
    earlier = (target[:, None] == target[None, :]) & (order[None, :] < order[:, None])
    slot = target * 2 + jnp.sum(earlier.astype(jnp.int32), 1)
    code = pair_block * blocks + pair_local
    own = jnp.max(
        jnp.where(
            slot[:, None] == jnp.arange(2 * devices, dtype=jnp.int32)[None, :], code[:, None], -1
        ),
        0,
    )
    everyone = lax.all_gather(own, AXES, axis=0, tiled=False).reshape(devices, devices, 2)
    asked = lax.dynamic_index_in_dim(everyone, me, 1, keepdims=False)
    own = own.reshape(devices, 2)

    geometry = jnp.concatenate([positions, normals], 0).reshape(6, blocks, BLK).transpose(1, 0, 2)
    all_geometry = lax.all_gather(geometry, AXES, axis=0, tiled=True)

    first_block = (jnp.arange(devices, dtype=jnp.int32) * blocks)[:, None]
    send_near = jnp.where(own >= 0, own % blocks, 0).reshape(-1)
    send_far = jnp.where(asked >= 0, asked // blocks, 0).reshape(-1)
    near_mine = jnp.where(asked >= 0, asked // blocks, -1).reshape(-1)
    near_other = (first_block + jnp.where(asked >= 0, asked % blocks, 0)).reshape(-1)
    far_mine = jnp.where(own >= 0, own % blocks, -1).reshape(-1)
    far_other = (first_block + jnp.where(own >= 0, own // blocks, 0)).reshape(-1)

    class_hot = (
        jnp.arange(reflect.shape[1], dtype=jnp.int32)[:, None] == material[None, :]
    ).astype(jnp.float32)
    albedo = jnp.dot(reflect, class_hot, precision=lax.Precision.HIGHEST)

    near_tiles = tiles(near_mine, near_other, geometry, all_geometry)
    far_tiles = tiles(far_mine, far_other, geometry, all_geometry)
    current = emission
    for sweep_index in range(SWEEPS):
        near_values = exchange(pack(send_near, current, areas))
        far_values = exchange(pack(send_far, current, areas))
        gathered = apply(near_mine, near_values, near_tiles, jnp.zeros_like(emission))
        gathered = apply(far_mine, far_values, far_tiles, gathered)
        current = emission + albedo * gathered
    return current


def solution(mesh):
    return jax.shard_map(
        on_device,
        mesh=mesh,
        in_specs=(
            P(None, AXES),
            P(None, AXES),
            P(None, AXES),
            P(AXES),
            P(AXES),
            P(),
            P(AXES),
            P(AXES, None),
            P(AXES),
        ),
        out_specs=P(None, AXES),
        check_vma=False,
    )
```

```python
import math

import jax
import jax.numpy as jnp
from jax import lax
from jax.experimental import pallas as pl
from jax.experimental.pallas import tpu as pltpu
from jax.sharding import PartitionSpec as P

BLK = 128
SWEEPS = 2
AXES = ("grp", "dev")
GROUP = 8
softening = 0.5


def pack_kernel(index_ref, current_ref, areas_ref, out_ref, scaled_ref):
    blocks = scaled_ref.shape[0]

    @pl.when(pl.program_id(0) == 0)
    def _():
        for block in range(blocks):
            lanes = pl.ds(block * BLK, BLK)
            scaled_ref[block] = (current_ref[:, lanes] * areas_ref[:, lanes]).astype(jnp.bfloat16)

    base = pl.program_id(0) * out_ref.shape[0]
    for slot in range(out_ref.shape[0]):
        out_ref[slot] = scaled_ref[index_ref[base + slot]]


def pack(index, current, areas):
    slots = index.shape[0]
    bands, patches = current.shape
    step = min(slots, 32)
    return pl.pallas_call(
        pack_kernel,
        grid_spec=pltpu.PrefetchScalarGridSpec(
            num_scalar_prefetch=1,
            grid=(slots // step,),
            in_specs=[
                pl.BlockSpec((bands, patches), lambda i, index: (0, 0)),
                pl.BlockSpec((1, patches), lambda i, index: (0, 0)),
            ],
            out_specs=pl.BlockSpec((step, bands, BLK), lambda i, index: (i, 0, 0)),
            scratch_shapes=[pltpu.VMEM((patches // BLK, bands, BLK), jnp.bfloat16)],
        ),
        out_shape=jax.ShapeDtypeStruct((slots, bands, BLK), jnp.bfloat16),
        compiler_params=pltpu.CompilerParams(vmem_limit_bytes=32 << 20),
        cost_estimate=pl.CostEstimate(
            flops=0, bytes_accessed=slots * bands * BLK * 4, transcendentals=0
        ),
        name="pack",
    )(index, current, areas)


def tiles_kernel(mine_ref, other_ref, own_geometry_ref, geometry_ref, out_ref):
    base = pl.program_id(0) * out_ref.shape[0]
    for slot in range(out_ref.shape[0]):
        mine = mine_ref[base + slot]
        other = other_ref[base + slot]

        @pl.when(mine >= 0)
        def _():
            far = geometry_ref[other]
            far = jnp.concatenate([far, jnp.zeros((2, BLK), jnp.float32)], 0).T
            near = own_geometry_ref[mine]
            distance_sq = softening
            facing_near = 0.0
            facing_far = 0.0
            for axis_index in range(3):
                offset = far[:, axis_index : axis_index + 1] - near[axis_index : axis_index + 1]
                distance_sq = distance_sq + offset * offset
                facing_near = facing_near + near[3 + axis_index : 4 + axis_index] * offset
                facing_far = facing_far - far[:, 3 + axis_index : 4 + axis_index] * offset
            out_ref[slot] = (
                jnp.maximum(facing_near, 0.0)
                * jnp.maximum(facing_far, 0.0)
                / (math.pi * distance_sq * distance_sq)
            ).astype(jnp.bfloat16)


def tiles(mine, other, own_geometry, geometry):
    slots = mine.shape[0]
    step = GROUP
    return pl.pallas_call(
        tiles_kernel,
        grid_spec=pltpu.PrefetchScalarGridSpec(
            num_scalar_prefetch=2,
            grid=(slots // step,),
            in_specs=[
                pl.BlockSpec(own_geometry.shape, lambda i, mine, other: (0, 0, 0)),
                pl.BlockSpec(
                    geometry.shape, lambda i, mine, other: (0, 0, 0), pipeline_mode=pl.Buffered(1)
                ),
            ],
            out_specs=pl.BlockSpec((step, BLK, BLK), lambda i, mine, other: (i, 0, 0)),
        ),
        out_shape=jax.ShapeDtypeStruct((slots, BLK, BLK), jnp.bfloat16),
        compiler_params=pltpu.CompilerParams(vmem_limit_bytes=40 << 20),
        cost_estimate=pl.CostEstimate(
            flops=slots * BLK * BLK * 30, bytes_accessed=slots * BLK * BLK * 2, transcendentals=0
        ),
        name="tiles",
    )(mine, other, own_geometry, geometry)


def apply_kernel(mine_ref, values_ref, tiles_ref, start_ref, out_ref):
    @pl.when(pl.program_id(0) == 0)
    def _():
        out_ref[...] = start_ref[...]

    base = pl.program_id(0) * values_ref.shape[0]
    for slot in range(values_ref.shape[0]):
        mine = mine_ref[base + slot]

        @pl.when(mine >= 0)
        def _():
            lanes = pl.ds(pl.multiple_of(mine * BLK, BLK), BLK)
            out_ref[:, lanes] += jnp.dot(
                values_ref[slot], tiles_ref[slot], preferred_element_type=jnp.float32
            )


def apply(mine, values, kernel_tiles, start):
    slots, bands, _ = values.shape
    step = GROUP
    whole = pl.BlockSpec(start.shape, lambda i, mine: (0, 0))
    return pl.pallas_call(
        apply_kernel,
        grid_spec=pltpu.PrefetchScalarGridSpec(
            num_scalar_prefetch=1,
            grid=(slots // step,),
            in_specs=[
                pl.BlockSpec((step, bands, BLK), lambda i, mine: (i, 0, 0)),
                pl.BlockSpec((step, BLK, BLK), lambda i, mine: (i, 0, 0)),
                whole,
            ],
            out_specs=whole,
        ),
        out_shape=jax.ShapeDtypeStruct(start.shape, jnp.float32),
        compiler_params=pltpu.CompilerParams(vmem_limit_bytes=32 << 20),
        cost_estimate=pl.CostEstimate(
            flops=slots * bands * BLK * BLK * 2,
            bytes_accessed=slots * BLK * (bands + BLK) * 2,
            transcendentals=0,
        ),
        name="apply",
    )(mine, values, kernel_tiles, start)


def torus_order():
    seen = set()
    groups = []
    for dx in range(4):
        for dy in range(4):
            for dz in range(4):
                for core in range(2):
                    group = []
                    for x, y, z in ((dx, dy, dz), (dy, dz, dx), (dz, dx, dy)):
                        for step in ((x, core, y, z), (-x % 4, core, -y % 4, -z % 4)):
                            if step not in seen and any(step):
                                seen.add(step)
                                group.append(step)
                    if group:
                        groups.append(group)
    groups.sort(key=lambda group: sum(min(v, 4 - v) for v in group[0][:1] + group[0][2:]))
    return [step for group in groups for step in group]


ORDER = torus_order()


def peer(grp, dev, step):
    x, core, y, z = step
    return (
        lax.rem(grp // 2 + x, 4) * 2 + lax.rem(lax.rem(grp, 2) + core, 2),
        lax.rem(dev // 4 + y, 4) * 4 + lax.rem(lax.rem(dev, 4) + z, 4),
    )


def exchange_kernel(send_ref, out_ref, send_sem, recv_sem, local_sem):
    grp, dev = lax.axis_index("grp"), lax.axis_index("dev")
    me = grp * 16 + dev
    slots = send_ref.shape[0] // 128
    barrier = pltpu.get_barrier_semaphore()
    for step in ORDER:
        pl.semaphore_signal(
            barrier, inc=1, device_id=peer(grp, dev, step), device_id_type=pl.DeviceIdType.MESH
        )
    pl.semaphore_wait(barrier, len(ORDER))
    copies = []
    for place, step in enumerate(ORDER):
        other = peer(grp, dev, step)
        copies.append(
            pltpu.make_async_remote_copy(
                src_ref=send_ref.at[pl.ds((other[0] * 16 + other[1]) * slots, slots)],
                dst_ref=out_ref.at[pl.ds(me * slots, slots)],
                send_sem=send_sem.at[place],
                recv_sem=recv_sem.at[place],
                device_id=other,
                device_id_type=pl.DeviceIdType.MESH,
            )
        )
        copies[-1].start()
    local = pltpu.make_async_copy(
        send_ref.at[pl.ds(me * slots, slots)], out_ref.at[pl.ds(me * slots, slots)], local_sem
    )
    local.start()
    local.wait()
    for copy in copies:
        copy.wait()


def exchange(values):
    return pl.pallas_call(
        exchange_kernel,
        in_specs=[pl.BlockSpec(memory_space=pl.ANY)],
        out_specs=pl.BlockSpec(memory_space=pl.ANY),
        out_shape=jax.ShapeDtypeStruct(values.shape, values.dtype),
        scratch_shapes=[
            pltpu.SemaphoreType.DMA((len(ORDER),)),
            pltpu.SemaphoreType.DMA((len(ORDER),)),
            pltpu.SemaphoreType.DMA,
        ],
        compiler_params=pltpu.CompilerParams(collective_id=0, has_side_effects=True),
        name="exchange",
    )(values)


def on_device(
    emission, positions, normals, areas, material, reflect, pair_local, pair_device, pair_block
):
    bands, patches = emission.shape
    blocks = patches // BLK
    devices = lax.axis_size(AXES)
    me = lax.axis_index(AXES)
    pairs = pair_local.shape[0]
    areas = areas[None, :]

    target = pair_device[:, 0]
    order = jnp.arange(pairs, dtype=jnp.int32)
    earlier = (target[:, None] == target[None, :]) & (order[None, :] < order[:, None])
    slot = target * 2 + jnp.sum(earlier.astype(jnp.int32), 1)
    code = pair_block * blocks + pair_local
    own = jnp.max(
        jnp.where(
            slot[:, None] == jnp.arange(2 * devices, dtype=jnp.int32)[None, :], code[:, None], -1
        ),
        0,
    )
    everyone = lax.all_gather(own, AXES, axis=0, tiled=False).reshape(devices, devices, 2)
    asked = lax.dynamic_index_in_dim(everyone, me, 1, keepdims=False)
    own = own.reshape(devices, 2)

    geometry = jnp.concatenate([positions, normals], 0).reshape(6, blocks, BLK).transpose(1, 0, 2)
    all_geometry = lax.all_gather(geometry, AXES, axis=0, tiled=True)

    first_block = (jnp.arange(devices, dtype=jnp.int32) * blocks)[:, None]
    send_near = jnp.where(own >= 0, own % blocks, 0).reshape(-1)
    send_far = jnp.where(asked >= 0, asked // blocks, 0).reshape(-1)
    near_mine = jnp.where(asked >= 0, asked // blocks, -1).reshape(-1)
    near_other = (first_block + jnp.where(asked >= 0, asked % blocks, 0)).reshape(-1)
    far_mine = jnp.where(own >= 0, own % blocks, -1).reshape(-1)
    far_other = (first_block + jnp.where(own >= 0, own // blocks, 0)).reshape(-1)

    class_hot = (
        jnp.arange(reflect.shape[1], dtype=jnp.int32)[:, None] == material[None, :]
    ).astype(jnp.float32)
    albedo = jnp.dot(reflect, class_hot, precision=lax.Precision.HIGHEST)

    near_tiles = tiles(near_mine, near_other, geometry, all_geometry)
    far_tiles = tiles(far_mine, far_other, geometry, all_geometry)
    current = emission
    for sweep_index in range(SWEEPS):
        near_values = exchange(pack(send_near, current, areas))
        far_values = exchange(pack(send_far, current, areas))
        gathered = apply(near_mine, near_values, near_tiles, jnp.zeros_like(emission))
        gathered = apply(far_mine, far_values, far_tiles, gathered)
        current = emission + albedo * gathered
    return current


def solution(mesh):
    return jax.shard_map(
        on_device,
        mesh=mesh,
        in_specs=(
            P(None, AXES),
            P(None, AXES),
            P(None, AXES),
            P(AXES),
            P(AXES),
            P(),
            P(AXES),
            P(AXES, None),
            P(AXES),
        ),
        out_specs=P(None, AXES),
        check_vma=False,
    )
```

```python
import math

import jax
import jax.numpy as jnp
import numpy as np
from jax import lax
from jax.experimental import pallas as pl
from jax.experimental.pallas import tpu as pltpu
from jax.sharding import PartitionSpec as P

BLK = 128
SWEEPS = 2
AXES = ("grp", "dev")
DEVICES = 128
BLOCKS = 32
BANDS = 64
SLOTS = 4
CHUNKS = 4
PLACES = DEVICES // CHUNKS
TASKS = PLACES * SLOTS
MESH = pl.DeviceIdType.MESH
softening = 0.5


def torus_order():
    seen = set()
    groups = []
    for dx in range(4):
        for dy in range(4):
            for dz in range(4):
                for core in range(2):
                    group = []
                    for x, y, z in ((dx, dy, dz), (dy, dz, dx), (dz, dx, dy)):
                        for step in ((x, core, y, z), (-x % 4, core, -y % 4, -z % 4)):
                            if step not in seen and any(step):
                                seen.add(step)
                                group.append(step)
                    if group:
                        groups.append(group)
    groups.sort(key=lambda group: sum(min(v, 4 - v) for v in group[0][:1] + group[0][2:]))
    return [step for group in groups for step in group]


ORDER = torus_order()
PEERS = len(ORDER)


def peer(grp, dev, step):
    x, core, y, z = step
    return (
        lax.rem(grp // 2 + x, 4) * 2 + lax.rem(lax.rem(grp, 2) + core, 2),
        lax.rem(dev // 4 + y, 4) * 4 + lax.rem(lax.rem(dev, 4) + z, 4),
    )


def fused_kernel(
    send_index,
    mine_index,
    order_index,
    keep,
    end_index,
    has,
    emission,
    areas,
    albedo,
    geometry,
    out,
    scaled,
    total,
    running,
    send,
    send_geometry,
    recv_geometry,
    tiles0,
    tiles1,
    tiles2,
    tiles3,
    recv00,
    recv01,
    recv02,
    recv03,
    recv10,
    recv11,
    recv12,
    recv13,
    geometry_send_sem,
    geometry_recv_sem,
    send_sem,
    recv_sem,
):
    tiles = (tiles0, tiles1, tiles2, tiles3)
    recv = ((recv00, recv01, recv02, recv03), (recv10, recv11, recv12, recv13))
    grp, dev = lax.axis_index("grp"), lax.axis_index("dev")
    peers = [peer(grp, dev, step) for step in ORDER]
    barrier = pltpu.get_barrier_semaphore()
    for other in peers:
        pl.semaphore_signal(barrier, inc=1, device_id=other, device_id_type=MESH)

    def pack_geometry(place, _):
        rows = [geometry[send_index[place * SLOTS + slot]][:6] for slot in range(SLOTS)]
        send_geometry[place] = jnp.concatenate(rows, 0)
        return 0

    lax.fori_loop(0, DEVICES, pack_geometry, 0)
    recv_geometry[PEERS] = send_geometry[PEERS]

    for block in range(BLOCKS):
        lanes = pl.ds(block * BLK, BLK)
        scaled[block] = (emission[:, lanes] * areas[:, lanes]).astype(jnp.bfloat16)

    pl.semaphore_wait(barrier, PEERS)
    geometry_copies = [
        pltpu.make_async_remote_copy(
            src_ref=send_geometry.at[place],
            dst_ref=recv_geometry.at[place],
            send_sem=geometry_send_sem.at[place],
            recv_sem=geometry_recv_sem.at[place],
            device_id=other,
            device_id_type=MESH,
        )
        for place, other in enumerate(peers)
    ]
    for copy in geometry_copies:
        copy.start()

    for sweep in range(SWEEPS):

        def pack(place, _):
            for slot in range(SLOTS):
                index = place * SLOTS + slot
                send[index] = scaled[send_index[index]]
            return 0

        lax.fori_loop(0, DEVICES, pack, 0)
        for slot in range(SLOTS):
            recv[sweep][CHUNKS - 1][TASKS - SLOTS + slot] = send[PEERS * SLOTS + slot]
        copies = [
            pltpu.make_async_remote_copy(
                src_ref=send.at[pl.ds(place * SLOTS, SLOTS)],
                dst_ref=recv[sweep][place // PLACES].at[pl.ds(place % PLACES * SLOTS, SLOTS)],
                send_sem=send_sem.at[sweep * PEERS + place],
                recv_sem=recv_sem.at[sweep * PEERS + place],
                device_id=other,
                device_id_type=MESH,
            )
            for place, other in enumerate(peers)
        ]
        for copy in copies:
            copy.start()

        if sweep == 0:
            for chunk in range(CHUNKS):
                for copy in geometry_copies[chunk * PLACES : (chunk + 1) * PLACES]:
                    copy.wait_recv()

                def build(place, _):
                    far_all = recv_geometry[chunk * PLACES + place].T
                    for slot in range(SLOTS):
                        index = place * SLOTS + slot
                        near = geometry[mine_index[chunk * TASKS + index]]
                        distance_sq = softening
                        facing_near = 0.0
                        facing_far = 0.0
                        for axis in range(3):
                            column = slot * 6 + axis
                            offset = far_all[:, column : column + 1] - near[axis : axis + 1]
                            distance_sq = distance_sq + offset * offset
                            facing_near = facing_near + near[3 + axis : 4 + axis] * offset
                            facing_far = facing_far - far_all[:, column + 3 : column + 4] * offset
                        tiles[chunk][index] = (
                            jnp.maximum(facing_near, 0.0)
                            * jnp.maximum(facing_far, 0.0)
                            / (math.pi * distance_sq * distance_sq)
                        ).astype(jnp.bfloat16)
                    return 0

                lax.fori_loop(0, PLACES, build, 0)

        for chunk in range(CHUNKS):
            for copy in copies[chunk * PLACES : (chunk + 1) * PLACES]:
                copy.wait_recv()

            def add(group, run):
                for inner in range(8):
                    task = group * 8 + inner
                    index = order_index[chunk * TASKS + task]
                    run = run * keep[chunk * TASKS + task] + jnp.dot(
                        recv[sweep][chunk][index],
                        tiles[chunk][index],
                        preferred_element_type=jnp.float32,
                    )
                    running[task] = run
                return run

            lax.fori_loop(0, TASKS // 8, add, jnp.zeros((BANDS, BLK), jnp.float32))

            def fold(block, _):
                part = running[end_index[chunk * BLOCKS + block]] * has[chunk * BLOCKS + block]
                total[block] = part if chunk == 0 else total[block] + part
                return 0

            lax.fori_loop(0, BLOCKS, fold, 0)

        for copy in copies:
            copy.wait_send()
        for block in range(BLOCKS):
            lanes = pl.ds(block * BLK, BLK)
            current = emission[:, lanes] + albedo[:, lanes] * total[block]
            if sweep + 1 < SWEEPS:
                scaled[block] = (current * areas[:, lanes]).astype(jnp.bfloat16)
            else:
                out[:, lanes] = current
    for copy in geometry_copies:
        copy.wait_send()


def fused(send_index, mine_index, order_index, keep, end_index, has, emission, areas, albedo, geometry):
    smem = pl.BlockSpec(memory_space=pltpu.SMEM)
    vmem = pl.BlockSpec(memory_space=pltpu.VMEM)
    values = pltpu.VMEM((TASKS, BANDS, BLK), jnp.bfloat16)
    tile = pltpu.VMEM((TASKS, BLK, BLK), jnp.bfloat16)
    return pl.pallas_call(
        fused_kernel,
        in_specs=[smem] * 6 + [vmem] * 4,
        out_specs=vmem,
        out_shape=jax.ShapeDtypeStruct(emission.shape, jnp.float32),
        scratch_shapes=[
            pltpu.VMEM((BLOCKS, BANDS, BLK), jnp.bfloat16),
            pltpu.VMEM((BLOCKS, BANDS, BLK), jnp.float32),
            pltpu.VMEM((TASKS, BANDS, BLK), jnp.float32),
            pltpu.VMEM((DEVICES * SLOTS, BANDS, BLK), jnp.bfloat16),
            pltpu.VMEM((DEVICES, SLOTS * 6, BLK), jnp.float32),
            pltpu.VMEM((DEVICES, SLOTS * 6, BLK), jnp.float32),
        ]
        + [tile] * CHUNKS
        + [values] * (SWEEPS * CHUNKS)
        + [
            pltpu.SemaphoreType.DMA((PEERS,)),
            pltpu.SemaphoreType.DMA((PEERS,)),
            pltpu.SemaphoreType.DMA((SWEEPS * PEERS,)),
            pltpu.SemaphoreType.DMA((SWEEPS * PEERS,)),
        ],
        compiler_params=pltpu.CompilerParams(
            collective_id=0, has_side_effects=True, vmem_limit_bytes=62 << 20
        ),
        name="fused",
    )(send_index, mine_index, order_index, keep, end_index, has, emission, areas, albedo, geometry)


def on_device(
    emission, positions, normals, areas, material, reflect, pair_local, pair_device, pair_block
):
    grp, dev = lax.axis_index("grp"), lax.axis_index("dev")
    me = grp * 16 + dev
    pairs = pair_local.shape[0]

    target = pair_device[:, 0]
    pair_order = jnp.arange(pairs, dtype=jnp.int32)
    earlier = (target[:, None] == target[None, :]) & (pair_order[None, :] < pair_order[:, None])
    slot = target * 2 + jnp.sum(earlier.astype(jnp.int32), 1)
    code = pair_block * BLOCKS + pair_local
    own = jnp.max(
        jnp.where(
            slot[:, None] == jnp.arange(2 * DEVICES, dtype=jnp.int32)[None, :], code[:, None], -1
        ),
        0,
    )
    everyone = lax.all_gather(own, AXES, axis=0, tiled=False).reshape(DEVICES, DEVICES, 2)
    asked = lax.dynamic_index_in_dim(everyone, me, 1, keepdims=False)
    own = own.reshape(DEVICES, 2)

    steps = np.array(ORDER + [(0, 0, 0, 0)], np.int32).T
    there = peer(grp, dev, steps)
    here = peer(grp, dev, (-steps) % np.array([[4], [2], [4], [4]], np.int32))
    there = there[0] * 16 + there[1]
    here = here[0] * 16 + here[1]
    own_there, asked_there = own[there], asked[there]
    own_here, asked_here = own[here], asked[here]
    send_index = jnp.concatenate([own_there % BLOCKS, asked_there // BLOCKS], 1)
    send_index = jnp.where(jnp.concatenate([own_there, asked_there], 1) >= 0, send_index, 0)
    mine = jnp.concatenate([asked_here // BLOCKS, own_here % BLOCKS], 1)
    mine = jnp.where(jnp.concatenate([asked_here, own_here], 1) >= 0, mine, BLOCKS)
    mine = mine.reshape(CHUNKS, TASKS)

    task = jnp.arange(TASKS, dtype=jnp.int32)
    block = jnp.arange(BLOCKS, dtype=jnp.int32)
    key = mine * TASKS + task
    rank = jnp.sum((key[:, None, :] < key[:, :, None]).astype(jnp.int32), 2)
    at_rank = rank[:, None, :] == task[None, :, None]
    order_index = jnp.sum(jnp.where(at_rank, task[None, None, :], 0), 2)
    sorted_mine = jnp.sum(jnp.where(at_rank, mine[:, None, :], 0), 2)
    keep = jnp.concatenate(
        [jnp.zeros((CHUNKS, 1), bool), sorted_mine[:, 1:] == sorted_mine[:, :-1]], 1
    ).astype(jnp.float32)
    upto = jnp.sum((mine[:, None, :] <= block[None, :, None]).astype(jnp.int32), 2)
    has = jnp.any(mine[:, None, :] == block[None, :, None], 2).astype(jnp.float32)

    class_hot = (
        jnp.arange(reflect.shape[1], dtype=jnp.int32)[:, None] == material[None, :]
    ).astype(jnp.float32)
    albedo = jnp.dot(reflect, class_hot, precision=lax.Precision.HIGHEST)
    geometry = jnp.concatenate([positions, normals, jnp.zeros((2, positions.shape[1]))], 0)
    geometry = geometry.astype(jnp.float32).reshape(8, BLOCKS, BLK).transpose(1, 0, 2)

    return fused(
        send_index.reshape(-1),
        jnp.minimum(mine, BLOCKS - 1).reshape(-1),
        order_index.reshape(-1),
        keep.reshape(-1),
        jnp.maximum(upto - 1, 0).reshape(-1),
        has.reshape(-1),
        emission,
        areas[None, :],
        albedo,
        geometry,
    )


def solution(mesh):
    return jax.shard_map(
        on_device,
        mesh=mesh,
        in_specs=(
            P(None, AXES),
            P(None, AXES),
            P(None, AXES),
            P(AXES),
            P(AXES),
            P(),
            P(AXES),
            P(AXES, None),
            P(AXES),
        ),
        out_specs=P(None, AXES),
        check_vma=False,
    )
```

```python
import math

import jax
import jax.numpy as jnp
import numpy as np
from jax import lax
from jax.experimental import pallas as pl
from jax.experimental.pallas import tpu as pltpu
from jax.sharding import PartitionSpec as P

BLK = 128
SWEEPS = 2
AXES = ("grp", "dev")
DEVICES = 128
BLOCKS = 32
BANDS = 64
SLOTS = 4
CHUNKS = 4
PLACES = DEVICES // CHUNKS
TASKS = PLACES * SLOTS
MESH = pl.DeviceIdType.MESH
softening = 0.5


def torus_order():
    seen = set()
    groups = []
    for dx in range(4):
        for dy in range(4):
            for dz in range(4):
                for core in range(2):
                    group = []
                    for x, y, z in ((dx, dy, dz), (dy, dz, dx), (dz, dx, dy)):
                        for step in ((x, core, y, z), (-x % 4, core, -y % 4, -z % 4)):
                            if step not in seen and any(step):
                                seen.add(step)
                                group.append(step)
                    if group:
                        groups.append(group)
    groups.sort(key=lambda group: sum(min(v, 4 - v) for v in group[0][:1] + group[0][2:]))
    return [step for group in groups for step in group]


ORDER = torus_order()
PEERS = len(ORDER)


def peer(grp, dev, step):
    x, core, y, z = step
    return (
        lax.rem(grp // 2 + x, 4) * 2 + lax.rem(lax.rem(grp, 2) + core, 2),
        lax.rem(dev // 4 + y, 4) * 4 + lax.rem(lax.rem(dev, 4) + z, 4),
    )


def opposite(step):
    x, core, y, z = step
    return (-x % 4, core, -y % 4, -z % 4)


BACK = [ORDER.index(opposite(step)) for step in ORDER] + [PEERS]


def turned(step):
    x, core, y, z = step
    return (y, core, z, x)


TURNS = [list(range(PEERS)), [ORDER.index(turned(step)) for step in ORDER]]


def route(asked, owned, out):
    row = lax.broadcasted_iota(jnp.int32, (BLK, BLK), 0)
    lane = lax.broadcasted_iota(jnp.int32, (BLK, BLK), 1)
    lane_row = lane[:1]
    asked0, asked1, owned0, owned1 = asked[0:1], asked[1:2], owned[0:1], owned[1:2]
    mine_rows = [
        jnp.where(asked0 >= 0, asked0 >> 5, BLOCKS),
        jnp.where(asked1 >= 0, asked1 >> 5, BLOCKS),
        jnp.where(owned0 >= 0, owned0 & (BLOCKS - 1), BLOCKS),
        jnp.where(owned1 >= 0, owned1 & (BLOCKS - 1), BLOCKS),
    ]
    place_row = lane_row // PLACES
    for chunk in range(CHUNKS):
        mine = jnp.zeros((1, BLK), jnp.int32)
        for slot in range(SLOTS):
            whole = jnp.broadcast_to(mine_rows[slot], (8, BLK))
            shifted = pltpu.roll(whole, (slot - chunk) * PLACES % BLK, 1)[:1]
            mine = jnp.where(place_row == slot, shifted, mine)
        key = (mine * BLK + lane_row).astype(jnp.float32)
        key_lane = jnp.broadcast_to(key, (BLK, BLK))
        rank = jnp.sum(jnp.where(key_lane.T < key_lane, 1.0, 0.0), 0, keepdims=True)
        at_rank = jnp.broadcast_to(rank, (BLK, BLK)).T == lane.astype(jnp.float32)
        place = ((row % PLACES) * SLOTS + row // PLACES).astype(jnp.float32)
        order = jnp.sum(jnp.where(at_rank, place, 0.0), 0, keepdims=True)
        mine_down = jnp.broadcast_to(mine.astype(jnp.float32), (BLK, BLK)).T
        sorted_mine = jnp.sum(jnp.where(at_rank, mine_down, 0.0), 0, keepdims=True)
        before = pltpu.roll(jnp.broadcast_to(sorted_mine, (8, BLK)), 1, 1)[:1]
        keep = jnp.where((sorted_mine == before) & (lane_row > 0), 1.0, 0.0)
        block = lane.astype(jnp.float32)
        upto = jnp.sum(jnp.where(mine_down <= block, 1.0, 0.0), 0, keepdims=True)
        has = jnp.sum(jnp.where(mine_down == block, 1.0, 0.0), 0, keepdims=True)
        rows = [
            order,
            keep,
            jnp.maximum(upto - 1.0, 0.0),
            jnp.minimum(has, 1.0),
            jnp.minimum(mine, BLOCKS - 1).astype(jnp.float32),
            jnp.zeros((3, BLK), jnp.float32),
        ]
        out[chunk * 8 : chunk * 8 + 8] = jnp.concatenate(rows, 0).astype(jnp.int32)
    asked = jnp.concatenate(
        [jnp.where(asked0 >= 0, asked0 >> 5, 0), jnp.where(asked1 >= 0, asked1 >> 5, 0)]
        + [jnp.zeros((6, BLK), jnp.int32)],
        0,
    )
    out[CHUNKS * 8 : CHUNKS * 8 + 8] = asked


def fused_kernel(
    near_index,
    near_code,
    owned,
    emission,
    areas,
    albedo,
    geometry,
    out,
    scaled,
    total,
    running,
    send,
    near_send,
    near_recv,
    far_send,
    far_recv,
    asked_rows,
    table_rows,
    table,
    tiles0,
    tiles1,
    tiles2,
    tiles3,
    recv00,
    recv01,
    recv02,
    recv03,
    recv10,
    recv11,
    recv12,
    recv13,
    send_sem,
    recv_sem,
    table_sem,
):
    tiles = (tiles0, tiles1, tiles2, tiles3)
    recv = ((recv00, recv01, recv02, recv03), (recv10, recv11, recv12, recv13))
    grp, dev = lax.axis_index("grp"), lax.axis_index("dev")
    core = lax.rem(grp, 2)
    peers = [peer(grp, dev, step) for step in ORDER]
    barrier = pltpu.get_barrier_semaphore()
    for other in peers:
        pl.semaphore_signal(barrier, inc=1, device_id=other, device_id_type=MESH)

    def exchange(kind, source, target):
        copies = [
            pltpu.make_async_remote_copy(
                src_ref=source(place),
                dst_ref=target(place),
                send_sem=send_sem.at[kind * PEERS + place],
                recv_sem=recv_sem.at[kind * PEERS + place],
                device_id=other,
                device_id_type=MESH,
            )
            for place, other in enumerate(peers)
        ]
        for turn in range(2):

            @pl.when(core == turn)
            def _():
                for place in TURNS[turn]:
                    copies[place].start()

        return copies

    def values(sweep, first, count):
        def source(place):
            return send.at[pl.ds(place * SLOTS + first, count)]

        def target(place):
            chunk = recv[sweep][place // PLACES]
            return chunk.at[pl.ds(place % PLACES * SLOTS + first, count)]

        return source, target

    lane = lax.broadcasted_iota(jnp.int32, (4, BLK), 1)

    def pack_near(place, _):
        codes = jnp.where(
            lane == 0,
            near_code[place * 2],
            jnp.where(lane == 1, near_code[place * 2 + 1], 0.0),
        )
        rows = [geometry[near_index[place * 2 + slot]][:6] for slot in range(2)]
        near_send[place] = jnp.concatenate(rows + [codes], 0)
        return 0

    lax.fori_loop(0, DEVICES, pack_near, 0)
    near_recv[PEERS] = near_send[PEERS]
    for block in range(BLOCKS):
        lanes = pl.ds(block * BLK, BLK)
        scaled[block] = (emission[:, lanes] * areas[:, lanes]).astype(jnp.bfloat16)

    def pack_near_values(place, _):
        for slot in range(2):
            send[place * SLOTS + slot] = scaled[near_index[place * 2 + slot]]
        return 0

    lax.fori_loop(0, DEVICES, pack_near_values, 0)
    pl.semaphore_wait(barrier, PEERS)
    near_copies = exchange(0, lambda place: near_send.at[place], lambda place: near_recv.at[place])
    value_copies = exchange(2, *values(0, 0, 2))

    for copy in near_copies:
        copy.wait_recv()

    def collect(place, _):
        asked_rows[pl.ds(place, 1)] = near_recv[place, 12:13]
        return 0

    lax.fori_loop(0, DEVICES, collect, 0)
    route(asked_rows[...].T[:8].astype(jnp.int32), owned[...], table_rows)
    to_table = pltpu.make_async_copy(table_rows, table, table_sem)
    to_table.start()
    to_table.wait()

    def far_index(place, slot):
        return table[CHUNKS * 8 + slot, BACK[place]] & (BLOCKS - 1)

    def pack_far_values():
        for place in range(DEVICES):
            for slot in range(2):
                send[place * SLOTS + 2 + slot] = scaled[far_index(place, slot)]

    for place in range(DEVICES):
        rows = [geometry[far_index(place, slot)][:6] for slot in range(2)]
        far_send[place] = jnp.concatenate(rows + [jnp.zeros((4, BLK), jnp.float32)], 0)
    far_recv[PEERS] = far_send[PEERS]
    far_copies = exchange(1, lambda place: far_send.at[place], lambda place: far_recv.at[place])
    pack_far_values()
    for slot in range(SLOTS):
        recv[0][CHUNKS - 1][TASKS - SLOTS + slot] = send[PEERS * SLOTS + slot]
    far_value_copies = exchange(3, *values(0, 2, 2))

    def build_tiles(chunk, source, first):
        def build(place, _):
            far_all = source[chunk * PLACES + place].T
            for slot in range(2):
                near = geometry[table[chunk * 8 + 4, (first + slot) * PLACES + place] & (BLOCKS - 1)]
                distance_sq = softening
                facing_near = 0.0
                facing_far = 0.0
                for axis in range(3):
                    column = slot * 6 + axis
                    offset = far_all[:, column : column + 1] - near[axis : axis + 1]
                    distance_sq = distance_sq + offset * offset
                    facing_near = facing_near + near[3 + axis : 4 + axis] * offset
                    facing_far = facing_far - far_all[:, column + 3 : column + 4] * offset
                tiles[chunk][place * SLOTS + first + slot] = (
                    jnp.maximum(facing_near, 0.0)
                    * jnp.maximum(facing_far, 0.0)
                    / (math.pi * distance_sq * distance_sq)
                ).astype(jnp.bfloat16)
            return 0

        lax.fori_loop(0, PLACES, build, 0)

    for chunk in range(CHUNKS):
        build_tiles(chunk, near_recv, 0)
    for chunk in range(CHUNKS):
        for copy in far_copies[chunk * PLACES : (chunk + 1) * PLACES]:
            copy.wait_recv()
        build_tiles(chunk, far_recv, 2)

    for sweep in range(SWEEPS):
        if sweep == 0:
            rounds = [value_copies, far_value_copies]
        else:
            for copy in value_copies + far_value_copies:
                copy.wait_send()

            def pack_all_near(place, _):
                for slot in range(2):
                    send[place * SLOTS + slot] = scaled[near_index[place * 2 + slot]]
                return 0

            lax.fori_loop(0, DEVICES, pack_all_near, 0)
            pack_far_values()
            for slot in range(SLOTS):
                recv[1][CHUNKS - 1][TASKS - SLOTS + slot] = send[PEERS * SLOTS + slot]
            rounds = [exchange(4, *values(1, 0, SLOTS))]

        for chunk in range(CHUNKS):
            for copies in rounds:
                for copy in copies[chunk * PLACES : (chunk + 1) * PLACES]:
                    copy.wait_recv()

            def add(group, run):
                for inner in range(8):
                    task = group * 8 + inner
                    index = table[chunk * 8, task] & (TASKS - 1)
                    run = run * table[chunk * 8 + 1, task].astype(jnp.float32) + jnp.dot(
                        recv[sweep][chunk][index],
                        tiles[chunk][index],
                        preferred_element_type=jnp.float32,
                    )
                    running[task] = run
                return run

            lax.fori_loop(0, TASKS // 8, add, jnp.zeros((BANDS, BLK), jnp.float32))

            def fold(block, _):
                part = running[table[chunk * 8 + 2, block] & (TASKS - 1)]
                part = part * table[chunk * 8 + 3, block].astype(jnp.float32)
                total[block] = part if chunk == 0 else total[block] + part
                return 0

            lax.fori_loop(0, BLOCKS, fold, 0)

        for block in range(BLOCKS):
            lanes = pl.ds(block * BLK, BLK)
            current = emission[:, lanes] + albedo[:, lanes] * total[block]
            if sweep + 1 < SWEEPS:
                scaled[block] = (current * areas[:, lanes]).astype(jnp.bfloat16)
            else:
                out[:, lanes] = current
    for copy in near_copies + far_copies + rounds[0]:
        copy.wait_send()


def fused(near_index, near_code, owned, emission, areas, albedo, geometry):
    smem = pl.BlockSpec(memory_space=pltpu.SMEM)
    vmem = pl.BlockSpec(memory_space=pltpu.VMEM)
    values = pltpu.VMEM((TASKS, BANDS, BLK), jnp.bfloat16)
    tile = pltpu.VMEM((TASKS, BLK, BLK), jnp.bfloat16)
    message = pltpu.VMEM((DEVICES, 16, BLK), jnp.float32)
    return pl.pallas_call(
        fused_kernel,
        in_specs=[smem] * 2 + [vmem] * 5,
        out_specs=vmem,
        out_shape=jax.ShapeDtypeStruct(emission.shape, jnp.float32),
        scratch_shapes=[
            pltpu.VMEM((BLOCKS, BANDS, BLK), jnp.bfloat16),
            pltpu.VMEM((BLOCKS, BANDS, BLK), jnp.float32),
            pltpu.VMEM((TASKS, BANDS, BLK), jnp.float32),
            pltpu.VMEM((DEVICES * SLOTS, BANDS, BLK), jnp.bfloat16),
            message,
            message,
            message,
            message,
            pltpu.VMEM((DEVICES, BLK), jnp.float32),
            pltpu.VMEM((CHUNKS * 8 + 8, BLK), jnp.int32),
            pltpu.SMEM((CHUNKS * 8 + 8, BLK), jnp.int32),
        ]
        + [tile] * CHUNKS
        + [values] * (SWEEPS * CHUNKS)
        + [
            pltpu.SemaphoreType.DMA((5 * PEERS,)),
            pltpu.SemaphoreType.DMA((5 * PEERS,)),
            pltpu.SemaphoreType.DMA,
        ],
        compiler_params=pltpu.CompilerParams(
            collective_id=0, has_side_effects=True, vmem_limit_bytes=62 << 20
        ),
        name="fused",
    )(near_index, near_code, owned, emission, areas, albedo, geometry)


def on_device(
    emission, positions, normals, areas, material, reflect, pair_local, pair_device, pair_block
):
    grp, dev = lax.axis_index("grp"), lax.axis_index("dev")
    pairs = pair_local.shape[0]

    target = pair_device[:, 0]
    pair_order = jnp.arange(pairs, dtype=jnp.int32)
    earlier = (target[:, None] == target[None, :]) & (pair_order[None, :] < pair_order[:, None])
    slot = target * 2 + jnp.sum(earlier.astype(jnp.int32), 1)
    code = pair_block * BLOCKS + pair_local
    own = jnp.max(
        jnp.where(
            slot[:, None] == jnp.arange(2 * DEVICES, dtype=jnp.int32)[None, :], code[:, None], -1
        ),
        0,
    )
    own = own.reshape(DEVICES, 2)

    steps = np.array(ORDER + [(0, 0, 0, 0)], np.int32).T
    there = peer(grp, dev, steps)
    here = peer(grp, dev, (-steps) % np.array([[4], [2], [4], [4]], np.int32))
    own_there = own[there[0] * 16 + there[1]]
    own_here = own[here[0] * 16 + here[1]]
    near_index = jnp.where(own_there >= 0, own_there % BLOCKS, 0)
    owned = jnp.concatenate([own_here.T, jnp.zeros((6, DEVICES), jnp.int32)], 0)

    class_hot = (
        jnp.arange(reflect.shape[1], dtype=jnp.int32)[:, None] == material[None, :]
    ).astype(jnp.float32)
    albedo = jnp.dot(reflect, class_hot, precision=lax.Precision.HIGHEST)
    geometry = jnp.concatenate([positions, normals, jnp.zeros((2, positions.shape[1]))], 0)
    geometry = geometry.astype(jnp.float32).reshape(8, BLOCKS, BLK).transpose(1, 0, 2)

    return fused(
        near_index.reshape(-1),
        own_there.astype(jnp.float32).reshape(-1),
        owned,
        emission,
        areas[None, :],
        albedo,
        geometry,
    )


def solution(mesh):
    return jax.shard_map(
        on_device,
        mesh=mesh,
        in_specs=(
            P(None, AXES),
            P(None, AXES),
            P(None, AXES),
            P(AXES),
            P(AXES),
            P(),
            P(AXES),
            P(AXES, None),
            P(AXES),
        ),
        out_specs=P(None, AXES),
        check_vma=False,
    )
```

```python
import math

import jax
import jax.numpy as jnp
import numpy as np
from jax import lax
from jax.experimental import pallas as pl
from jax.experimental.pallas import tpu as pltpu
from jax.sharding import PartitionSpec as P

BLK = 128
SWEEPS = 2
AXES = ("grp", "dev")
DEVICES = 128
BLOCKS = 32
BANDS = 64
SLOTS = 3
RANKS = 16
PIECES = 4
RELAYS = RANKS * PIECES
ROWS = 64 // PIECES
CHUNKS = 4
PLACES = DEVICES // CHUNKS
TASKS = PLACES * SLOTS
MESH = pl.DeviceIdType.MESH
softening = 0.5


def view_tile(near, far):
    distance_sq = softening
    facing_near = 0.0
    facing_far = 0.0
    for axis_index in range(3):
        offset = far[:, axis_index, None, :] - near[:, axis_index, :, None]
        distance_sq = distance_sq + offset * offset
        facing_near = facing_near + near[:, 3 + axis_index, :, None] * offset
        facing_far = facing_far - far[:, 3 + axis_index, None, :] * offset
    return (
        jnp.maximum(facing_near, 0.0)
        * jnp.maximum(facing_far, 0.0)
        / (math.pi * distance_sq * distance_sq)
    )


def general(
    emission, positions, normals, areas, material, reflect, pair_local, pair_device, pair_block
):
    band_count, patch_count = emission.shape
    local_blocks = patch_count // BLK
    device_count = lax.axis_size(("grp", "dev"))
    pair_count = pair_local.shape[0]
    capacity = max(2, (2 * pair_count + device_count - 1) // device_count)
    slot_total = device_count * capacity
    target = pair_device[:, 0]
    target_hot = (target[:, None] == jnp.arange(device_count, dtype=jnp.int32)[None, :]).astype(
        jnp.int32
    )
    earlier = jnp.cumsum(target_hot, 0) - target_hot
    slot_index = target * capacity + jnp.sum(earlier * target_hot, 1)
    wanted = jnp.zeros((slot_total,), jnp.int32).at[slot_index].set(pair_block)
    asked_for = lax.all_to_all(wanted, ("grp", "dev"), split_axis=0, concat_axis=0, tiled=True)
    geometry = jnp.concatenate([positions, normals, areas[None, :]], 0)
    geometry = geometry.reshape(7, local_blocks, BLK).transpose(1, 0, 2)
    lent_geometry = geometry[asked_for]
    served = lax.all_to_all(lent_geometry, ("grp", "dev"), split_axis=0, concat_axis=0, tiled=True)
    far_geometry = served[slot_index]
    near_geometry = geometry[pair_local]
    block_ids = jnp.arange(local_blocks, dtype=jnp.int32)
    local_hot = (pair_local[:, None] == block_ids[None, :]).astype(jnp.float32)
    asked_hot = (asked_for[:, None] == block_ids[None, :]).astype(jnp.float32)
    class_hot = (
        jnp.arange(reflect.shape[1], dtype=jnp.int32)[:, None] == material[None, :]
    ).astype(jnp.float32)
    albedo = jnp.dot(reflect, class_hot, precision=lax.Precision.HIGHEST)
    albedo = albedo.reshape(band_count, local_blocks, BLK).transpose(1, 0, 2)
    source = emission.reshape(band_count, local_blocks, BLK).transpose(1, 0, 2)
    area_blocks = geometry[:, 6, :]
    current = source
    for sweep_index in range(SWEEPS):
        scaled = (current * area_blocks[:, None, :]).astype(jnp.bfloat16)
        lent_values = scaled[asked_for]
        kernel = view_tile(near_geometry, far_geometry).astype(jnp.bfloat16)
        incoming = lax.all_to_all(
            lent_values, ("grp", "dev"), split_axis=0, concat_axis=0, tiled=True
        )
        to_near = jnp.einsum(
            "pnj,pij->pni", incoming[slot_index], kernel, preferred_element_type=jnp.float32
        )
        to_far = jnp.einsum(
            "pni,pij->pnj", scaled[pair_local], kernel, preferred_element_type=jnp.float32
        )
        replies = jnp.zeros((slot_total, band_count, BLK), jnp.float32).at[slot_index].set(to_far)
        returned = lax.all_to_all(replies, ("grp", "dev"), split_axis=0, concat_axis=0, tiled=True)
        gathered = jnp.einsum("pb,pnk->bnk", local_hot, to_near, precision=lax.Precision.HIGHEST)
        gathered = gathered + jnp.einsum(
            "sb,snk->bnk", asked_hot, returned, precision=lax.Precision.HIGHEST
        )
        current = source + albedo * gathered
    return current.transpose(1, 0, 2).reshape(band_count, patch_count)


def torus_order():
    seen = set()
    groups = []
    for dx in range(4):
        for dy in range(4):
            for dz in range(4):
                for core in range(2):
                    group = []
                    for x, y, z in ((dx, dy, dz), (dy, dz, dx), (dz, dx, dy)):
                        for step in ((x, core, y, z), (-x % 4, core, -y % 4, -z % 4)):
                            if step not in seen and any(step):
                                seen.add(step)
                                group.append(step)
                    if group:
                        groups.append(group)
    groups.sort(key=lambda group: sum(min(v, 4 - v) for v in group[0][:1] + group[0][2:]))
    return [step for group in groups for step in group]


ORDER = torus_order()
PEERS = len(ORDER)


def peer(grp, dev, step):
    x, core, y, z = step
    return (
        lax.rem(grp // 2 + x, 4) * 2 + lax.rem(lax.rem(grp, 2) + core, 2),
        lax.rem(dev // 4 + y, 4) * 4 + lax.rem(lax.rem(dev, 4) + z, 4),
    )


def opposite(step):
    x, core, y, z = step
    return (-x % 4, core, -y % 4, -z % 4)


BACK = [ORDER.index(opposite(step)) for step in ORDER] + [PEERS]


def turned(step):
    x, core, y, z = step
    return (y, core, z, x)


TURNS = [list(range(PEERS)), [ORDER.index(turned(step)) for step in ORDER]]


def across(row):
    return jnp.broadcast_to(row, (BLK, BLK))


def down(row):
    return jnp.broadcast_to(row, (BLK, BLK)).T


def column_sum(terms):
    return jnp.sum(terms, 0, keepdims=True)


def sort_rows(mine, names, lane):
    lane_row = lane[:1]
    key = mine * BLK + lane_row
    rank = column_sum(jnp.where(down(key) < across(key), 1.0, 0.0))
    at_rank = down(rank) == lane
    order = column_sum(jnp.where(at_rank, names, 0.0))
    mine_down = down(mine)
    sorted_mine = column_sum(jnp.where(at_rank, mine_down, 0.0))
    before = pltpu.roll(jnp.broadcast_to(sorted_mine, (8, BLK)), 1, 1)[:1]
    keep = jnp.where((sorted_mine == before) & (lane_row > 0), 1.0, 0.0)
    upto = column_sum(jnp.where(mine_down <= lane, 1.0, 0.0))
    has = column_sum(jnp.where(mine_down == lane, 1.0, 0.0))
    return [order, keep, jnp.maximum(upto - 1.0, 0.0), jnp.minimum(has, 1.0)]


def iotas():
    row = lax.broadcasted_iota(jnp.int32, (BLK, BLK), 0)
    lane = lax.broadcasted_iota(jnp.int32, (BLK, BLK), 1)
    return row, lane


def route(asked, owned, out):
    row, lane = iotas()
    lane_row = lane[:1]
    lane = lane.astype(jnp.float32)
    asked0, asked1, owned0, owned1 = asked[0:1], asked[1:2], owned[0:1], owned[1:2]
    owned_mine = owned1 & (BLOCKS - 1)
    mine_rows = [
        jnp.where(asked0 >= 0, asked0 >> 5, BLOCKS),
        jnp.where(owned0 >= 0, owned0 & (BLOCKS - 1), BLOCKS),
        jnp.where(asked1 >= 0, asked1 >> 5, jnp.where(owned1 >= 0, owned_mine, BLOCKS)),
    ]
    place_row = lane_row // PLACES
    names = ((row % PLACES) * SLOTS + row // PLACES).astype(jnp.float32)
    for chunk in range(CHUNKS):
        mine = jnp.full((1, BLK), BLOCKS, jnp.int32)
        for slot in range(SLOTS):
            whole = jnp.broadcast_to(mine_rows[slot], (8, BLK))
            shifted = pltpu.roll(whole, (slot - chunk) * PLACES % BLK, 1)[:1]
            mine = jnp.where(place_row == slot, shifted, mine)
        mine = mine.astype(jnp.float32)
        rows = sort_rows(mine, names, lane)
        rows += [jnp.minimum(mine, BLOCKS - 1.0), jnp.zeros((3, BLK), jnp.float32)]
        out[chunk * 8 : chunk * 8 + 8] = jnp.concatenate(rows, 0).astype(jnp.int32)
    asked_first = jnp.where(asked0 >= 0, asked0 >> 5, 0)
    asked_second = jnp.where(asked1 >= 0, asked1 >> 5, 0)
    both = (owned1 >= 0) & (asked1 >= 0)
    crowded = jnp.max(jnp.where(both, 1.0, 0.0), 1, keepdims=True)
    out[CHUNKS * 8 : CHUNKS * 8 + 8] = jnp.concatenate(
        [
            asked_first,
            asked_second,
            jnp.where(owned1 >= 0, owned_mine, asked_second),
            (asked1 >= 0).astype(jnp.int32),
            jnp.broadcast_to(crowded, (1, BLK)).astype(jnp.int32),
            jnp.zeros((3, BLK), jnp.int32),
        ],
        0,
    )


def route_rest(crowded, asked, owned, relay_shift, out):
    row, lane = iotas()
    lane = lane.astype(jnp.float32)
    lane_row = lane[:1]
    asked1, owned1 = asked[1:2], owned[1:2]
    ids = owned[2:3].astype(jnp.float32)
    rank = column_sum(jnp.where(down(ids) < across(ids), down(crowded), 0.0))
    rank_down = down(rank)
    hot_down = down(crowded) > 0.5
    my_rank = jnp.sum(jnp.where(lane_row == PEERS, rank, 0.0), 1, keepdims=True)
    count = jnp.sum(crowded, 1, keepdims=True)

    def pick(wanted, terms):
        wanted = jnp.where(wanted >= RANKS, wanted - RANKS, wanted)
        wanted = jnp.where(wanted < 0, wanted + RANKS, wanted)
        return column_sum(jnp.where(hot_down & (rank_down == across(wanted)), terms, 0.0))

    ahead = my_rank + lane_row
    behind = my_rank - lane_row
    asked_second = jnp.where(asked1 >= 0, asked1 >> 5, 0).astype(jnp.float32)
    both = (owned1 >= 0) & (asked1 >= 0)
    mine = jnp.where(both, owned1 & (BLOCKS - 1), BLOCKS).astype(jnp.float32)
    places = row.astype(jnp.float32)
    lend = pick(ahead, down(asked_second))
    source = pick(behind, places)
    found = pick(behind, jnp.ones((BLK, BLK), jnp.float32))
    mine = jnp.where((lane_row < RANKS) & (found > 0.5), pick(behind, down(mine)), float(BLOCKS))
    relay = pick(rank - relay_shift, places)
    rows = sort_rows(mine, places, lane)
    rows += [jnp.minimum(mine, BLOCKS - 1.0), lend, source, relay]
    out[...] = jnp.concatenate(rows, 0).astype(jnp.int32)
    return count


def fused_kernel(
    near_index,
    near_code,
    owned,
    emission,
    areas,
    albedo,
    geometry,
    out,
    fits,
    scaled,
    total,
    running,
    send,
    near_send,
    near_recv,
    far_send,
    far_recv,
    asked_rows,
    table_rows,
    table,
    rest_rows,
    rest,
    tiles0,
    tiles1,
    tiles2,
    tiles3,
    recv00,
    recv01,
    recv02,
    recv03,
    recv10,
    recv11,
    recv12,
    recv13,
    lend_send,
    lend_recv0,
    lend_recv1,
    relay_send,
    relay_recv0,
    relay_recv1,
    rest_tiles,
    rest_values,
    send_sem,
    recv_sem,
    table_sem,
):
    tiles = (tiles0, tiles1, tiles2, tiles3)
    recv = ((recv00, recv01, recv02, recv03), (recv10, recv11, recv12, recv13))
    lend_recv = (lend_recv0, lend_recv1)
    relay_recv = (relay_recv0, relay_recv1)
    grp, dev = lax.axis_index("grp"), lax.axis_index("dev")
    core = lax.rem(grp, 2)
    chip = (grp // 2) * 16 + dev
    peers = [peer(grp, dev, step) for step in ORDER]
    barrier = pltpu.get_barrier_semaphore()
    for other in peers:
        pl.semaphore_signal(barrier, inc=1, device_id=other, device_id_type=MESH)

    def describe(kind, source, target):
        return [
            pltpu.make_async_remote_copy(
                src_ref=source(place),
                dst_ref=target(place),
                send_sem=send_sem.at[kind * PEERS + place],
                recv_sem=recv_sem.at[kind * PEERS + place],
                device_id=other,
                device_id_type=MESH,
            )
            for place, other in enumerate(peers)
        ]

    def exchange(kind, source, target):
        copies = describe(kind, source, target)
        for turn in range(2):

            @pl.when(core == turn)
            def _():
                for place in TURNS[turn]:
                    copies[place].start()

        return copies

    def values(sweep, first, count):
        def source(place):
            return send.at[pl.ds(place * SLOTS + first, count)]

        def target(place):
            chunk = recv[sweep][place // PLACES]
            return chunk.at[pl.ds(place % PLACES * SLOTS + first, count)]

        return source, target

    def keep_own(sweep, slots):
        for slot in slots:
            recv[sweep][CHUNKS - 1][TASKS - SLOTS + slot] = send[PEERS * SLOTS + slot]

    def pack_near_values(place, _):
        send[place * SLOTS] = scaled[near_index[place * 2]]
        return 0

    def sent(row, place):
        return table[CHUNKS * 8 + row, BACK[place]] & (BLOCKS - 1)

    def pack_values(slot, row):
        for place in range(DEVICES):
            send[place * SLOTS + slot] = scaled[sent(row, place)]

    sides = [[place for place in range(PEERS) if ORDER[place][1] == side] for side in range(2)]

    def on_core(side, places, act):
        @pl.when(core == side)
        def _():
            for place in places:
                act(place)

    def lend(sweep):
        for apart in range(RANKS):
            block = scaled[rest[5, apart] & (BLOCKS - 1)]
            for piece in range(PIECES):
                lend_send[apart * PIECES + piece] = block[piece * ROWS : (piece + 1) * ROWS]
        lend_recv[sweep][PEERS] = lend_send[chip]
        copies = describe(
            7 + sweep,
            lambda place: lend_send.at[(peers[place][0] // 2) * 16 + peers[place][1]],
            lambda place: lend_recv[sweep].at[place],
        )
        for side in range(2):
            on_core(side, sides[side], lambda place: copies[place].start())
        return copies

    def pass_on(sweep, lent):
        on_core(0, range(PEERS), lambda place: lent[place].wait_recv())
        copies = describe(
            9 + sweep,
            lambda place: relay_send.at[place],
            lambda place: relay_recv[sweep].at[chip],
        )

        @pl.when(core == 0)
        def _():
            for place in range(DEVICES):
                relay_send[place] = lend_recv[sweep][rest[7, BACK[place]] & (DEVICES - 1)]
            relay_recv[sweep][chip] = relay_send[PEERS]
            for place in range(PEERS):
                copies[place].start()

        return copies

    def finish_rest(lent, passed):
        for side in range(2):
            on_core(side, sides[side], lambda place: lent[place].wait_send())
        on_core(0, range(PEERS), lambda place: passed[place].wait_send())

    lane = lax.broadcasted_iota(jnp.int32, (4, BLK), 1)

    def pack_near(place, _):
        codes = jnp.where(
            lane == 0,
            near_code[place * 2],
            jnp.where(lane == 1, near_code[place * 2 + 1], 0.0),
        )
        rows = [geometry[near_index[place * 2 + slot]][:6] for slot in range(2)]
        near_send[place] = jnp.concatenate(rows + [codes], 0)
        return 0

    lax.fori_loop(0, DEVICES, pack_near, 0)
    near_recv[PEERS] = near_send[PEERS]
    for block in range(BLOCKS):
        lanes = pl.ds(block * BLK, BLK)
        scaled[block] = (emission[:, lanes] * areas[:, lanes]).astype(jnp.bfloat16)
    lax.fori_loop(0, DEVICES, pack_near_values, 0)
    pl.semaphore_wait(barrier, PEERS)
    near_copies = exchange(0, lambda place: near_send.at[place], lambda place: near_recv.at[place])
    value_copies = exchange(2, *values(0, 0, 1))

    for copy in near_copies:
        copy.wait_recv()

    def collect_asked(place, _):
        asked_rows[pl.ds(place, 1)] = near_recv[place, 12:13]
        return 0

    lax.fori_loop(0, DEVICES, collect_asked, 0)
    asked = asked_rows[...].T[:8].astype(jnp.int32)
    route(asked, owned[...], table_rows)
    to_table = pltpu.make_async_copy(table_rows, table, table_sem.at[0])
    to_table.start()
    to_table.wait()

    crowded_row = table_rows[CHUNKS * 8 + 4 : CHUNKS * 8 + 5].astype(jnp.float32)
    blank = jnp.zeros((3, BLK), jnp.float32)
    for place in range(DEVICES):
        rows = [geometry[sent(slot, place)][:6] for slot in range(2)]
        far_send[place] = jnp.concatenate(rows + [crowded_row, blank], 0)
    far_recv[PEERS] = far_send[PEERS]
    far_copies = exchange(1, lambda place: far_send.at[place], lambda place: far_recv.at[place])
    pack_values(1, 0)
    far_value_copies = exchange(3, *values(0, 1, 1))

    def tile(far_columns, near, first):
        distance_sq = softening
        facing_near = 0.0
        facing_far = 0.0
        for axis in range(3):
            column = first + axis
            offset = far_columns[:, column : column + 1] - near[axis : axis + 1]
            distance_sq = distance_sq + offset * offset
            facing_near = facing_near + near[3 + axis : 4 + axis] * offset
            facing_far = facing_far - far_columns[:, column + 3 : column + 4] * offset
        return (
            jnp.maximum(facing_near, 0.0)
            * jnp.maximum(facing_far, 0.0)
            / (math.pi * distance_sq * distance_sq)
        ).astype(jnp.bfloat16)

    def near_of(chunk, slot, place):
        return geometry[table[chunk * 8 + 4, slot * PLACES + place] & (BLOCKS - 1)]

    for chunk in range(CHUNKS):

        def build_near(place, _):
            columns = near_recv[chunk * PLACES + place].T
            tiles[chunk][place * SLOTS] = tile(columns, near_of(chunk, 0, place), 0)
            return 0

        lax.fori_loop(0, PLACES, build_near, 0)

    for copy in far_copies:
        copy.wait_recv()

    def collect_crowded(place, _):
        asked_rows[pl.ds(place, 1)] = far_recv[place, 12:13]
        return 0

    lax.fori_loop(0, DEVICES, collect_crowded, 0)
    crowded = asked_rows[...].T[:1]
    shift = (chip // PIECES).astype(jnp.float32)
    count = route_rest(crowded, asked, owned[...], shift, rest_rows)
    fits[...] = jnp.broadcast_to(count, (8, BLK))
    to_rest = pltpu.make_async_copy(rest_rows, rest, table_sem.at[1])
    to_rest.start()
    to_rest.wait()
    lent = lend(0)
    pack_values(2, 2)
    keep_own(0, range(SLOTS))
    last_copies = exchange(4, *values(0, 2, 1))

    for chunk in range(CHUNKS):

        def build_far(place, _):
            whole = chunk * PLACES + place
            far = far_recv[whole]
            tiles[chunk][place * SLOTS + 1] = tile(far.T, near_of(chunk, 1, place), 0)
            other = jnp.where(table[CHUNKS * 8 + 3, whole] > 0, near_recv[whole], far)
            tiles[chunk][place * SLOTS + 2] = tile(other.T, near_of(chunk, 2, place), 6)
            return 0

        lax.fori_loop(0, PLACES, build_far, 0)

    passed = pass_on(0, lent)

    def build_rest(apart, _):
        near = geometry[rest[4, apart] & (BLOCKS - 1)]
        columns = far_recv[rest[6, apart] & (DEVICES - 1)].T
        rest_tiles[apart] = tile(columns, near, 6)
        return 0

    lax.fori_loop(0, RANKS, build_rest, 0)

    def accumulate(values_ref, tiles_ref, tasks, rows, base, first):
        def add(group, run):
            for inner in range(8):
                task = group * 8 + inner
                index = rows[base, task] & (BLK - 1)
                index = jnp.minimum(index, tasks - 1)
                run = run * rows[base + 1, task].astype(jnp.float32) + jnp.dot(
                    values_ref[index], tiles_ref[index], preferred_element_type=jnp.float32
                )
                running[task] = run
            return run

        lax.fori_loop(0, tasks // 8, add, jnp.zeros((BANDS, BLK), jnp.float32))

        def fold(block, _):
            end = jnp.minimum(rows[base + 2, block] & (BLK - 1), tasks - 1)
            part = running[end] * rows[base + 3, block].astype(jnp.float32)
            total[block] = part if first else total[block] + part
            return 0

        lax.fori_loop(0, BLOCKS, fold, 0)

    for sweep in range(SWEEPS):
        if sweep == 0:
            rounds = [value_copies, far_value_copies, last_copies]
        else:
            for copies in rounds:
                for copy in copies:
                    copy.wait_send()
            finish_rest(lent, passed)
            lent = lend(1)
            lax.fori_loop(0, DEVICES, pack_near_values, 0)
            pack_values(1, 0)
            first_copies = exchange(5, *values(1, 0, 2))
            pack_values(2, 2)
            keep_own(1, range(SLOTS))
            passed = pass_on(1, lent)
            rounds = [first_copies, exchange(6, *values(1, 2, 1))]

        for chunk in range(CHUNKS):
            for copies in rounds:
                for copy in copies[chunk * PLACES : (chunk + 1) * PLACES]:
                    copy.wait_recv()
            accumulate(recv[sweep][chunk], tiles[chunk], TASKS, table, chunk * 8, chunk == 0)

        for side in range(2):
            on_core(side, sides[side], lambda place: passed[place].wait_recv())
        for apart in range(RANKS):
            for piece in range(PIECES):
                rest_values[apart, piece * ROWS : (piece + 1) * ROWS] = relay_recv[sweep][
                    apart * PIECES + piece
                ]
        accumulate(rest_values, rest_tiles, RANKS, rest, 0, False)

        for block in range(BLOCKS):
            lanes = pl.ds(block * BLK, BLK)
            current = emission[:, lanes] + albedo[:, lanes] * total[block]
            if sweep + 1 < SWEEPS:
                scaled[block] = (current * areas[:, lanes]).astype(jnp.bfloat16)
            else:
                out[:, lanes] = current
    for copies in [near_copies, far_copies] + rounds:
        for copy in copies:
            copy.wait_send()
    finish_rest(lent, passed)


def fused(near_index, near_code, owned, emission, areas, albedo, geometry):
    smem = pl.BlockSpec(memory_space=pltpu.SMEM)
    vmem = pl.BlockSpec(memory_space=pltpu.VMEM)
    values = pltpu.VMEM((TASKS, BANDS, BLK), jnp.bfloat16)
    tile = pltpu.VMEM((TASKS, BLK, BLK), jnp.bfloat16)
    message = pltpu.VMEM((DEVICES, 16, BLK), jnp.float32)
    lent = pltpu.VMEM((DEVICES, ROWS, BLK), jnp.bfloat16)
    passed = pltpu.VMEM((RELAYS, ROWS, BLK), jnp.bfloat16)
    return pl.pallas_call(
        fused_kernel,
        in_specs=[smem] * 2 + [vmem] * 5,
        out_specs=[vmem, vmem],
        out_shape=[
            jax.ShapeDtypeStruct(emission.shape, jnp.float32),
            jax.ShapeDtypeStruct((8, BLK), jnp.float32),
        ],
        scratch_shapes=[
            pltpu.VMEM((BLOCKS, BANDS, BLK), jnp.bfloat16),
            pltpu.VMEM((BLOCKS, BANDS, BLK), jnp.float32),
            pltpu.VMEM((TASKS, BANDS, BLK), jnp.float32),
            pltpu.VMEM((DEVICES * SLOTS, BANDS, BLK), jnp.bfloat16),
            message,
            message,
            message,
            message,
            pltpu.VMEM((DEVICES, BLK), jnp.float32),
            pltpu.VMEM((CHUNKS * 8 + 8, BLK), jnp.int32),
            pltpu.SMEM((CHUNKS * 8 + 8, BLK), jnp.int32),
            pltpu.VMEM((8, BLK), jnp.int32),
            pltpu.SMEM((8, BLK), jnp.int32),
        ]
        + [tile] * CHUNKS
        + [values] * (SWEEPS * CHUNKS)
        + [passed, lent, lent, lent, passed, passed]
        + [
            pltpu.VMEM((RANKS, BLK, BLK), jnp.bfloat16),
            pltpu.VMEM((RANKS, BANDS, BLK), jnp.bfloat16),
            pltpu.SemaphoreType.DMA((11 * PEERS,)),
            pltpu.SemaphoreType.DMA((11 * PEERS,)),
            pltpu.SemaphoreType.DMA((2,)),
        ],
        compiler_params=pltpu.CompilerParams(
            collective_id=0, has_side_effects=True, vmem_limit_bytes=62 << 20
        ),
        name="fused",
    )(near_index, near_code, owned, emission, areas, albedo, geometry)


def on_device(
    emission, positions, normals, areas, material, reflect, pair_local, pair_device, pair_block
):
    grp, dev = lax.axis_index("grp"), lax.axis_index("dev")
    pairs = pair_local.shape[0]

    target = pair_device[:, 0]
    pair_order = jnp.arange(pairs, dtype=jnp.int32)
    earlier = (target[:, None] == target[None, :]) & (pair_order[None, :] < pair_order[:, None])
    slot = target * 2 + jnp.sum(earlier.astype(jnp.int32), 1)
    code = pair_block * BLOCKS + pair_local
    own = jnp.max(
        jnp.where(
            slot[:, None] == jnp.arange(2 * DEVICES, dtype=jnp.int32)[None, :], code[:, None], -1
        ),
        0,
    )
    own = own.reshape(DEVICES, 2)

    steps = np.array(ORDER + [(0, 0, 0, 0)], np.int32).T
    there = peer(grp, dev, steps)
    here = peer(grp, dev, (-steps) % np.array([[4], [2], [4], [4]], np.int32))
    own_there = own[there[0] * 16 + there[1]]
    own_here = own[here[0] * 16 + here[1]]
    near_index = jnp.where(own_there >= 0, own_there % BLOCKS, 0)
    here = (here[0] * 16 + here[1])[None, :]
    owned = jnp.concatenate([own_here.T, here, jnp.zeros((5, DEVICES), jnp.int32)], 0)

    class_hot = (
        jnp.arange(reflect.shape[1], dtype=jnp.int32)[:, None] == material[None, :]
    ).astype(jnp.float32)
    albedo = jnp.dot(reflect, class_hot, precision=lax.Precision.HIGHEST)
    geometry = jnp.concatenate([positions, normals, jnp.zeros((2, positions.shape[1]))], 0)
    geometry = geometry.astype(jnp.float32).reshape(8, BLOCKS, BLK).transpose(1, 0, 2)

    radiosity, crowded = fused(
        near_index.reshape(-1),
        own_there.astype(jnp.float32).reshape(-1),
        owned,
        emission,
        areas[None, :],
        albedo,
        geometry,
    )
    return lax.cond(
        crowded[0, 0] <= RANKS,
        lambda: radiosity,
        lambda: general(
            emission,
            positions,
            normals,
            areas,
            material,
            reflect,
            pair_local,
            pair_device,
            pair_block,
        ),
    )


def solution(mesh):
    return jax.shard_map(
        on_device,
        mesh=mesh,
        in_specs=(
            P(None, AXES),
            P(None, AXES),
            P(None, AXES),
            P(AXES),
            P(AXES),
            P(),
            P(AXES),
            P(AXES, None),
            P(AXES),
        ),
        out_specs=P(None, AXES),
        check_vma=False,
    )
```

```python
import math

import jax
import jax.numpy as jnp
import numpy as np
from jax import lax
from jax.experimental import pallas as pl
from jax.experimental.pallas import tpu as pltpu
from jax.sharding import PartitionSpec as P

BLK = 128
SWEEPS = 2
AXES = ("grp", "dev")
DEVICES = 128
BLOCKS = 32
BANDS = 64
RANKS = 16
PIECES = 4
RELAYS = RANKS * PIECES
ROWS = 64 // PIECES
HALVES = 2
PLACES = DEVICES // HALVES
FEATURES = 64
MISC = 32
MESH = pl.DeviceIdType.MESH
softening = 0.5


def view_tile(near, far):
    distance_sq = softening
    facing_near = 0.0
    facing_far = 0.0
    for axis_index in range(3):
        offset = far[:, axis_index, None, :] - near[:, axis_index, :, None]
        distance_sq = distance_sq + offset * offset
        facing_near = facing_near + near[:, 3 + axis_index, :, None] * offset
        facing_far = facing_far - far[:, 3 + axis_index, None, :] * offset
    return (
        jnp.maximum(facing_near, 0.0)
        * jnp.maximum(facing_far, 0.0)
        / (math.pi * distance_sq * distance_sq)
    )


def general(
    emission, positions, normals, areas, material, reflect, pair_local, pair_device, pair_block
):
    band_count, patch_count = emission.shape
    local_blocks = patch_count // BLK
    device_count = lax.axis_size(("grp", "dev"))
    pair_count = pair_local.shape[0]
    capacity = max(2, (2 * pair_count + device_count - 1) // device_count)
    slot_total = device_count * capacity
    target = pair_device[:, 0]
    target_hot = (target[:, None] == jnp.arange(device_count, dtype=jnp.int32)[None, :]).astype(
        jnp.int32
    )
    earlier = jnp.cumsum(target_hot, 0) - target_hot
    slot_index = target * capacity + jnp.sum(earlier * target_hot, 1)
    wanted = jnp.zeros((slot_total,), jnp.int32).at[slot_index].set(pair_block)
    asked_for = lax.all_to_all(wanted, ("grp", "dev"), split_axis=0, concat_axis=0, tiled=True)
    geometry = jnp.concatenate([positions, normals, areas[None, :]], 0)
    geometry = geometry.reshape(7, local_blocks, BLK).transpose(1, 0, 2)
    lent_geometry = geometry[asked_for]
    served = lax.all_to_all(lent_geometry, ("grp", "dev"), split_axis=0, concat_axis=0, tiled=True)
    far_geometry = served[slot_index]
    near_geometry = geometry[pair_local]
    block_ids = jnp.arange(local_blocks, dtype=jnp.int32)
    local_hot = (pair_local[:, None] == block_ids[None, :]).astype(jnp.float32)
    asked_hot = (asked_for[:, None] == block_ids[None, :]).astype(jnp.float32)
    class_hot = (
        jnp.arange(reflect.shape[1], dtype=jnp.int32)[:, None] == material[None, :]
    ).astype(jnp.float32)
    albedo = jnp.dot(reflect, class_hot, precision=lax.Precision.HIGHEST)
    albedo = albedo.reshape(band_count, local_blocks, BLK).transpose(1, 0, 2)
    source = emission.reshape(band_count, local_blocks, BLK).transpose(1, 0, 2)
    area_blocks = geometry[:, 6, :]
    current = source
    for sweep_index in range(SWEEPS):
        scaled = (current * area_blocks[:, None, :]).astype(jnp.bfloat16)
        lent_values = scaled[asked_for]
        kernel = view_tile(near_geometry, far_geometry).astype(jnp.bfloat16)
        incoming = lax.all_to_all(
            lent_values, ("grp", "dev"), split_axis=0, concat_axis=0, tiled=True
        )
        to_near = jnp.einsum(
            "pnj,pij->pni", incoming[slot_index], kernel, preferred_element_type=jnp.float32
        )
        to_far = jnp.einsum(
            "pni,pij->pnj", scaled[pair_local], kernel, preferred_element_type=jnp.float32
        )
        replies = jnp.zeros((slot_total, band_count, BLK), jnp.float32).at[slot_index].set(to_far)
        returned = lax.all_to_all(replies, ("grp", "dev"), split_axis=0, concat_axis=0, tiled=True)
        gathered = jnp.einsum("pb,pnk->bnk", local_hot, to_near, precision=lax.Precision.HIGHEST)
        gathered = gathered + jnp.einsum(
            "sb,snk->bnk", asked_hot, returned, precision=lax.Precision.HIGHEST
        )
        current = source + albedo * gathered
    return current.transpose(1, 0, 2).reshape(band_count, patch_count)


def torus_order():
    seen = set()
    groups = []
    for dx in range(4):
        for dy in range(4):
            for dz in range(4):
                for core in range(2):
                    group = []
                    for x, y, z in ((dx, dy, dz), (dy, dz, dx), (dz, dx, dy)):
                        for step in ((x, core, y, z), (-x % 4, core, -y % 4, -z % 4)):
                            if step not in seen and any(step):
                                seen.add(step)
                                group.append(step)
                    if group:
                        groups.append(group)
    groups.sort(key=lambda group: sum(min(v, 4 - v) for v in group[0][:1] + group[0][2:]))
    return [step for group in groups for step in group]


ORDER = torus_order()
PEERS = len(ORDER)


def peer(grp, dev, step):
    x, core, y, z = step
    return (
        lax.rem(grp // 2 + x, 4) * 2 + lax.rem(lax.rem(grp, 2) + core, 2),
        lax.rem(dev // 4 + y, 4) * 4 + lax.rem(lax.rem(dev, 4) + z, 4),
    )


def opposite(step):
    x, core, y, z = step
    return (-x % 4, core, -y % 4, -z % 4)


BACK = [ORDER.index(opposite(step)) for step in ORDER] + [PEERS]


TURNS = [list(range(PEERS)), list(range(PEERS))[::-1]]


def across(row):
    return jnp.broadcast_to(row, (BLK, BLK))


def down(row):
    return jnp.broadcast_to(row, (BLK, BLK)).T


def column_sum(terms):
    return jnp.sum(terms, 0, keepdims=True)


def sort_rows(mine, names, lane):
    lane_row = lane[:1]
    key = mine * BLK + lane_row
    rank = column_sum(jnp.where(down(key) < across(key), 1.0, 0.0))
    at_rank = down(rank) == lane
    order = column_sum(jnp.where(at_rank, names, 0.0))
    mine_down = down(mine)
    sorted_mine = column_sum(jnp.where(at_rank, mine_down, 0.0))
    before = pltpu.roll(jnp.broadcast_to(sorted_mine, (8, BLK)), 1, 1)[:1]
    keep = jnp.where((sorted_mine == before) & (lane_row > 0), 1.0, 0.0)
    upto = column_sum(jnp.where(mine_down <= lane, 1.0, 0.0))
    has = column_sum(jnp.where(mine_down == lane, 1.0, 0.0))
    return [order, keep, jnp.maximum(upto - 1.0, 0.0), jnp.minimum(has, 1.0)]


def iotas():
    row = lax.broadcasted_iota(jnp.int32, (BLK, BLK), 0)
    lane = lax.broadcasted_iota(jnp.int32, (BLK, BLK), 1)
    return row, lane


def route(asked, owned, out):
    row, lane = iotas()
    lane_row = lane[:1]
    lane = lane.astype(jnp.float32)
    asked0, asked1, owned0, owned1 = asked[0:1], asked[1:2], owned[0:1], owned[1:2]
    owned_mine = owned1 & (BLOCKS - 1)
    first_near = jnp.where(asked0 >= 0, asked0 >> 5, BLOCKS)
    first_far = jnp.where(owned0 >= 0, owned0 & (BLOCKS - 1), BLOCKS)
    second = jnp.where(asked1 >= 0, asked1 >> 5, jnp.where(owned1 >= 0, owned_mine, BLOCKS))

    def shifted(values, lanes):
        return pltpu.roll(jnp.broadcast_to(values, (8, BLK)), lanes % BLK, 1)[:1]

    low = lane_row < PLACES
    paired = ((row % PLACES) * 2 + row // PLACES).astype(jnp.float32)
    single = row.astype(jnp.float32)
    for half in range(HALVES):
        shift = -half * PLACES
        both = jnp.where(low, shifted(first_near, shift), shifted(first_far, shift + PLACES))
        last = jnp.where(low, shifted(second, shift), BLOCKS)
        for table, mine, names in ((half, both, paired), (HALVES + half, last, single)):
            mine = mine.astype(jnp.float32)
            rows = sort_rows(mine, names, lane)
            rows += [jnp.minimum(mine, BLOCKS - 1.0), jnp.zeros((3, BLK), jnp.float32)]
            out[table * 8 : table * 8 + 8] = jnp.concatenate(rows, 0).astype(jnp.int32)
    asked_first = jnp.where(asked0 >= 0, asked0 >> 5, 0)
    asked_second = jnp.where(asked1 >= 0, asked1 >> 5, 0)
    both = (owned1 >= 0) & (asked1 >= 0)
    crowded = jnp.max(jnp.where(both, 1.0, 0.0), 1, keepdims=True)
    out[MISC : MISC + 8] = jnp.concatenate(
        [
            asked_first,
            asked_second,
            jnp.where(owned1 >= 0, owned_mine, asked_second),
            (asked1 >= 0).astype(jnp.int32),
            jnp.broadcast_to(crowded, (1, BLK)).astype(jnp.int32),
            jnp.zeros((3, BLK), jnp.int32),
        ],
        0,
    )


def route_rest(crowded, asked, owned, relay_shift, out):
    row, lane = iotas()
    lane = lane.astype(jnp.float32)
    lane_row = lane[:1]
    asked1, owned1 = asked[1:2], owned[1:2]
    ids = owned[2:3].astype(jnp.float32)
    rank = column_sum(jnp.where(down(ids) < across(ids), down(crowded), 0.0))
    rank_down = down(rank)
    hot_down = down(crowded) > 0.5
    my_rank = jnp.sum(jnp.where(lane_row == PEERS, rank, 0.0), 1, keepdims=True)
    count = jnp.sum(crowded, 1, keepdims=True)

    def pick(wanted, terms):
        wanted = jnp.where(wanted >= RANKS, wanted - RANKS, wanted)
        wanted = jnp.where(wanted < 0, wanted + RANKS, wanted)
        return column_sum(jnp.where(hot_down & (rank_down == across(wanted)), terms, 0.0))

    ahead = my_rank + lane_row
    behind = my_rank - lane_row
    asked_second = jnp.where(asked1 >= 0, asked1 >> 5, 0).astype(jnp.float32)
    both = (owned1 >= 0) & (asked1 >= 0)
    mine = jnp.where(both, owned1 & (BLOCKS - 1), BLOCKS).astype(jnp.float32)
    places = row.astype(jnp.float32)
    lend = pick(ahead, down(asked_second))
    source = pick(behind, places)
    found = pick(behind, jnp.ones((BLK, BLK), jnp.float32))
    mine = jnp.where((lane_row < RANKS) & (found > 0.5), pick(behind, down(mine)), float(BLOCKS))
    relay = pick(rank - relay_shift, places)
    rows = sort_rows(mine, places, lane)
    rows += [jnp.minimum(mine, BLOCKS - 1.0), lend, source, relay]
    out[...] = jnp.concatenate(rows, 0).astype(jnp.int32)
    return count


def with_norms(rows, extra):
    points, normals = rows[0:3], rows[3:6]
    square = points * points
    product = points * normals
    return jnp.concatenate(
        [
            rows[0:6],
            square[0:1] + square[1:2] + square[2:3] + extra,
            -(product[0:1] + product[1:2] + product[2:3]),
        ],
        0,
    )


def split(values):
    high = values.astype(jnp.bfloat16).astype(jnp.float32)
    rest = values - high
    middle = rest.astype(jnp.bfloat16).astype(jnp.float32)
    return high, middle, rest - middle


def other_features(rows):
    high, middle, low = split(with_norms(rows, softening))
    ones = jnp.where(lax.broadcasted_iota(jnp.int32, (8, BLK), 0) < 3, 1.0, 0.0)
    parts = [high, high, middle, middle, high, low, ones, jnp.zeros((8, BLK), jnp.float32)]
    return jnp.concatenate(parts, 0).T.astype(jnp.bfloat16)


def own_features(rows):
    pieces = split(with_norms(rows, 0.0))
    zero = jnp.zeros((1, BLK), jnp.float32)
    zeros3 = jnp.zeros((3, BLK), jnp.float32)
    columns = ([], [], [])
    for which in (0, 1, 0, 1, 2, 0):
        part = pieces[which]
        one = zero + 1.0 if which == 0 else zero
        columns[0].append(jnp.concatenate([part[3:6], zeros3, zero, zero], 0))
        columns[1].append(jnp.concatenate([zeros3, part[0:3], zero, one], 0))
        columns[2].append(jnp.concatenate([-2.0 * part[0:3], zeros3, one, zero], 0))
    tail = jnp.zeros((5, BLK), jnp.float32)
    blank = jnp.zeros((8, BLK), jnp.float32)
    for column, row in ((0, 7), (1, None), (2, 6)):
        if row is None:
            columns[column].append(blank)
        else:
            columns[column].append(
                jnp.concatenate([part[row : row + 1] for part in pieces] + [tail], 0)
            )
        columns[column].append(blank)
    return [jnp.concatenate(column, 0).astype(jnp.bfloat16) for column in columns]


def tile(rows, own):
    forms = jnp.dot(other_features(rows), own, preferred_element_type=jnp.float32)
    facing = jnp.maximum(forms[:, :BLK], 0.0) * jnp.maximum(forms[:, BLK : 2 * BLK], 0.0)
    distance_sq = forms[:, 2 * BLK :]
    bottom = math.pi * distance_sq * distance_sq
    inverse = pl.reciprocal(bottom, approx=True)
    inverse = inverse * (2.0 - bottom * inverse)
    return (facing * inverse).astype(jnp.bfloat16)


def fused_kernel(
    near_code,
    owned,
    emission,
    areas,
    material,
    reflect,
    positions,
    normals,
    out,
    fits,
    geometry,
    features,
    albedo,
    classes,
    scaled,
    total,
    running,
    send,
    last_send,
    near_send,
    near_recv,
    far_send,
    far_recv,
    asked_rows,
    table_rows,
    table,
    rest_rows,
    rest,
    tiles0,
    tiles1,
    last_tiles0,
    last_tiles1,
    recv00,
    recv01,
    recv10,
    recv11,
    last_recv00,
    last_recv01,
    last_recv10,
    last_recv11,
    lend_send,
    lend_recv0,
    lend_recv1,
    relay_send,
    relay_recv0,
    relay_recv1,
    rest_tiles,
    rest_values,
    send_sem,
    recv_sem,
    table_sem,
):
    tiles = (tiles0, tiles1)
    last_tiles = (last_tiles0, last_tiles1)
    recv = ((recv00, recv01), (recv10, recv11))
    last_recv = ((last_recv00, last_recv01), (last_recv10, last_recv11))
    lend_recv = (lend_recv0, lend_recv1)
    relay_recv = (relay_recv0, relay_recv1)
    grp, dev = lax.axis_index("grp"), lax.axis_index("dev")
    core = lax.rem(grp, 2)
    chip = (grp // 2) * 16 + dev
    peers = [peer(grp, dev, step) for step in ORDER]
    barrier = pltpu.get_barrier_semaphore()
    for other in peers:
        pl.semaphore_signal(barrier, inc=1, device_id=other, device_id_type=MESH)

    def describe(kind, source, target):
        return [
            pltpu.make_async_remote_copy(
                src_ref=source(place),
                dst_ref=target(place),
                send_sem=send_sem.at[kind * PEERS + place],
                recv_sem=recv_sem.at[kind * PEERS + place],
                device_id=other,
                device_id_type=MESH,
            )
            for place, other in enumerate(peers)
        ]

    def exchange(kind, source, target):
        copies = describe(kind, source, target)
        for turn in range(2):

            @pl.when(core == turn)
            def _():
                for place in TURNS[turn]:
                    copies[place].start()

        return copies

    def firsts(sweep, first, count):
        def source(place):
            return send.at[pl.ds(place * 2 + first, count)]

        def target(place):
            half = recv[sweep][place // PLACES]
            return half.at[pl.ds(place % PLACES * 2 + first, count)]

        return source, target

    def lasts(sweep):
        def target(place):
            return last_recv[sweep][place // PLACES].at[place % PLACES]

        return lambda place: last_send.at[place], target

    def near_index(place, slot):
        return near_code[place * 2 + slot] & (BLOCKS - 1)

    def sent(row, place):
        return table[MISC + row, BACK[place]] & (BLOCKS - 1)

    def pack_near_values():
        def pack(place, _):
            send[place * 2] = scaled[near_index(place, 0)]
            return 0

        lax.fori_loop(0, DEVICES, pack, 0)

    def pack_far_values():
        for place in range(DEVICES):
            send[place * 2 + 1] = scaled[sent(0, place)]

    def pack_last_values(sweep):
        for place in range(DEVICES):
            last_send[place] = scaled[sent(2, place)]
        last_recv[sweep][1][PLACES - 1] = last_send[PEERS]

    def keep_own(sweep):
        for slot in range(2):
            recv[sweep][1][PLACES * 2 - 2 + slot] = send[PEERS * 2 + slot]

    sides = [[place for place in range(PEERS) if ORDER[place][1] == side] for side in range(2)]

    def on_core(side, places, act):
        @pl.when(core == side)
        def _():
            for place in places:
                act(place)

    def lend(sweep):
        for apart in range(RANKS):
            block = scaled[rest[5, apart] & (BLOCKS - 1)]
            for piece in range(PIECES):
                lend_send[apart * PIECES + piece] = block[piece * ROWS : (piece + 1) * ROWS]
        lend_recv[sweep][PEERS] = lend_send[chip]
        copies = describe(
            7 + sweep,
            lambda place: lend_send.at[(peers[place][0] // 2) * 16 + peers[place][1]],
            lambda place: lend_recv[sweep].at[place],
        )
        for side in range(2):
            on_core(side, sides[side], lambda place: copies[place].start())
        return copies

    def pass_on(sweep, lent):
        on_core(0, range(PEERS), lambda place: lent[place].wait_recv())
        copies = describe(
            9 + sweep,
            lambda place: relay_send.at[place],
            lambda place: relay_recv[sweep].at[chip],
        )

        @pl.when(core == 0)
        def _():
            for place in range(DEVICES):
                relay_send[place] = lend_recv[sweep][rest[7, BACK[place]] & (DEVICES - 1)]
            relay_recv[sweep][chip] = relay_send[PEERS]
            for place in range(PEERS):
                copies[place].start()

        return copies

    def finish_rest(lent, passed):
        for side in range(2):
            on_core(side, sides[side], lambda place: lent[place].wait_send())
        on_core(0, range(PEERS), lambda place: passed[place].wait_send())

    for block in range(BLOCKS):
        lanes = pl.ds(block * BLK, BLK)
        geometry[block] = jnp.concatenate(
            [positions[:, lanes], normals[:, lanes], jnp.zeros((2, BLK), jnp.float32)], 0
        )
    lane = lax.broadcasted_iota(jnp.int32, (4, BLK), 1)

    def pack_near(place, _):
        first, second = near_code[place * 2], near_code[place * 2 + 1]
        codes = jnp.where(lane == 0, first, jnp.where(lane == 1, second, 0)).astype(jnp.float32)
        rows = [geometry[near_index(place, slot)][:6] for slot in range(2)]
        near_send[place] = jnp.concatenate(rows + [codes], 0)
        return 0

    lax.fori_loop(0, DEVICES, pack_near, 0)
    near_recv[PEERS] = near_send[PEERS]
    for block in range(BLOCKS):
        lanes = pl.ds(block * BLK, BLK)
        scaled[block] = (emission[:, lanes] * areas[:, lanes]).astype(jnp.bfloat16)
    pl.semaphore_wait(barrier, PEERS)
    near_copies = exchange(0, lambda place: near_send.at[place], lambda place: near_recv.at[place])
    pack_near_values()
    value_copies = exchange(2, *firsts(0, 0, 1))

    for which in range(classes.shape[0]):
        classes[which] = jnp.broadcast_to(reflect[:, which : which + 1], (BANDS, BLK))
    for block in range(BLOCKS):
        lanes = pl.ds(block * BLK, BLK)
        row = material[:, lanes]
        part = classes[0]
        for which in range(1, classes.shape[0]):
            part = jnp.where(row == which, classes[which], part)
        albedo[:, lanes] = part

    def build_features(block, _):
        for index, column in enumerate(own_features(geometry[block])):
            features[block, :, index * BLK : (index + 1) * BLK] = column
        return 0

    lax.fori_loop(0, BLOCKS, build_features, 0)

    for copy in near_copies:
        copy.wait_recv()

    def collect_asked(place, _):
        asked_rows[pl.ds(place, 1)] = near_recv[place, 12:13]
        return 0

    lax.fori_loop(0, DEVICES, collect_asked, 0)
    asked = asked_rows[...].T[:8].astype(jnp.int32)
    route(asked, owned[...], table_rows)
    to_table = pltpu.make_async_copy(table_rows, table, table_sem.at[0])
    to_table.start()
    to_table.wait()

    crowded_row = table_rows[MISC + 4 : MISC + 5].astype(jnp.float32)
    blank = jnp.zeros((3, BLK), jnp.float32)
    for place in range(DEVICES):
        rows = [geometry[sent(slot, place)][:6] for slot in range(2)]
        far_send[place] = jnp.concatenate(rows + [crowded_row, blank], 0)
    far_recv[PEERS] = far_send[PEERS]
    far_copies = exchange(1, lambda place: far_send.at[place], lambda place: far_recv.at[place])
    pack_far_values()
    keep_own(0)
    far_value_copies = exchange(3, *firsts(0, 1, 1))

    def own_side(group, task):
        return features[table[group * 8 + 4, task] & (BLOCKS - 1)]

    def build(source, slot, half):
        def step(pair, _):
            for inner in range(2):
                place = pair * 2 + inner
                rows = source[half * PLACES + place][:6]
                tiles[half][place * 2 + slot] = tile(rows, own_side(half, slot * PLACES + place))
            return 0

        lax.fori_loop(0, PLACES // 2, step, 0)

    for half in range(HALVES):
        build(near_recv, 0, half)

    for copy in far_copies:
        copy.wait_recv()

    def collect_crowded(place, _):
        asked_rows[pl.ds(place, 1)] = far_recv[place, 12:13]
        return 0

    lax.fori_loop(0, DEVICES, collect_crowded, 0)
    crowded = asked_rows[...].T[:1]
    shift = (chip // PIECES).astype(jnp.float32)
    count = route_rest(crowded, asked, owned[...], shift, rest_rows)
    fits[...] = jnp.broadcast_to(count, (8, BLK))
    to_rest = pltpu.make_async_copy(rest_rows, rest, table_sem.at[1])
    to_rest.start()
    to_rest.wait()
    lent = lend(0)
    pack_last_values(0)
    last_copies = exchange(4, *lasts(0))

    for half in range(HALVES):
        build(far_recv, 1, half)
    passed = pass_on(0, lent)

    for half in range(HALVES):

        def build_last(pair, _):
            for inner in range(2):
                place = pair * 2 + inner
                whole = half * PLACES + place
                near = table[MISC + 3, whole] > 0
                rows = jnp.where(near, near_recv[whole], far_recv[whole])[6:12]
                last_tiles[half][place] = tile(rows, own_side(HALVES + half, place))
            return 0

        lax.fori_loop(0, PLACES // 2, build_last, 0)

    def build_rest(apart, _):
        rows = far_recv[rest[6, apart] & (DEVICES - 1)][6:12]
        rest_tiles[apart] = tile(rows, features[rest[4, apart] & (BLOCKS - 1)])
        return 0

    lax.fori_loop(0, RANKS, build_rest, 0)

    def accumulate(values_ref, tiles_ref, rows, base, first):
        tasks = values_ref.shape[0]

        def add(group, run):
            for inner in range(8):
                task = group * 8 + inner
                index = rows[base, task] & (tasks - 1)
                run = run * rows[base + 1, task].astype(jnp.float32) + jnp.dot(
                    values_ref[index], tiles_ref[index], preferred_element_type=jnp.float32
                )
                running[task] = run
            return run

        lax.fori_loop(0, tasks // 8, add, jnp.zeros((BANDS, BLK), jnp.float32))

        def fold(block, _):
            part = running[rows[base + 2, block] & (tasks - 1)]
            part = part * rows[base + 3, block].astype(jnp.float32)
            total[block] = part if first else total[block] + part
            return 0

        lax.fori_loop(0, BLOCKS, fold, 0)

    for sweep in range(SWEEPS):
        if sweep == 0:
            rounds = [value_copies, far_value_copies]
        else:
            for copies in rounds + [last_copies]:
                for copy in copies:
                    copy.wait_send()
            finish_rest(lent, passed)
            lent = lend(1)
            pack_near_values()
            pack_far_values()
            rounds = [exchange(5, *firsts(1, 0, 2))]
            keep_own(1)
            pack_last_values(1)
            passed = pass_on(1, lent)
            last_copies = exchange(6, *lasts(1))

        for half in range(HALVES):
            for copies in rounds:
                for copy in copies[half * PLACES : (half + 1) * PLACES]:
                    copy.wait_recv()
            accumulate(recv[sweep][half], tiles[half], table, half * 8, half == 0)

        for side in range(2):
            on_core(side, sides[side], lambda place: passed[place].wait_recv())
        for apart in range(RANKS):
            for piece in range(PIECES):
                rest_values[apart, piece * ROWS : (piece + 1) * ROWS] = relay_recv[sweep][
                    apart * PIECES + piece
                ]
        accumulate(rest_values, rest_tiles, rest, 0, False)

        for half in range(HALVES):
            for copy in last_copies[half * PLACES : (half + 1) * PLACES]:
                copy.wait_recv()
            accumulate(
                last_recv[sweep][half], last_tiles[half], table, (HALVES + half) * 8, False
            )

        for block in range(BLOCKS):
            lanes = pl.ds(block * BLK, BLK)
            reflected = albedo[:, lanes] * total[block]
            if sweep + 1 < SWEEPS:
                current = emission[:, lanes] + reflected
                scaled[block] = (current * areas[:, lanes]).astype(jnp.bfloat16)
            else:
                out[:, lanes] = reflected
    for copies in [near_copies, far_copies, last_copies] + rounds:
        for copy in copies:
            copy.wait_send()
    finish_rest(lent, passed)


def fused(near_code, owned, emission, areas, material, reflect, positions, normals):
    smem = pl.BlockSpec(memory_space=pltpu.SMEM)
    vmem = pl.BlockSpec(memory_space=pltpu.VMEM)
    values = pltpu.VMEM((PLACES * 2, BANDS, BLK), jnp.bfloat16)
    last_values = pltpu.VMEM((PLACES, BANDS, BLK), jnp.bfloat16)
    tiles = pltpu.VMEM((PLACES * 2, BLK, BLK), jnp.bfloat16)
    last_tiles = pltpu.VMEM((PLACES, BLK, BLK), jnp.bfloat16)
    message = pltpu.VMEM((DEVICES, 16, BLK), jnp.float32)
    lent = pltpu.VMEM((DEVICES, ROWS, BLK), jnp.bfloat16)
    passed = pltpu.VMEM((RELAYS, ROWS, BLK), jnp.bfloat16)
    return pl.pallas_call(
        fused_kernel,
        in_specs=[smem] + [vmem] * 7,
        out_specs=[vmem, vmem],
        out_shape=[
            jax.ShapeDtypeStruct(emission.shape, jnp.float32),
            jax.ShapeDtypeStruct((8, BLK), jnp.float32),
        ],
        scratch_shapes=[
            pltpu.VMEM((BLOCKS, 8, BLK), jnp.float32),
            pltpu.VMEM((BLOCKS, FEATURES, 3 * BLK), jnp.bfloat16),
            pltpu.VMEM(emission.shape, jnp.float32),
            pltpu.VMEM((reflect.shape[1], BANDS, BLK), jnp.float32),
            pltpu.VMEM((BLOCKS, BANDS, BLK), jnp.bfloat16),
            pltpu.VMEM((BLOCKS, BANDS, BLK), jnp.float32),
            pltpu.VMEM((PLACES * 2, BANDS, BLK), jnp.float32),
            pltpu.VMEM((DEVICES * 2, BANDS, BLK), jnp.bfloat16),
            pltpu.VMEM((DEVICES, BANDS, BLK), jnp.bfloat16),
            message,
            message,
            message,
            message,
            pltpu.VMEM((DEVICES, BLK), jnp.float32),
            pltpu.VMEM((MISC + 8, BLK), jnp.int32),
            pltpu.SMEM((MISC + 8, BLK), jnp.int32),
            pltpu.VMEM((8, BLK), jnp.int32),
            pltpu.SMEM((8, BLK), jnp.int32),
        ]
        + [tiles] * HALVES
        + [last_tiles] * HALVES
        + [values] * (SWEEPS * HALVES)
        + [last_values] * (SWEEPS * HALVES)
        + [passed, lent, lent, lent, passed, passed]
        + [
            pltpu.VMEM((RANKS, BLK, BLK), jnp.bfloat16),
            pltpu.VMEM((RANKS, BANDS, BLK), jnp.bfloat16),
            pltpu.SemaphoreType.DMA((11 * PEERS,)),
            pltpu.SemaphoreType.DMA((11 * PEERS,)),
            pltpu.SemaphoreType.DMA((2,)),
        ],
        compiler_params=pltpu.CompilerParams(
            collective_id=0, has_side_effects=True, vmem_limit_bytes=62 << 20
        ),
        name="fused",
    )(near_code, owned, emission, areas, material, reflect, positions, normals)


def on_device(
    emission, positions, normals, areas, material, reflect, pair_local, pair_device, pair_block
):
    grp, dev = lax.axis_index("grp"), lax.axis_index("dev")
    pairs = pair_local.shape[0]

    steps = np.array(ORDER + [(0, 0, 0, 0)], np.int32).T
    there = peer(grp, dev, steps)
    there = there[0] * 16 + there[1]
    here = peer(grp, dev, (-steps) % np.array([[4], [2], [4], [4]], np.int32))
    here = here[0] * 16 + here[1]
    target = pair_device[:, 0]
    pair_order = jnp.arange(pairs, dtype=jnp.int32)
    earlier = (target[:, None] == target[None, :]) & (pair_order[None, :] < pair_order[:, None])
    second = jnp.any(earlier, 1)
    code = pair_block * BLOCKS + pair_local

    def named(ids, is_second):
        found = (target[None, :] == ids[:, None]) & (second == is_second)[None, :]
        return jnp.max(jnp.where(found, code[None, :], -1), 1)

    near_code = jnp.stack([named(there, False), named(there, True)], 1).reshape(-1)
    owned = jnp.stack([named(here, False), named(here, True), here] + [here * 0] * 5, 0)

    reflected, crowded = fused(
        near_code,
        owned,
        emission,
        areas[None, :],
        material[None, :],
        reflect,
        positions,
        normals,
    )
    return lax.cond(
        crowded[0, 0] <= RANKS,
        lambda: emission + reflected,
        lambda: general(
            emission,
            positions,
            normals,
            areas,
            material,
            reflect,
            pair_local,
            pair_device,
            pair_block,
        ),
    )


def solution(mesh):
    return jax.shard_map(
        on_device,
        mesh=mesh,
        in_specs=(
            P(None, AXES),
            P(None, AXES),
            P(None, AXES),
            P(AXES),
            P(AXES),
            P(),
            P(AXES),
            P(AXES, None),
            P(AXES),
        ),
        out_specs=P(None, AXES),
        check_vma=False,
    )
```

```python
import math

import jax
import jax.numpy as jnp
import numpy as np
from jax import lax
from jax.experimental import pallas as pl
from jax.experimental.pallas import tpu as pltpu
from jax.sharding import PartitionSpec as P

BLK = 128
SWEEPS = 2
AXES = ("grp", "dev")
DEVICES = 128
BLOCKS = 32
BANDS = 64
RANKS = 16
PIECES = 4
RELAYS = RANKS * PIECES
ROWS = 64 // PIECES
HALVES = 2
PLACES = DEVICES // HALVES
FEATURES = 64
MISC = 32
MESH = pl.DeviceIdType.MESH
softening = 0.5


def view_tile(near, far):
    distance_sq = softening
    facing_near = 0.0
    facing_far = 0.0
    for axis_index in range(3):
        offset = far[:, axis_index, None, :] - near[:, axis_index, :, None]
        distance_sq = distance_sq + offset * offset
        facing_near = facing_near + near[:, 3 + axis_index, :, None] * offset
        facing_far = facing_far - far[:, 3 + axis_index, None, :] * offset
    return (
        jnp.maximum(facing_near, 0.0)
        * jnp.maximum(facing_far, 0.0)
        / (math.pi * distance_sq * distance_sq)
    )


def general(
    emission, positions, normals, areas, material, reflect, pair_local, pair_device, pair_block
):
    band_count, patch_count = emission.shape
    local_blocks = patch_count // BLK
    device_count = lax.axis_size(("grp", "dev"))
    pair_count = pair_local.shape[0]
    capacity = max(2, (2 * pair_count + device_count - 1) // device_count)
    slot_total = device_count * capacity
    target = pair_device[:, 0]
    target_hot = (target[:, None] == jnp.arange(device_count, dtype=jnp.int32)[None, :]).astype(
        jnp.int32
    )
    earlier = jnp.cumsum(target_hot, 0) - target_hot
    slot_index = target * capacity + jnp.sum(earlier * target_hot, 1)
    wanted = jnp.zeros((slot_total,), jnp.int32).at[slot_index].set(pair_block)
    asked_for = lax.all_to_all(wanted, ("grp", "dev"), split_axis=0, concat_axis=0, tiled=True)
    geometry = jnp.concatenate([positions, normals, areas[None, :]], 0)
    geometry = geometry.reshape(7, local_blocks, BLK).transpose(1, 0, 2)
    lent_geometry = geometry[asked_for]
    served = lax.all_to_all(lent_geometry, ("grp", "dev"), split_axis=0, concat_axis=0, tiled=True)
    far_geometry = served[slot_index]
    near_geometry = geometry[pair_local]
    block_ids = jnp.arange(local_blocks, dtype=jnp.int32)
    local_hot = (pair_local[:, None] == block_ids[None, :]).astype(jnp.float32)
    asked_hot = (asked_for[:, None] == block_ids[None, :]).astype(jnp.float32)
    class_hot = (
        jnp.arange(reflect.shape[1], dtype=jnp.int32)[:, None] == material[None, :]
    ).astype(jnp.float32)
    albedo = jnp.dot(reflect, class_hot, precision=lax.Precision.HIGHEST)
    albedo = albedo.reshape(band_count, local_blocks, BLK).transpose(1, 0, 2)
    source = emission.reshape(band_count, local_blocks, BLK).transpose(1, 0, 2)
    area_blocks = geometry[:, 6, :]
    current = source
    for sweep_index in range(SWEEPS):
        scaled = (current * area_blocks[:, None, :]).astype(jnp.bfloat16)
        lent_values = scaled[asked_for]
        kernel = view_tile(near_geometry, far_geometry).astype(jnp.bfloat16)
        incoming = lax.all_to_all(
            lent_values, ("grp", "dev"), split_axis=0, concat_axis=0, tiled=True
        )
        to_near = jnp.einsum(
            "pnj,pij->pni", incoming[slot_index], kernel, preferred_element_type=jnp.float32
        )
        to_far = jnp.einsum(
            "pni,pij->pnj", scaled[pair_local], kernel, preferred_element_type=jnp.float32
        )
        replies = jnp.zeros((slot_total, band_count, BLK), jnp.float32).at[slot_index].set(to_far)
        returned = lax.all_to_all(replies, ("grp", "dev"), split_axis=0, concat_axis=0, tiled=True)
        gathered = jnp.einsum("pb,pnk->bnk", local_hot, to_near, precision=lax.Precision.HIGHEST)
        gathered = gathered + jnp.einsum(
            "sb,snk->bnk", asked_hot, returned, precision=lax.Precision.HIGHEST
        )
        current = source + albedo * gathered
    return current.transpose(1, 0, 2).reshape(band_count, patch_count)


def torus_order():
    seen = set()
    groups = []
    for dx in range(4):
        for dy in range(4):
            for dz in range(4):
                for core in range(2):
                    group = []
                    for x, y, z in ((dx, dy, dz), (dy, dz, dx), (dz, dx, dy)):
                        for step in ((x, core, y, z), (-x % 4, core, -y % 4, -z % 4)):
                            if step not in seen and any(step):
                                seen.add(step)
                                group.append(step)
                    if group:
                        groups.append(group)
    groups.sort(key=lambda group: sum(min(v, 4 - v) for v in group[0][:1] + group[0][2:]))
    return [step for group in groups for step in group]


ORDER = torus_order()
PEERS = len(ORDER)


def peer(grp, dev, step):
    x, core, y, z = step
    return (
        lax.rem(grp // 2 + x, 4) * 2 + lax.rem(lax.rem(grp, 2) + core, 2),
        lax.rem(dev // 4 + y, 4) * 4 + lax.rem(lax.rem(dev, 4) + z, 4),
    )


def opposite(step):
    x, core, y, z = step
    return (-x % 4, core, -y % 4, -z % 4)


BACK = [ORDER.index(opposite(step)) for step in ORDER] + [PEERS]


TURNS = [list(range(PEERS)), list(range(PEERS))[::-1]]


def across(row):
    return jnp.broadcast_to(row, (BLK, BLK))


def down(row):
    return jnp.broadcast_to(row, (BLK, BLK)).T


def column_sum(terms):
    return jnp.sum(terms, 0, keepdims=True)


def sort_rows(mine, names, lane):
    lane_row = lane[:1]
    key = mine * BLK + lane_row
    rank = column_sum(jnp.where(down(key) < across(key), 1.0, 0.0))
    at_rank = down(rank) == lane
    order = column_sum(jnp.where(at_rank, names, 0.0))
    mine_down = down(mine)
    sorted_mine = column_sum(jnp.where(at_rank, mine_down, 0.0))
    before = pltpu.roll(jnp.broadcast_to(sorted_mine, (8, BLK)), 1, 1)[:1]
    keep = jnp.where((sorted_mine == before) & (lane_row > 0), 1.0, 0.0)
    upto = column_sum(jnp.where(mine_down <= lane, 1.0, 0.0))
    has = column_sum(jnp.where(mine_down == lane, 1.0, 0.0))
    return [order, keep, jnp.maximum(upto - 1.0, 0.0), jnp.minimum(has, 1.0)]


def iotas():
    row = lax.broadcasted_iota(jnp.int32, (BLK, BLK), 0)
    lane = lax.broadcasted_iota(jnp.int32, (BLK, BLK), 1)
    return row, lane


def route(asked, owned, out):
    row, lane = iotas()
    lane_row = lane[:1]
    lane = lane.astype(jnp.float32)
    asked0, asked1, owned0, owned1 = asked[0:1], asked[1:2], owned[0:1], owned[1:2]
    owned_mine = owned1 & (BLOCKS - 1)
    first_near = jnp.where(asked0 >= 0, asked0 >> 5, BLOCKS)
    first_far = jnp.where(owned0 >= 0, owned0 & (BLOCKS - 1), BLOCKS)
    second = jnp.where(asked1 >= 0, asked1 >> 5, jnp.where(owned1 >= 0, owned_mine, BLOCKS))

    def shifted(values, lanes):
        return pltpu.roll(jnp.broadcast_to(values, (8, BLK)), lanes % BLK, 1)[:1]

    low = lane_row < PLACES
    paired = ((row % PLACES) * 2 + row // PLACES).astype(jnp.float32)
    single = row.astype(jnp.float32)
    for half in range(HALVES):
        shift = -half * PLACES
        both = jnp.where(low, shifted(first_near, shift), shifted(first_far, shift + PLACES))
        last = jnp.where(low, shifted(second, shift), BLOCKS)
        for table, mine, names in ((half, both, paired), (HALVES + half, last, single)):
            mine = mine.astype(jnp.float32)
            rows = sort_rows(mine, names, lane)
            rows += [jnp.minimum(mine, BLOCKS - 1.0), jnp.zeros((3, BLK), jnp.float32)]
            out[table * 8 : table * 8 + 8] = jnp.concatenate(rows, 0).astype(jnp.int32)
    asked_first = jnp.where(asked0 >= 0, asked0 >> 5, 0)
    asked_second = jnp.where(asked1 >= 0, asked1 >> 5, 0)
    both = (owned1 >= 0) & (asked1 >= 0)
    crowded = jnp.max(jnp.where(both, 1.0, 0.0), 1, keepdims=True)
    out[MISC : MISC + 8] = jnp.concatenate(
        [
            asked_first,
            asked_second,
            jnp.where(owned1 >= 0, owned_mine, asked_second),
            (asked1 >= 0).astype(jnp.int32),
            jnp.broadcast_to(crowded, (1, BLK)).astype(jnp.int32),
            jnp.zeros((3, BLK), jnp.int32),
        ],
        0,
    )


def route_rest(crowded, asked, owned, relay_shift, out):
    row, lane = iotas()
    lane = lane.astype(jnp.float32)
    lane_row = lane[:1]
    asked1, owned1 = asked[1:2], owned[1:2]
    ids = owned[2:3].astype(jnp.float32)
    rank = column_sum(jnp.where(down(ids) < across(ids), down(crowded), 0.0))
    rank_down = down(rank)
    hot_down = down(crowded) > 0.5
    my_rank = jnp.sum(jnp.where(lane_row == PEERS, rank, 0.0), 1, keepdims=True)
    count = jnp.sum(crowded, 1, keepdims=True)

    def pick(wanted, terms):
        wanted = jnp.where(wanted >= RANKS, wanted - RANKS, wanted)
        wanted = jnp.where(wanted < 0, wanted + RANKS, wanted)
        return column_sum(jnp.where(hot_down & (rank_down == across(wanted)), terms, 0.0))

    ahead = my_rank + lane_row
    behind = my_rank - lane_row
    asked_second = jnp.where(asked1 >= 0, asked1 >> 5, 0).astype(jnp.float32)
    both = (owned1 >= 0) & (asked1 >= 0)
    mine = jnp.where(both, owned1 & (BLOCKS - 1), BLOCKS).astype(jnp.float32)
    places = row.astype(jnp.float32)
    lend = pick(ahead, down(asked_second))
    source = pick(behind, places)
    found = pick(behind, jnp.ones((BLK, BLK), jnp.float32))
    mine = jnp.where((lane_row < RANKS) & (found > 0.5), pick(behind, down(mine)), float(BLOCKS))
    relay = pick(rank - relay_shift, places)
    rows = sort_rows(mine, places, lane)
    rows += [jnp.minimum(mine, BLOCKS - 1.0), lend, source, relay]
    out[...] = jnp.concatenate(rows, 0).astype(jnp.int32)
    return count


def with_norms(rows, extra):
    points, normals = rows[0:3], rows[3:6]
    square = points * points
    product = points * normals
    return jnp.concatenate(
        [
            rows[0:6],
            square[0:1] + square[1:2] + square[2:3] + extra,
            -(product[0:1] + product[1:2] + product[2:3]),
        ],
        0,
    )


def split(values):
    high = values.astype(jnp.bfloat16).astype(jnp.float32)
    rest = values - high
    middle = rest.astype(jnp.bfloat16).astype(jnp.float32)
    return high, middle, rest - middle


def other_features(rows):
    high, middle, low = split(with_norms(rows, softening))
    ones = jnp.where(lax.broadcasted_iota(jnp.int32, (8, BLK), 0) < 3, 1.0, 0.0)
    parts = [high, high, middle, middle, high, low, ones, jnp.zeros((8, BLK), jnp.float32)]
    return jnp.concatenate(parts, 0).T.astype(jnp.bfloat16)


def own_features(rows):
    pieces = split(with_norms(rows, 0.0))
    zero = jnp.zeros((1, BLK), jnp.float32)
    zeros3 = jnp.zeros((3, BLK), jnp.float32)
    columns = ([], [], [])
    for which in (0, 1, 0, 1, 2, 0):
        part = pieces[which]
        one = zero + 1.0 if which == 0 else zero
        columns[0].append(jnp.concatenate([part[3:6], zeros3, zero, zero], 0))
        columns[1].append(jnp.concatenate([zeros3, part[0:3], zero, one], 0))
        columns[2].append(jnp.concatenate([-2.0 * part[0:3], zeros3, one, zero], 0))
    tail = jnp.zeros((5, BLK), jnp.float32)
    blank = jnp.zeros((8, BLK), jnp.float32)
    for column, row in ((0, 7), (1, None), (2, 6)):
        if row is None:
            columns[column].append(blank)
        else:
            columns[column].append(
                jnp.concatenate([part[row : row + 1] for part in pieces] + [tail], 0)
            )
        columns[column].append(blank)
    return [jnp.concatenate(column, 0).astype(jnp.bfloat16) for column in columns]


def tile(rows, own):
    forms = jnp.dot(other_features(rows), own, preferred_element_type=jnp.float32)
    facing = jnp.maximum(forms[:, :BLK], 0.0) * jnp.maximum(forms[:, BLK : 2 * BLK], 0.0)
    distance_sq = forms[:, 2 * BLK :]
    bottom = math.pi * distance_sq * distance_sq
    inverse = pl.reciprocal(bottom, approx=True)
    inverse = inverse * (2.0 - bottom * inverse)
    return (facing * inverse).astype(jnp.bfloat16)


def fused_kernel(
    near_code,
    owned,
    emission,
    areas,
    material,
    reflect,
    positions,
    normals,
    out,
    fits,
    geometry,
    features,
    albedo,
    classes,
    scaled,
    total,
    running,
    send,
    last_send,
    near_send,
    near_recv,
    far_send,
    far_recv,
    asked_rows,
    table_rows,
    table,
    rest_rows,
    rest,
    tiles0,
    tiles1,
    last_tiles0,
    last_tiles1,
    recv00,
    recv01,
    recv10,
    recv11,
    last_recv00,
    last_recv01,
    last_recv10,
    last_recv11,
    lend_send,
    lend_recv0,
    lend_recv1,
    relay_send,
    relay_recv0,
    relay_recv1,
    rest_tiles,
    rest_values,
    send_sem,
    recv_sem,
    table_sem,
):
    tiles = (tiles0, tiles1)
    last_tiles = (last_tiles0, last_tiles1)
    recv = ((recv00, recv01), (recv10, recv11))
    last_recv = ((last_recv00, last_recv01), (last_recv10, last_recv11))
    lend_recv = (lend_recv0, lend_recv1)
    relay_recv = (relay_recv0, relay_recv1)
    grp, dev = lax.axis_index("grp"), lax.axis_index("dev")
    core = lax.rem(grp, 2)
    chip = (grp // 2) * 16 + dev
    peers = [peer(grp, dev, step) for step in ORDER]
    barrier = pltpu.get_barrier_semaphore()
    for other in peers:
        pl.semaphore_signal(barrier, inc=1, device_id=other, device_id_type=MESH)

    def describe(kind, source, target, halves=True):
        return [
            pltpu.make_async_remote_copy(
                src_ref=source(place),
                dst_ref=target(place),
                send_sem=send_sem.at[kind],
                recv_sem=recv_sem.at[kind * 2 + (place // PLACES if halves else 0)],
                device_id=other,
                device_id_type=MESH,
            )
            for place, other in enumerate(peers)
        ]

    def all_of(kind, ref, half=0):
        return pltpu.make_async_remote_copy(
            src_ref=ref,
            dst_ref=ref,
            send_sem=send_sem.at[kind],
            recv_sem=recv_sem.at[kind * 2 + half],
            device_id=peers[0],
            device_id_type=MESH,
        )

    def start(copies, first=0, count=PEERS):
        for turn in range(2):

            @pl.when(core == turn)
            def _():
                for place in TURNS[turn][first : first + count]:
                    copies[place].start()

    def exchange(kind, source, target, halves=True):
        start(describe(kind, source, target, halves))

    def came(kind, ref, half, each):
        count = (PLACES if half == 0 else PLACES - 1) * each
        all_of(kind, ref.at[pl.ds(0, count)], half).wait_recv()

    def left(kind, ref, count):
        all_of(kind, ref.at[pl.ds(0, count)]).wait_send()

    def firsts(sweep, first, count):
        def source(place):
            return send.at[pl.ds(place * 2 + first, count)]

        def target(place):
            half = recv[sweep][place // PLACES]
            return half.at[pl.ds(place % PLACES * 2 + first, count)]

        return source, target

    def lasts(sweep):
        def target(place):
            return last_recv[sweep][place // PLACES].at[place % PLACES]

        return lambda place: last_send.at[place], target

    def near_index(place, slot):
        return near_code[place * 2 + slot] & (BLOCKS - 1)

    def sent(row, place):
        return table[MISC + row, BACK[place]] & (BLOCKS - 1)

    def pack_near_values():
        def pack(place, _):
            send[place * 2] = scaled[near_index(place, 0)]
            return 0

        lax.fori_loop(0, DEVICES, pack, 0)

    def pack_far_values():
        for place in range(DEVICES):
            send[place * 2 + 1] = scaled[sent(0, place)]

    def pack_last_values(sweep):
        for place in range(DEVICES):
            last_send[place] = scaled[sent(2, place)]
        last_recv[sweep][1][PLACES - 1] = last_send[PEERS]

    def keep_own(sweep):
        for slot in range(2):
            recv[sweep][1][PLACES * 2 - 2 + slot] = send[PEERS * 2 + slot]

    sides = [[place for place in range(PEERS) if ORDER[place][1] == side] for side in range(2)]

    def on_core(side, act):
        @pl.when(core == side)
        def _():
            act()

    def lend(sweep):
        for apart in range(RANKS):
            block = scaled[rest[5, apart] & (BLOCKS - 1)]
            for piece in range(PIECES):
                lend_send[apart * PIECES + piece] = block[piece * ROWS : (piece + 1) * ROWS]
        lend_recv[sweep][PEERS] = lend_send[chip]
        copies = describe(
            7 + sweep,
            lambda place: lend_send.at[(peers[place][0] // 2) * 16 + peers[place][1]],
            lambda place: lend_recv[sweep].at[place],
            False,
        )
        for side in range(2):
            on_core(side, lambda: [copies[place].start() for place in sides[side]] and None)

    def pass_on(sweep):
        copies = describe(
            9 + sweep,
            lambda place: relay_send.at[place],
            lambda place: relay_recv[sweep].at[chip],
            False,
        )

        @pl.when(core == 0)
        def _():
            all_of(7 + sweep, lend_recv[sweep].at[pl.ds(0, PEERS)]).wait_recv()
            for place in range(DEVICES):
                relay_send[place] = lend_recv[sweep][rest[7, BACK[place]] & (DEVICES - 1)]
            relay_recv[sweep][chip] = relay_send[PEERS]
            for place in range(PEERS):
                copies[place].start()

    def passed_came(sweep):
        for side in range(2):
            pieces = relay_recv[sweep].at[pl.ds(0, len(sides[side]))]
            on_core(side, lambda: all_of(9 + sweep, pieces).wait_recv())

    def rest_left(sweep):
        for side in range(2):
            on_core(side, lambda: left(7 + sweep, lend_send, len(sides[side])))
        on_core(0, lambda: left(9 + sweep, relay_send, PEERS))

    for block in range(BLOCKS):
        lanes = pl.ds(block * BLK, BLK)
        geometry[block] = jnp.concatenate(
            [positions[:, lanes], normals[:, lanes], jnp.zeros((2, BLK), jnp.float32)], 0
        )
    lane = lax.broadcasted_iota(jnp.int32, (4, BLK), 1)

    def pack_near(place, _):
        first, second = near_code[place * 2], near_code[place * 2 + 1]
        codes = jnp.where(lane == 0, first, jnp.where(lane == 1, second, 0)).astype(jnp.float32)
        rows = [geometry[near_index(place, slot)][:6] for slot in range(2)]
        near_send[place] = jnp.concatenate(rows + [codes], 0)
        return 0

    lax.fori_loop(0, DEVICES, pack_near, 0)
    near_recv[PEERS] = near_send[PEERS]
    for block in range(BLOCKS):
        lanes = pl.ds(block * BLK, BLK)
        scaled[block] = (emission[:, lanes] * areas[:, lanes]).astype(jnp.bfloat16)
    pl.semaphore_wait(barrier, PEERS)
    exchange(0, lambda place: near_send.at[place], lambda place: near_recv.at[place], False)
    pack_near_values()
    exchange(2, *firsts(0, 0, 1))

    for which in range(classes.shape[0]):
        classes[which] = jnp.broadcast_to(reflect[:, which : which + 1], (BANDS, BLK))
    for block in range(BLOCKS):
        lanes = pl.ds(block * BLK, BLK)
        row = material[:, lanes]
        part = classes[0]
        for which in range(1, classes.shape[0]):
            part = jnp.where(row == which, classes[which], part)
        albedo[:, lanes] = part

    def build_features(block, _):
        for index, column in enumerate(own_features(geometry[block])):
            features[block, :, index * BLK : (index + 1) * BLK] = column
        return 0

    lax.fori_loop(0, BLOCKS, build_features, 0)

    all_of(0, near_recv.at[pl.ds(0, PEERS)]).wait_recv()

    def collect_asked(place, _):
        asked_rows[pl.ds(place, 1)] = near_recv[place, 12:13]
        return 0

    lax.fori_loop(0, DEVICES, collect_asked, 0)
    asked = asked_rows[...].T[:8].astype(jnp.int32)
    route(asked, owned[...], table_rows)
    to_table = pltpu.make_async_copy(table_rows, table, table_sem.at[0])
    to_table.start()
    to_table.wait()

    crowded_row = table_rows[MISC + 4 : MISC + 5].astype(jnp.float32)
    blank = jnp.zeros((3, BLK), jnp.float32)
    for place in range(DEVICES):
        rows = [geometry[sent(slot, place)][:6] for slot in range(2)]
        far_send[place] = jnp.concatenate(rows + [crowded_row, blank], 0)
    far_recv[PEERS] = far_send[PEERS]
    exchange(1, lambda place: far_send.at[place], lambda place: far_recv.at[place], False)
    pack_far_values()
    keep_own(0)
    exchange(3, *firsts(0, 1, 1))
    pack_last_values(0)
    last_copies = describe(4, *lasts(0))
    start(last_copies, 0, PLACES)

    def own_side(group, task):
        return features[table[group * 8 + 4, task] & (BLOCKS - 1)]

    def build(source, slot, half):
        def step(pair, _):
            for inner in range(2):
                place = pair * 2 + inner
                rows = source[half * PLACES + place][:6]
                tiles[half][place * 2 + slot] = tile(rows, own_side(half, slot * PLACES + place))
            return 0

        lax.fori_loop(0, PLACES // 2, step, 0)

    for half in range(HALVES):
        build(near_recv, 0, half)

    all_of(1, far_recv.at[pl.ds(0, PEERS)]).wait_recv()

    def collect_crowded(place, _):
        asked_rows[pl.ds(place, 1)] = far_recv[place, 12:13]
        return 0

    lax.fori_loop(0, DEVICES, collect_crowded, 0)
    crowded = asked_rows[...].T[:1]
    shift = (chip // PIECES).astype(jnp.float32)
    count = route_rest(crowded, asked, owned[...], shift, rest_rows)
    fits[...] = jnp.broadcast_to(count, (8, BLK))
    to_rest = pltpu.make_async_copy(rest_rows, rest, table_sem.at[1])
    to_rest.start()
    to_rest.wait()
    lend(0)
    start(last_copies, PLACES, PEERS - PLACES)

    for half in range(HALVES):
        build(far_recv, 1, half)
    pass_on(0)

    for half in range(HALVES):

        def build_last(pair, _):
            for inner in range(2):
                place = pair * 2 + inner
                whole = half * PLACES + place
                near = table[MISC + 3, whole] > 0
                rows = jnp.where(near, near_recv[whole], far_recv[whole])[6:12]
                last_tiles[half][place] = tile(rows, own_side(HALVES + half, place))
            return 0

        lax.fori_loop(0, PLACES // 2, build_last, 0)

    def build_rest(apart, _):
        rows = far_recv[rest[6, apart] & (DEVICES - 1)][6:12]
        rest_tiles[apart] = tile(rows, features[rest[4, apart] & (BLOCKS - 1)])
        return 0

    lax.fori_loop(0, RANKS, build_rest, 0)

    def accumulate(values_ref, tiles_ref, rows, base, first):
        tasks = values_ref.shape[0]

        def add(group, run):
            for inner in range(8):
                task = group * 8 + inner
                index = rows[base, task] & (tasks - 1)
                run = run * rows[base + 1, task].astype(jnp.float32) + jnp.dot(
                    values_ref[index], tiles_ref[index], preferred_element_type=jnp.float32
                )
                running[task] = run
            return run

        lax.fori_loop(0, tasks // 8, add, jnp.zeros((BANDS, BLK), jnp.float32))

        def fold(block, _):
            part = running[rows[base + 2, block] & (tasks - 1)]
            part = part * rows[base + 3, block].astype(jnp.float32)
            total[block] = part if first else total[block] + part
            return 0

        lax.fori_loop(0, BLOCKS, fold, 0)

    for sweep in range(SWEEPS):
        if sweep == 0:
            rounds = ((2, 1), (3, 1))
        else:
            rounds = ((5, 2),)
            lend(1)
            pack_near_values()
            pack_far_values()
            exchange(5, *firsts(1, 0, 2))
            keep_own(1)
            pack_last_values(1)
            pass_on(1)
            exchange(6, *lasts(1))

        for half in range(HALVES):
            for kind, each in rounds:
                came(kind, recv[sweep][half], half, each)
            accumulate(recv[sweep][half], tiles[half], table, half * 8, half == 0)
        for kind, each in rounds:
            left(kind, send, PEERS * each)

        passed_came(sweep)
        for apart in range(RANKS):
            for piece in range(PIECES):
                rest_values[apart, piece * ROWS : (piece + 1) * ROWS] = relay_recv[sweep][
                    apart * PIECES + piece
                ]
        accumulate(rest_values, rest_tiles, rest, 0, False)
        rest_left(sweep)
        if sweep == 0:
            left(0, near_send, PEERS)
            left(1, far_send, PEERS)

        for half in range(HALVES):
            came(4 + 2 * sweep, last_recv[sweep][half], half, 1)
            accumulate(
                last_recv[sweep][half], last_tiles[half], table, (HALVES + half) * 8, False
            )
        left(4 + 2 * sweep, last_send, PEERS)

        for block in range(BLOCKS):
            lanes = pl.ds(block * BLK, BLK)
            reflected = albedo[:, lanes] * total[block]
            if sweep + 1 < SWEEPS:
                current = emission[:, lanes] + reflected
                scaled[block] = (current * areas[:, lanes]).astype(jnp.bfloat16)
            else:
                out[:, lanes] = reflected


def fused(near_code, owned, emission, areas, material, reflect, positions, normals):
    smem = pl.BlockSpec(memory_space=pltpu.SMEM)
    vmem = pl.BlockSpec(memory_space=pltpu.VMEM)
    values = pltpu.VMEM((PLACES * 2, BANDS, BLK), jnp.bfloat16)
    last_values = pltpu.VMEM((PLACES, BANDS, BLK), jnp.bfloat16)
    tiles = pltpu.VMEM((PLACES * 2, BLK, BLK), jnp.bfloat16)
    last_tiles = pltpu.VMEM((PLACES, BLK, BLK), jnp.bfloat16)
    message = pltpu.VMEM((DEVICES, 16, BLK), jnp.float32)
    lent = pltpu.VMEM((DEVICES, ROWS, BLK), jnp.bfloat16)
    passed = pltpu.VMEM((RELAYS, ROWS, BLK), jnp.bfloat16)
    return pl.pallas_call(
        fused_kernel,
        in_specs=[smem] + [vmem] * 7,
        out_specs=[vmem, vmem],
        out_shape=[
            jax.ShapeDtypeStruct(emission.shape, jnp.float32),
            jax.ShapeDtypeStruct((8, BLK), jnp.float32),
        ],
        scratch_shapes=[
            pltpu.VMEM((BLOCKS, 8, BLK), jnp.float32),
            pltpu.VMEM((BLOCKS, FEATURES, 3 * BLK), jnp.bfloat16),
            pltpu.VMEM(emission.shape, jnp.float32),
            pltpu.VMEM((reflect.shape[1], BANDS, BLK), jnp.float32),
            pltpu.VMEM((BLOCKS, BANDS, BLK), jnp.bfloat16),
            pltpu.VMEM((BLOCKS, BANDS, BLK), jnp.float32),
            pltpu.VMEM((PLACES * 2, BANDS, BLK), jnp.float32),
            pltpu.VMEM((DEVICES * 2, BANDS, BLK), jnp.bfloat16),
            pltpu.VMEM((DEVICES, BANDS, BLK), jnp.bfloat16),
            message,
            message,
            message,
            message,
            pltpu.VMEM((DEVICES, BLK), jnp.float32),
            pltpu.VMEM((MISC + 8, BLK), jnp.int32),
            pltpu.SMEM((MISC + 8, BLK), jnp.int32),
            pltpu.VMEM((8, BLK), jnp.int32),
            pltpu.SMEM((8, BLK), jnp.int32),
        ]
        + [tiles] * HALVES
        + [last_tiles] * HALVES
        + [values] * (SWEEPS * HALVES)
        + [last_values] * (SWEEPS * HALVES)
        + [passed, lent, lent, lent, passed, passed]
        + [
            pltpu.VMEM((RANKS, BLK, BLK), jnp.bfloat16),
            pltpu.VMEM((RANKS, BANDS, BLK), jnp.bfloat16),
            pltpu.SemaphoreType.DMA((11,)),
            pltpu.SemaphoreType.DMA((22,)),
            pltpu.SemaphoreType.DMA((2,)),
        ],
        compiler_params=pltpu.CompilerParams(
            collective_id=0, has_side_effects=True, vmem_limit_bytes=62 << 20
        ),
        name="fused",
    )(near_code, owned, emission, areas, material, reflect, positions, normals)


def on_device(
    emission, positions, normals, areas, material, reflect, pair_local, pair_device, pair_block
):
    grp, dev = lax.axis_index("grp"), lax.axis_index("dev")
    pairs = pair_local.shape[0]

    steps = np.array(ORDER + [(0, 0, 0, 0)], np.int32).T
    there = peer(grp, dev, steps)
    there = there[0] * 16 + there[1]
    here = peer(grp, dev, (-steps) % np.array([[4], [2], [4], [4]], np.int32))
    here = here[0] * 16 + here[1]
    target = pair_device[:, 0]
    pair_order = jnp.arange(pairs, dtype=jnp.int32)
    earlier = (target[:, None] == target[None, :]) & (pair_order[None, :] < pair_order[:, None])
    second = jnp.any(earlier, 1)
    code = pair_block * BLOCKS + pair_local

    def named(ids, is_second):
        found = (target[None, :] == ids[:, None]) & (second == is_second)[None, :]
        return jnp.max(jnp.where(found, code[None, :], -1), 1)

    near_code = jnp.stack([named(there, False), named(there, True)], 1).reshape(-1)
    owned = jnp.stack([named(here, False), named(here, True), here] + [here * 0] * 5, 0)

    reflected, crowded = fused(
        near_code,
        owned,
        emission,
        areas[None, :],
        material[None, :],
        reflect,
        positions,
        normals,
    )
    return lax.cond(
        crowded[0, 0] <= RANKS,
        lambda: emission + reflected,
        lambda: general(
            emission,
            positions,
            normals,
            areas,
            material,
            reflect,
            pair_local,
            pair_device,
            pair_block,
        ),
    )


def solution(mesh):
    return jax.shard_map(
        on_device,
        mesh=mesh,
        in_specs=(
            P(None, AXES),
            P(None, AXES),
            P(None, AXES),
            P(AXES),
            P(AXES),
            P(),
            P(AXES),
            P(AXES, None),
            P(AXES),
        ),
        out_specs=P(None, AXES),
        check_vma=False,
    )
```

```python
import math

import jax
import jax.numpy as jnp
import numpy as np
from jax import lax
from jax.experimental import pallas as pl
from jax.experimental.pallas import tpu as pltpu
from jax.sharding import PartitionSpec as P

BLK = 128
SWEEPS = 2
AXES = ("grp", "dev")
DEVICES = 128
BLOCKS = 32
BANDS = 64
RANKS = 16
PIECES = 4
RELAYS = RANKS * PIECES
ROWS = 64 // PIECES
HALVES = 2
PLACES = DEVICES // HALVES
FEATURES = 64
MISC = 32
MESH = pl.DeviceIdType.MESH
softening = 0.5


def view_tile(near, far):
    distance_sq = softening
    facing_near = 0.0
    facing_far = 0.0
    for axis_index in range(3):
        offset = far[:, axis_index, None, :] - near[:, axis_index, :, None]
        distance_sq = distance_sq + offset * offset
        facing_near = facing_near + near[:, 3 + axis_index, :, None] * offset
        facing_far = facing_far - far[:, 3 + axis_index, None, :] * offset
    return (
        jnp.maximum(facing_near, 0.0)
        * jnp.maximum(facing_far, 0.0)
        / (math.pi * distance_sq * distance_sq)
    )


def general(
    emission, positions, normals, areas, material, reflect, pair_local, pair_device, pair_block
):
    band_count, patch_count = emission.shape
    local_blocks = patch_count // BLK
    device_count = lax.axis_size(("grp", "dev"))
    pair_count = pair_local.shape[0]
    capacity = max(2, (2 * pair_count + device_count - 1) // device_count)
    slot_total = device_count * capacity
    target = pair_device[:, 0]
    target_hot = (target[:, None] == jnp.arange(device_count, dtype=jnp.int32)[None, :]).astype(
        jnp.int32
    )
    earlier = jnp.cumsum(target_hot, 0) - target_hot
    slot_index = target * capacity + jnp.sum(earlier * target_hot, 1)
    wanted = jnp.zeros((slot_total,), jnp.int32).at[slot_index].set(pair_block)
    asked_for = lax.all_to_all(wanted, ("grp", "dev"), split_axis=0, concat_axis=0, tiled=True)
    geometry = jnp.concatenate([positions, normals, areas[None, :]], 0)
    geometry = geometry.reshape(7, local_blocks, BLK).transpose(1, 0, 2)
    lent_geometry = geometry[asked_for]
    served = lax.all_to_all(lent_geometry, ("grp", "dev"), split_axis=0, concat_axis=0, tiled=True)
    far_geometry = served[slot_index]
    near_geometry = geometry[pair_local]
    block_ids = jnp.arange(local_blocks, dtype=jnp.int32)
    local_hot = (pair_local[:, None] == block_ids[None, :]).astype(jnp.float32)
    asked_hot = (asked_for[:, None] == block_ids[None, :]).astype(jnp.float32)
    class_hot = (
        jnp.arange(reflect.shape[1], dtype=jnp.int32)[:, None] == material[None, :]
    ).astype(jnp.float32)
    albedo = jnp.dot(reflect, class_hot, precision=lax.Precision.HIGHEST)
    albedo = albedo.reshape(band_count, local_blocks, BLK).transpose(1, 0, 2)
    source = emission.reshape(band_count, local_blocks, BLK).transpose(1, 0, 2)
    area_blocks = geometry[:, 6, :]
    current = source
    for sweep_index in range(SWEEPS):
        scaled = (current * area_blocks[:, None, :]).astype(jnp.bfloat16)
        lent_values = scaled[asked_for]
        kernel = view_tile(near_geometry, far_geometry).astype(jnp.bfloat16)
        incoming = lax.all_to_all(
            lent_values, ("grp", "dev"), split_axis=0, concat_axis=0, tiled=True
        )
        to_near = jnp.einsum(
            "pnj,pij->pni", incoming[slot_index], kernel, preferred_element_type=jnp.float32
        )
        to_far = jnp.einsum(
            "pni,pij->pnj", scaled[pair_local], kernel, preferred_element_type=jnp.float32
        )
        replies = jnp.zeros((slot_total, band_count, BLK), jnp.float32).at[slot_index].set(to_far)
        returned = lax.all_to_all(replies, ("grp", "dev"), split_axis=0, concat_axis=0, tiled=True)
        gathered = jnp.einsum("pb,pnk->bnk", local_hot, to_near, precision=lax.Precision.HIGHEST)
        gathered = gathered + jnp.einsum(
            "sb,snk->bnk", asked_hot, returned, precision=lax.Precision.HIGHEST
        )
        current = source + albedo * gathered
    return current.transpose(1, 0, 2).reshape(band_count, patch_count)


def torus_order():
    seen = set()
    groups = []
    for dx in range(4):
        for dy in range(4):
            for dz in range(4):
                for core in range(2):
                    group = []
                    for x, y, z in ((dx, dy, dz), (dy, dz, dx), (dz, dx, dy)):
                        for step in ((x, core, y, z), (-x % 4, core, -y % 4, -z % 4)):
                            if step not in seen and any(step):
                                seen.add(step)
                                group.append(step)
                    if group:
                        groups.append(group)
    groups.sort(key=lambda group: sum(min(v, 4 - v) for v in group[0][:1] + group[0][2:]))
    return [step for group in groups for step in group]


ORDER = torus_order()
PEERS = len(ORDER)


def peer(grp, dev, step):
    x, core, y, z = step
    return (
        lax.rem(grp // 2 + x, 4) * 2 + lax.rem(lax.rem(grp, 2) + core, 2),
        lax.rem(dev // 4 + y, 4) * 4 + lax.rem(lax.rem(dev, 4) + z, 4),
    )


def opposite(step):
    x, core, y, z = step
    return (-x % 4, core, -y % 4, -z % 4)


BACK = [ORDER.index(opposite(step)) for step in ORDER] + [PEERS]


TURNS = [list(range(PEERS)), [ORDER.index((y, core, z, x)) for x, core, y, z in ORDER]]


def across(row):
    return jnp.broadcast_to(row, (BLK, BLK))


def down(row):
    return jnp.broadcast_to(row, (BLK, BLK)).T


def column_sum(terms):
    return jnp.sum(terms, 0, keepdims=True)


def sort_rows(mine, names, lane):
    lane_row = lane[:1]
    key = mine * BLK + lane_row
    rank = column_sum(jnp.where(down(key) < across(key), 1.0, 0.0))
    at_rank = down(rank) == lane
    order = column_sum(jnp.where(at_rank, names, 0.0))
    mine_down = down(mine)
    sorted_mine = column_sum(jnp.where(at_rank, mine_down, 0.0))
    before = pltpu.roll(jnp.broadcast_to(sorted_mine, (8, BLK)), 1, 1)[:1]
    keep = jnp.where((sorted_mine == before) & (lane_row > 0), 1.0, 0.0)
    upto = column_sum(jnp.where(mine_down <= lane, 1.0, 0.0))
    has = column_sum(jnp.where(mine_down == lane, 1.0, 0.0))
    return [order, keep, jnp.maximum(upto - 1.0, 0.0), jnp.minimum(has, 1.0)]


def iotas():
    row = lax.broadcasted_iota(jnp.int32, (BLK, BLK), 0)
    lane = lax.broadcasted_iota(jnp.int32, (BLK, BLK), 1)
    return row, lane


def name_rows(grp, dev, steps, target, code):
    row, lane = iotas()

    def ids(first):
        x, core, y, z = (steps[first + part : first + part + 1] for part in range(4))
        x, core = (x + grp // 2) & 3, (core + lax.rem(grp, 2)) & 1
        y, z = (y + dev // 4) & 3, (z + lax.rem(dev, 4)) & 3
        return ((x * 2 + core) * 16 + y * 4 + z).astype(jnp.float32)

    there, here = ids(0), ids(4)
    target, code = target.astype(jnp.float32), code.astype(jnp.float32)
    target_down, code_down = down(target), down(code)
    earlier = (target_down == across(target)) & (row < lane)
    second = jnp.max(jnp.where(earlier, 1.0, 0.0), 0, keepdims=True)
    second_down = down(second)

    def named(ids, which):
        found = (target_down == across(ids)) & (second_down == which)
        return jnp.max(jnp.where(found, code_down, -1.0), 0, keepdims=True)

    rows = [named(there, 0.0), named(there, 1.0), named(here, 0.0), named(here, 1.0), here]
    return jnp.concatenate(rows + [jnp.zeros((3, BLK), jnp.float32)], 0).astype(jnp.int32)


def route(asked, owned, out):
    row, lane = iotas()
    lane_row = lane[:1]
    lane = lane.astype(jnp.float32)
    asked0, asked1, owned0, owned1 = asked[0:1], asked[1:2], owned[0:1], owned[1:2]
    owned_mine = owned1 & (BLOCKS - 1)
    first_near = jnp.where(asked0 >= 0, asked0 >> 5, BLOCKS)
    first_far = jnp.where(owned0 >= 0, owned0 & (BLOCKS - 1), BLOCKS)
    second = jnp.where(asked1 >= 0, asked1 >> 5, jnp.where(owned1 >= 0, owned_mine, BLOCKS))

    def shifted(values, lanes):
        return pltpu.roll(jnp.broadcast_to(values, (8, BLK)), lanes % BLK, 1)[:1]

    low = lane_row < PLACES
    paired = ((row % PLACES) * 2 + row // PLACES).astype(jnp.float32)
    single = row.astype(jnp.float32)
    for half in range(HALVES):
        shift = -half * PLACES
        both = jnp.where(low, shifted(first_near, shift), shifted(first_far, shift + PLACES))
        last = jnp.where(low, shifted(second, shift), BLOCKS)
        for table, mine, names in ((half, both, paired), (HALVES + half, last, single)):
            mine = mine.astype(jnp.float32)
            rows = sort_rows(mine, names, lane)
            rows += [jnp.minimum(mine, BLOCKS - 1.0), jnp.zeros((3, BLK), jnp.float32)]
            out[table * 8 : table * 8 + 8] = jnp.concatenate(rows, 0).astype(jnp.int32)
    asked_first = jnp.where(asked0 >= 0, asked0 >> 5, 0)
    asked_second = jnp.where(asked1 >= 0, asked1 >> 5, 0)
    both = (owned1 >= 0) & (asked1 >= 0)
    crowded = jnp.max(jnp.where(both, 1.0, 0.0), 1, keepdims=True)
    out[MISC : MISC + 8] = jnp.concatenate(
        [
            asked_first,
            asked_second,
            jnp.where(owned1 >= 0, owned_mine, asked_second),
            (asked1 >= 0).astype(jnp.int32),
            jnp.broadcast_to(crowded, (1, BLK)).astype(jnp.int32),
            jnp.zeros((3, BLK), jnp.int32),
        ],
        0,
    )


def route_rest(crowded, asked, owned, relay_shift, out):
    row, lane = iotas()
    lane = lane.astype(jnp.float32)
    lane_row = lane[:1]
    asked1, owned1 = asked[1:2], owned[1:2]
    ids = owned[2:3].astype(jnp.float32)
    rank = column_sum(jnp.where(down(ids) < across(ids), down(crowded), 0.0))
    rank_down = down(rank)
    hot_down = down(crowded) > 0.5
    my_rank = jnp.sum(jnp.where(lane_row == PEERS, rank, 0.0), 1, keepdims=True)
    count = jnp.sum(crowded, 1, keepdims=True)

    def pick(wanted, terms):
        wanted = jnp.where(wanted >= RANKS, wanted - RANKS, wanted)
        wanted = jnp.where(wanted < 0, wanted + RANKS, wanted)
        return column_sum(jnp.where(hot_down & (rank_down == across(wanted)), terms, 0.0))

    ahead = my_rank + lane_row
    behind = my_rank - lane_row
    asked_second = jnp.where(asked1 >= 0, asked1 >> 5, 0).astype(jnp.float32)
    both = (owned1 >= 0) & (asked1 >= 0)
    mine = jnp.where(both, owned1 & (BLOCKS - 1), BLOCKS).astype(jnp.float32)
    places = row.astype(jnp.float32)
    lend = pick(ahead, down(asked_second))
    source = pick(behind, places)
    found = pick(behind, jnp.ones((BLK, BLK), jnp.float32))
    mine = jnp.where((lane_row < RANKS) & (found > 0.5), pick(behind, down(mine)), float(BLOCKS))
    relay = pick(rank - relay_shift, places)
    rows = sort_rows(mine, places, lane)
    lend = jnp.where(lane_row == BLK - 1, count, lend)
    rows += [jnp.minimum(mine, BLOCKS - 1.0), lend, source, relay]
    out[...] = jnp.concatenate(rows, 0).astype(jnp.int32)


def with_norms(rows, extra):
    points, normals = rows[0:3], rows[3:6]
    square = points * points
    product = points * normals
    return jnp.concatenate(
        [
            rows[0:6],
            square[0:1] + square[1:2] + square[2:3] + extra,
            -(product[0:1] + product[1:2] + product[2:3]),
        ],
        0,
    )


def split(values):
    high = values.astype(jnp.bfloat16).astype(jnp.float32)
    rest = values - high
    middle = rest.astype(jnp.bfloat16).astype(jnp.float32)
    return high, middle, rest - middle


def other_features(rows):
    high, middle, low = split(with_norms(rows, softening))
    ones = jnp.where(lax.broadcasted_iota(jnp.int32, (8, BLK), 0) < 3, 1.0, 0.0)
    parts = [high, high, middle, middle, high, low, ones, jnp.zeros((8, BLK), jnp.float32)]
    return jnp.concatenate(parts, 0).T.astype(jnp.bfloat16)


def own_features(rows):
    pieces = split(with_norms(rows, 0.0))
    zero = jnp.zeros((1, BLK), jnp.float32)
    zeros3 = jnp.zeros((3, BLK), jnp.float32)
    columns = ([], [], [])
    for which in (0, 1, 0, 1, 2, 0):
        part = pieces[which]
        one = zero + 1.0 if which == 0 else zero
        columns[0].append(jnp.concatenate([part[3:6], zeros3, zero, zero], 0))
        columns[1].append(jnp.concatenate([zeros3, part[0:3], zero, one], 0))
        columns[2].append(jnp.concatenate([-2.0 * part[0:3], zeros3, one, zero], 0))
    tail = jnp.zeros((5, BLK), jnp.float32)
    blank = jnp.zeros((8, BLK), jnp.float32)
    for column, row in ((0, 7), (1, None), (2, 6)):
        if row is None:
            columns[column].append(blank)
        else:
            columns[column].append(
                jnp.concatenate([part[row : row + 1] for part in pieces] + [tail], 0)
            )
        columns[column].append(blank)
    return [jnp.concatenate(column, 0).astype(jnp.bfloat16) for column in columns]


def tile(rows, own):
    forms = jnp.dot(other_features(rows), own, preferred_element_type=jnp.float32)
    facing = jnp.maximum(forms[:, :BLK], 0.0) * jnp.maximum(forms[:, BLK : 2 * BLK], 0.0)
    distance_sq = forms[:, 2 * BLK :]
    bottom = math.pi * distance_sq * distance_sq
    inverse = pl.reciprocal(bottom, approx=True)
    inverse = inverse * (2.0 - bottom * inverse)
    return (facing * inverse).astype(jnp.bfloat16)


def fused_kernel(
    steps,
    target,
    pair_block,
    pair_local,
    emission,
    areas,
    material,
    reflect,
    positions,
    normals,
    out,
    fits,
    name_table,
    names,
    geometry,
    features,
    albedo,
    classes,
    scaled,
    total,
    running,
    send,
    last_send,
    near_send,
    near_recv,
    far_send,
    far_recv,
    asked_rows,
    table_rows,
    table,
    rest_rows,
    rest,
    tiles0,
    tiles1,
    last_tiles0,
    last_tiles1,
    recv00,
    recv01,
    recv10,
    recv11,
    last_recv00,
    last_recv01,
    last_recv10,
    last_recv11,
    lend_send,
    lend_recv0,
    lend_recv1,
    relay_send,
    relay_recv0,
    relay_recv1,
    rest_tiles,
    rest_values,
    send_sem,
    recv_sem,
    table_sem,
):
    tiles = (tiles0, tiles1)
    last_tiles = (last_tiles0, last_tiles1)
    recv = ((recv00, recv01), (recv10, recv11))
    last_recv = ((last_recv00, last_recv01), (last_recv10, last_recv11))
    lend_recv = (lend_recv0, lend_recv1)
    relay_recv = (relay_recv0, relay_recv1)
    grp, dev = lax.axis_index("grp"), lax.axis_index("dev")
    core = lax.rem(grp, 2)
    chip = (grp // 2) * 16 + dev
    peers = [peer(grp, dev, step) for step in ORDER]
    barrier = pltpu.get_barrier_semaphore()
    for other in peers:
        pl.semaphore_signal(barrier, inc=1, device_id=other, device_id_type=MESH)

    def describe(kind, source, target, halves=True):
        return [
            pltpu.make_async_remote_copy(
                src_ref=source(place),
                dst_ref=target(place),
                send_sem=send_sem.at[kind],
                recv_sem=recv_sem.at[kind * 2 + (place // PLACES if halves else 0)],
                device_id=other,
                device_id_type=MESH,
            )
            for place, other in enumerate(peers)
        ]

    def all_of(kind, ref, half=0):
        return pltpu.make_async_remote_copy(
            src_ref=ref,
            dst_ref=ref,
            send_sem=send_sem.at[kind],
            recv_sem=recv_sem.at[kind * 2 + half],
            device_id=peers[0],
            device_id_type=MESH,
        )

    def start(copies, first=0, count=PEERS):
        for turn in range(2):

            @pl.when(core == turn)
            def _():
                for place in TURNS[turn][first : first + count]:
                    copies[place].start()

    def exchange(kind, source, target, halves=True):
        start(describe(kind, source, target, halves))

    def came(kind, ref, half, each):
        count = (PLACES if half == 0 else PLACES - 1) * each
        all_of(kind, ref.at[pl.ds(0, count)], half).wait_recv()

    def left(kind, ref, count):
        all_of(kind, ref.at[pl.ds(0, count)]).wait_send()

    def firsts(sweep, first, count):
        def source(place):
            return send.at[pl.ds(place * 2 + first, count)]

        def target(place):
            half = recv[sweep][place // PLACES]
            return half.at[pl.ds(place % PLACES * 2 + first, count)]

        return source, target

    def lasts(sweep):
        def target(place):
            return last_recv[sweep][place // PLACES].at[place % PLACES]

        return lambda place: last_send.at[place], target

    def near_index(place, slot):
        return names[slot, place] & (BLOCKS - 1)

    def sent(row, place):
        return table[MISC + row, BACK[place]] & (BLOCKS - 1)

    def pack_near_values():
        def pack(place, _):
            send[place * 2] = scaled[near_index(place, 0)]
            return 0

        lax.fori_loop(0, DEVICES, pack, 0)

    def pack_far_values():
        for place in range(DEVICES):
            send[place * 2 + 1] = scaled[sent(0, place)]

    def pack_last_values(sweep):
        for place in range(DEVICES):
            last_send[place] = scaled[sent(2, place)]
        last_recv[sweep][1][PLACES - 1] = last_send[PEERS]

    def keep_own(sweep):
        for slot in range(2):
            recv[sweep][1][PLACES * 2 - 2 + slot] = send[PEERS * 2 + slot]

    sides = [[place for place in range(PEERS) if ORDER[place][1] == side] for side in range(2)]

    def on_core(side, act):
        @pl.when(core == side)
        def _():
            act()

    def lend(sweep):
        for apart in range(RANKS):
            block = scaled[rest[5, apart] & (BLOCKS - 1)]
            for piece in range(PIECES):
                lend_send[apart * PIECES + piece] = block[piece * ROWS : (piece + 1) * ROWS]
        lend_recv[sweep][PEERS] = lend_send[chip]
        copies = describe(
            7 + sweep,
            lambda place: lend_send.at[(peers[place][0] // 2) * 16 + peers[place][1]],
            lambda place: lend_recv[sweep].at[place],
            False,
        )
        for side in range(2):
            on_core(side, lambda: [copies[place].start() for place in sides[side]] and None)

    def pass_on(sweep):
        copies = describe(
            9 + sweep,
            lambda place: relay_send.at[place],
            lambda place: relay_recv[sweep].at[chip],
            False,
        )

        @pl.when(core == 0)
        def _():
            all_of(7 + sweep, lend_recv[sweep].at[pl.ds(0, PEERS)]).wait_recv()
            for place in range(DEVICES):
                relay_send[place] = lend_recv[sweep][rest[7, BACK[place]] & (DEVICES - 1)]
            relay_recv[sweep][chip] = relay_send[PEERS]
            for place in range(PEERS):
                copies[place].start()

    def passed_came(sweep):
        for side in range(2):
            pieces = relay_recv[sweep].at[pl.ds(0, len(sides[side]))]
            on_core(side, lambda: all_of(9 + sweep, pieces).wait_recv())

    def rest_left(sweep):
        for side in range(2):
            on_core(side, lambda: left(7 + sweep, lend_send, len(sides[side])))
        on_core(0, lambda: left(9 + sweep, relay_send, PEERS))

    code = pair_block[...] * BLOCKS + pair_local[...]
    name_table[...] = name_rows(grp, dev, steps[...], target[...], code)
    to_names = pltpu.make_async_copy(name_table, names, table_sem.at[2])
    to_names.start()

    for block in range(BLOCKS):
        lanes = pl.ds(block * BLK, BLK)
        geometry[block] = jnp.concatenate(
            [positions[:, lanes], normals[:, lanes], jnp.zeros((2, BLK), jnp.float32)], 0
        )
    to_names.wait()
    lane = lax.broadcasted_iota(jnp.int32, (4, BLK), 1)

    def pack_near(place, _):
        first, second = names[0, place], names[1, place]
        codes = jnp.where(lane == 0, first, jnp.where(lane == 1, second, 0)).astype(jnp.float32)
        rows = [geometry[near_index(place, slot)][:6] for slot in range(2)]
        near_send[place] = jnp.concatenate(rows + [codes], 0)
        return 0

    lax.fori_loop(0, DEVICES, pack_near, 0)
    near_recv[PEERS] = near_send[PEERS]
    for block in range(BLOCKS):
        lanes = pl.ds(block * BLK, BLK)
        scaled[block] = (emission[:, lanes] * areas[:, lanes]).astype(jnp.bfloat16)
    pl.semaphore_wait(barrier, PEERS)
    exchange(0, lambda place: near_send.at[place], lambda place: near_recv.at[place], False)
    pack_near_values()
    exchange(2, *firsts(0, 0, 1))

    by_band = jnp.concatenate([reflect[...], jnp.zeros_like(reflect[...])], 1).T[:BANDS]
    for which in range(classes.shape[0]):
        classes[which] = jnp.broadcast_to(by_band[:, which : which + 1], (BANDS, BLK))
    for block in range(BLOCKS):
        lanes = pl.ds(block * BLK, BLK)
        row = material[:, lanes]
        part = classes[0]
        for which in range(1, classes.shape[0]):
            part = jnp.where(row == which, classes[which], part)
        albedo[:, lanes] = part

    def build_features(block, _):
        for index, column in enumerate(own_features(geometry[block])):
            features[block, :, index * BLK : (index + 1) * BLK] = column
        return 0

    lax.fori_loop(0, BLOCKS, build_features, 0)

    all_of(0, near_recv.at[pl.ds(0, PEERS)]).wait_recv()

    def collect_asked(place, _):
        asked_rows[pl.ds(place, 1)] = near_recv[place, 12:13]
        return 0

    lax.fori_loop(0, DEVICES, collect_asked, 0)
    asked = asked_rows[...].T[:8].astype(jnp.int32)
    route(asked, name_table[2:5], table_rows)
    to_table = pltpu.make_async_copy(table_rows, table, table_sem.at[0])
    to_table.start()
    to_table.wait()

    crowded_row = table_rows[MISC + 4 : MISC + 5].astype(jnp.float32)
    blank = jnp.zeros((3, BLK), jnp.float32)
    for place in range(DEVICES):
        rows = [geometry[sent(slot, place)][:6] for slot in range(2)]
        far_send[place] = jnp.concatenate(rows + [crowded_row, blank], 0)
    far_recv[PEERS] = far_send[PEERS]
    exchange(1, lambda place: far_send.at[place], lambda place: far_recv.at[place], False)
    pack_far_values()
    keep_own(0)
    exchange(3, *firsts(0, 1, 1))
    pack_last_values(0)
    last_copies = describe(4, *lasts(0))
    start(last_copies, 0, PLACES)

    def own_side(group, task):
        return features[table[group * 8 + 4, task] & (BLOCKS - 1)]

    def build(source, slot, half):
        def step(pair, _):
            for inner in range(2):
                place = pair * 2 + inner
                rows = source[half * PLACES + place][:6]
                tiles[half][place * 2 + slot] = tile(rows, own_side(half, slot * PLACES + place))
            return 0

        lax.fori_loop(0, PLACES // 2, step, 0)

    for half in range(HALVES):
        build(near_recv, 0, half)

    all_of(1, far_recv.at[pl.ds(0, PEERS)]).wait_recv()

    def collect_crowded(place, _):
        asked_rows[pl.ds(place, 1)] = far_recv[place, 12:13]
        return 0

    lax.fori_loop(0, DEVICES, collect_crowded, 0)
    crowded = asked_rows[...].T[:1]
    shift = (chip // PIECES).astype(jnp.float32)
    route_rest(crowded, asked, name_table[2:5], shift, rest_rows)
    to_rest = pltpu.make_async_copy(rest_rows, rest, table_sem.at[1])
    to_rest.start()
    to_rest.wait()
    fits[0, 0] = rest[5, BLK - 1]
    lend(0)
    start(last_copies, PLACES, PEERS - PLACES)

    for half in range(HALVES):
        build(far_recv, 1, half)
    pass_on(0)

    for half in range(HALVES):

        def build_last(pair, _):
            for inner in range(2):
                place = pair * 2 + inner
                whole = half * PLACES + place
                near = table[MISC + 3, whole] > 0
                rows = jnp.where(near, near_recv[whole], far_recv[whole])[6:12]
                last_tiles[half][place] = tile(rows, own_side(HALVES + half, place))
            return 0

        lax.fori_loop(0, PLACES // 2, build_last, 0)

    def build_rest(apart, _):
        rows = far_recv[rest[6, apart] & (DEVICES - 1)][6:12]
        rest_tiles[apart] = tile(rows, features[rest[4, apart] & (BLOCKS - 1)])
        return 0

    lax.fori_loop(0, RANKS, build_rest, 0)

    def accumulate(values_ref, tiles_ref, rows, base, first):
        tasks = values_ref.shape[0]

        def add(group, run):
            for inner in range(8):
                task = group * 8 + inner
                index = rows[base, task] & (tasks - 1)
                run = run * rows[base + 1, task].astype(jnp.float32) + jnp.dot(
                    values_ref[index], tiles_ref[index], preferred_element_type=jnp.float32
                )
                running[task] = run
            return run

        lax.fori_loop(0, tasks // 8, add, jnp.zeros((BANDS, BLK), jnp.float32))

        def fold(block, _):
            part = running[rows[base + 2, block] & (tasks - 1)]
            part = part * rows[base + 3, block].astype(jnp.float32)
            total[block] = part if first else total[block] + part
            return 0

        lax.fori_loop(0, BLOCKS, fold, 0)

    for sweep in range(SWEEPS):
        if sweep == 0:
            rounds = ((2, 1), (3, 1))
        else:
            rounds = ((5, 2),)
            lend(1)
            pack_near_values()
            pack_far_values()
            exchange(5, *firsts(1, 0, 2))
            keep_own(1)
            pack_last_values(1)
            pass_on(1)
            exchange(6, *lasts(1))

        for half in range(HALVES):
            for kind, each in rounds:
                came(kind, recv[sweep][half], half, each)
            accumulate(recv[sweep][half], tiles[half], table, half * 8, half == 0)
        for kind, each in rounds:
            left(kind, send, PEERS * each)

        passed_came(sweep)
        for apart in range(RANKS):
            for piece in range(PIECES):
                rest_values[apart, piece * ROWS : (piece + 1) * ROWS] = relay_recv[sweep][
                    apart * PIECES + piece
                ]
        accumulate(rest_values, rest_tiles, rest, 0, False)
        rest_left(sweep)
        if sweep == 0:
            left(0, near_send, PEERS)
            left(1, far_send, PEERS)

        for half in range(HALVES):
            came(4 + 2 * sweep, last_recv[sweep][half], half, 1)
            accumulate(
                last_recv[sweep][half], last_tiles[half], table, (HALVES + half) * 8, False
            )
        left(4 + 2 * sweep, last_send, PEERS)

        for block in range(BLOCKS):
            lanes = pl.ds(block * BLK, BLK)
            reflected = albedo[:, lanes] * total[block]
            if sweep + 1 < SWEEPS:
                current = emission[:, lanes] + reflected
                scaled[block] = (current * areas[:, lanes]).astype(jnp.bfloat16)
            else:
                out[:, lanes] = reflected


def fused(steps, target, pair_block, pair_local, emission, areas, material, reflect, positions, normals):
    smem = pl.BlockSpec(memory_space=pltpu.SMEM)
    vmem = pl.BlockSpec(memory_space=pltpu.VMEM)
    values = pltpu.VMEM((PLACES * 2, BANDS, BLK), jnp.bfloat16)
    last_values = pltpu.VMEM((PLACES, BANDS, BLK), jnp.bfloat16)
    tiles = pltpu.VMEM((PLACES * 2, BLK, BLK), jnp.bfloat16)
    last_tiles = pltpu.VMEM((PLACES, BLK, BLK), jnp.bfloat16)
    message = pltpu.VMEM((DEVICES, 16, BLK), jnp.float32)
    lent = pltpu.VMEM((DEVICES, ROWS, BLK), jnp.bfloat16)
    passed = pltpu.VMEM((RELAYS, ROWS, BLK), jnp.bfloat16)
    return pl.pallas_call(
        fused_kernel,
        in_specs=[vmem] * 10,
        out_specs=[vmem, smem],
        out_shape=[
            jax.ShapeDtypeStruct(emission.shape, jnp.float32),
            jax.ShapeDtypeStruct((1, 1), jnp.int32),
        ],
        scratch_shapes=[
            pltpu.VMEM((8, BLK), jnp.int32),
            pltpu.SMEM((8, BLK), jnp.int32),
            pltpu.VMEM((BLOCKS, 8, BLK), jnp.float32),
            pltpu.VMEM((BLOCKS, FEATURES, 3 * BLK), jnp.bfloat16),
            pltpu.VMEM(emission.shape, jnp.float32),
            pltpu.VMEM((reflect.shape[0], BANDS, BLK), jnp.float32),
            pltpu.VMEM((BLOCKS, BANDS, BLK), jnp.bfloat16),
            pltpu.VMEM((BLOCKS, BANDS, BLK), jnp.float32),
            pltpu.VMEM((PLACES * 2, BANDS, BLK), jnp.float32),
            pltpu.VMEM((DEVICES * 2, BANDS, BLK), jnp.bfloat16),
            pltpu.VMEM((DEVICES, BANDS, BLK), jnp.bfloat16),
            message,
            message,
            message,
            message,
            pltpu.VMEM((DEVICES, BLK), jnp.float32),
            pltpu.VMEM((MISC + 8, BLK), jnp.int32),
            pltpu.SMEM((MISC + 8, BLK), jnp.int32),
            pltpu.VMEM((8, BLK), jnp.int32),
            pltpu.SMEM((8, BLK), jnp.int32),
        ]
        + [tiles] * HALVES
        + [last_tiles] * HALVES
        + [values] * (SWEEPS * HALVES)
        + [last_values] * (SWEEPS * HALVES)
        + [passed, lent, lent, lent, passed, passed]
        + [
            pltpu.VMEM((RANKS, BLK, BLK), jnp.bfloat16),
            pltpu.VMEM((RANKS, BANDS, BLK), jnp.bfloat16),
            pltpu.SemaphoreType.DMA((11,)),
            pltpu.SemaphoreType.DMA((22,)),
            pltpu.SemaphoreType.DMA((3,)),
        ],
        compiler_params=pltpu.CompilerParams(
            collective_id=0, has_side_effects=True, vmem_limit_bytes=62 << 20
        ),
        name="fused",
    )(
        steps,
        target,
        pair_block,
        pair_local,
        emission,
        areas,
        material,
        reflect,
        positions,
        normals,
    )


def on_device(
    emission, positions, normals, areas, material, reflect, pair_local, pair_device, pair_block
):
    steps = ORDER + [(0, 0, 0, 0)]
    steps = np.array([step + opposite(step) for step in steps], np.int32).T
    reflected, crowded = fused(
        jnp.asarray(steps),
        pair_device.reshape(1, -1),
        pair_block[None, :],
        pair_local[None, :],
        emission,
        areas[None, :],
        material[None, :],
        reflect.T,
        positions,
        normals,
    )
    return lax.cond(
        crowded[0, 0] <= RANKS,
        lambda: emission + reflected,
        lambda: general(
            emission,
            positions,
            normals,
            areas,
            material,
            reflect,
            pair_local,
            pair_device,
            pair_block,
        ),
    )


def solution(mesh):
    return jax.shard_map(
        on_device,
        mesh=mesh,
        in_specs=(
            P(None, AXES),
            P(None, AXES),
            P(None, AXES),
            P(AXES),
            P(AXES),
            P(),
            P(AXES),
            P(AXES, None),
            P(AXES),
        ),
        out_specs=P(None, AXES),
        check_vma=False,
    )
```

```python
import math

import jax
import jax.numpy as jnp
import numpy as np
from jax import lax
from jax.experimental import pallas as pl
from jax.experimental.pallas import tpu as pltpu
from jax.sharding import PartitionSpec as P

BLK = 128
SWEEPS = 2
AXES = ("grp", "dev")
DEVICES = 128
BLOCKS = 32
BANDS = 64
RANKS = 16
PIECES = 4
RELAYS = RANKS * PIECES
ROWS = 64 // PIECES
HALVES = 2
PLACES = DEVICES // HALVES
FEATURES = 64
MISC = 32
MESH = pl.DeviceIdType.MESH
softening = 0.5


def view_tile(near, far):
    distance_sq = softening
    facing_near = 0.0
    facing_far = 0.0
    for axis_index in range(3):
        offset = far[:, axis_index, None, :] - near[:, axis_index, :, None]
        distance_sq = distance_sq + offset * offset
        facing_near = facing_near + near[:, 3 + axis_index, :, None] * offset
        facing_far = facing_far - far[:, 3 + axis_index, None, :] * offset
    return (
        jnp.maximum(facing_near, 0.0)
        * jnp.maximum(facing_far, 0.0)
        / (math.pi * distance_sq * distance_sq)
    )


def general(
    emission, positions, normals, areas, material, reflect, pair_local, pair_device, pair_block
):
    band_count, patch_count = emission.shape
    local_blocks = patch_count // BLK
    device_count = lax.axis_size(("grp", "dev"))
    pair_count = pair_local.shape[0]
    capacity = max(2, (2 * pair_count + device_count - 1) // device_count)
    slot_total = device_count * capacity
    target = pair_device[:, 0]
    target_hot = (target[:, None] == jnp.arange(device_count, dtype=jnp.int32)[None, :]).astype(
        jnp.int32
    )
    earlier = jnp.cumsum(target_hot, 0) - target_hot
    slot_index = target * capacity + jnp.sum(earlier * target_hot, 1)
    wanted = jnp.zeros((slot_total,), jnp.int32).at[slot_index].set(pair_block)
    asked_for = lax.all_to_all(wanted, ("grp", "dev"), split_axis=0, concat_axis=0, tiled=True)
    geometry = jnp.concatenate([positions, normals, areas[None, :]], 0)
    geometry = geometry.reshape(7, local_blocks, BLK).transpose(1, 0, 2)
    lent_geometry = geometry[asked_for]
    served = lax.all_to_all(lent_geometry, ("grp", "dev"), split_axis=0, concat_axis=0, tiled=True)
    far_geometry = served[slot_index]
    near_geometry = geometry[pair_local]
    block_ids = jnp.arange(local_blocks, dtype=jnp.int32)
    local_hot = (pair_local[:, None] == block_ids[None, :]).astype(jnp.float32)
    asked_hot = (asked_for[:, None] == block_ids[None, :]).astype(jnp.float32)
    class_hot = (
        jnp.arange(reflect.shape[1], dtype=jnp.int32)[:, None] == material[None, :]
    ).astype(jnp.float32)
    albedo = jnp.dot(reflect, class_hot, precision=lax.Precision.HIGHEST)
    albedo = albedo.reshape(band_count, local_blocks, BLK).transpose(1, 0, 2)
    source = emission.reshape(band_count, local_blocks, BLK).transpose(1, 0, 2)
    area_blocks = geometry[:, 6, :]
    current = source
    for sweep_index in range(SWEEPS):
        scaled = (current * area_blocks[:, None, :]).astype(jnp.bfloat16)
        lent_values = scaled[asked_for]
        kernel = view_tile(near_geometry, far_geometry).astype(jnp.bfloat16)
        incoming = lax.all_to_all(
            lent_values, ("grp", "dev"), split_axis=0, concat_axis=0, tiled=True
        )
        to_near = jnp.einsum(
            "pnj,pij->pni", incoming[slot_index], kernel, preferred_element_type=jnp.float32
        )
        to_far = jnp.einsum(
            "pni,pij->pnj", scaled[pair_local], kernel, preferred_element_type=jnp.float32
        )
        replies = jnp.zeros((slot_total, band_count, BLK), jnp.float32).at[slot_index].set(to_far)
        returned = lax.all_to_all(replies, ("grp", "dev"), split_axis=0, concat_axis=0, tiled=True)
        gathered = jnp.einsum("pb,pnk->bnk", local_hot, to_near, precision=lax.Precision.HIGHEST)
        gathered = gathered + jnp.einsum(
            "sb,snk->bnk", asked_hot, returned, precision=lax.Precision.HIGHEST
        )
        current = source + albedo * gathered
    return current.transpose(1, 0, 2).reshape(band_count, patch_count)


def torus_order():
    seen = set()
    groups = []
    for dx in range(4):
        for dy in range(4):
            for dz in range(4):
                for core in range(2):
                    group = []
                    for x, y, z in ((dx, dy, dz), (dy, dz, dx), (dz, dx, dy)):
                        for step in ((x, core, y, z), (-x % 4, core, -y % 4, -z % 4)):
                            if step not in seen and any(step):
                                seen.add(step)
                                group.append(step)
                    if group:
                        groups.append(group)
    groups.sort(key=lambda group: sum(min(v, 4 - v) for v in group[0][:1] + group[0][2:]))
    return [step for group in groups for step in group]


ORDER = torus_order()
PEERS = len(ORDER)


def peer(grp, dev, step):
    x, core, y, z = step
    return (
        lax.rem(grp // 2 + x, 4) * 2 + lax.rem(lax.rem(grp, 2) + core, 2),
        lax.rem(dev // 4 + y, 4) * 4 + lax.rem(lax.rem(dev, 4) + z, 4),
    )


def opposite(step):
    x, core, y, z = step
    return (-x % 4, core, -y % 4, -z % 4)


BACK = [ORDER.index(opposite(step)) for step in ORDER] + [PEERS]


TURNS = [list(range(PEERS)), [ORDER.index((y, core, z, x)) for x, core, y, z in ORDER]]


def across(row):
    return jnp.broadcast_to(row, (BLK, BLK))


def down(row):
    return jnp.broadcast_to(row, (BLK, BLK)).T


def column_sum(terms):
    return jnp.sum(terms, 0, keepdims=True)


def sort_rows(mine, names, lane):
    lane_row = lane[:1]
    key = mine * BLK + lane_row
    rank = column_sum(jnp.where(down(key) < across(key), 1.0, 0.0))
    at_rank = down(rank) == lane
    order = column_sum(jnp.where(at_rank, names, 0.0))
    mine_down = down(mine)
    sorted_mine = column_sum(jnp.where(at_rank, mine_down, 0.0))
    before = pltpu.roll(jnp.broadcast_to(sorted_mine, (8, BLK)), 1, 1)[:1]
    keep = jnp.where((sorted_mine == before) & (lane_row > 0), 1.0, 0.0)
    upto = column_sum(jnp.where(mine_down <= lane, 1.0, 0.0))
    has = column_sum(jnp.where(mine_down == lane, 1.0, 0.0))
    return [order, keep, jnp.maximum(upto - 1.0, 0.0), jnp.minimum(has, 1.0)]


def iotas():
    row = lax.broadcasted_iota(jnp.int32, (BLK, BLK), 0)
    lane = lax.broadcasted_iota(jnp.int32, (BLK, BLK), 1)
    return row, lane


def name_rows(grp, dev, steps, target, code):
    row, lane = iotas()

    def ids(first):
        x, core, y, z = (steps[first + part : first + part + 1] for part in range(4))
        x, core = (x + grp // 2) & 3, (core + lax.rem(grp, 2)) & 1
        y, z = (y + dev // 4) & 3, (z + lax.rem(dev, 4)) & 3
        return ((x * 2 + core) * 16 + y * 4 + z).astype(jnp.float32)

    there, here = ids(0), ids(4)
    target, code = target.astype(jnp.float32), code.astype(jnp.float32)
    target_down, code_down = down(target), down(code)
    earlier = (target_down == across(target)) & (row < lane)
    second = jnp.max(jnp.where(earlier, 1.0, 0.0), 0, keepdims=True)
    second_down = down(second)

    def named(ids, which):
        found = (target_down == across(ids)) & (second_down == which)
        return jnp.max(jnp.where(found, code_down, -1.0), 0, keepdims=True)

    rows = [named(there, 0.0), named(there, 1.0), named(here, 0.0), named(here, 1.0), here]
    return jnp.concatenate(rows + [jnp.zeros((3, BLK), jnp.float32)], 0).astype(jnp.int32)


def route(asked, owned, out):
    row, lane = iotas()
    lane_row = lane[:1]
    lane = lane.astype(jnp.float32)
    asked0, asked1, owned0, owned1 = asked[0:1], asked[1:2], owned[0:1], owned[1:2]
    owned_mine = owned1 & (BLOCKS - 1)
    first_near = jnp.where(asked0 >= 0, asked0 >> 5, BLOCKS)
    first_far = jnp.where(owned0 >= 0, owned0 & (BLOCKS - 1), BLOCKS)
    second = jnp.where(asked1 >= 0, asked1 >> 5, jnp.where(owned1 >= 0, owned_mine, BLOCKS))

    def shifted(values, lanes):
        return pltpu.roll(jnp.broadcast_to(values, (8, BLK)), lanes % BLK, 1)[:1]

    low = lane_row < PLACES
    paired = ((row % PLACES) * 2 + row // PLACES).astype(jnp.float32)
    single = row.astype(jnp.float32)
    for half in range(HALVES):
        shift = -half * PLACES
        both = jnp.where(low, shifted(first_near, shift), shifted(first_far, shift + PLACES))
        last = jnp.where(low, shifted(second, shift), BLOCKS)
        for table, mine, names in ((half, both, paired), (HALVES + half, last, single)):
            mine = mine.astype(jnp.float32)
            rows = sort_rows(mine, names, lane)
            rows += [jnp.minimum(mine, BLOCKS - 1.0), jnp.zeros((3, BLK), jnp.float32)]
            out[table * 8 : table * 8 + 8] = jnp.concatenate(rows, 0).astype(jnp.int32)
    asked_first = jnp.where(asked0 >= 0, asked0 >> 5, 0)
    asked_second = jnp.where(asked1 >= 0, asked1 >> 5, 0)
    both = (owned1 >= 0) & (asked1 >= 0)
    crowded = jnp.max(jnp.where(both, 1.0, 0.0), 1, keepdims=True)
    out[MISC : MISC + 8] = jnp.concatenate(
        [
            asked_first,
            jnp.zeros((1, BLK), jnp.int32),
            jnp.where(owned1 >= 0, owned_mine, asked_second),
            jnp.zeros((1, BLK), jnp.int32),
            jnp.broadcast_to(crowded, (1, BLK)).astype(jnp.int32),
            jnp.zeros((3, BLK), jnp.int32),
        ],
        0,
    )


def route_rest(crowded, asked, owned, relay_shift, out):
    row, lane = iotas()
    lane = lane.astype(jnp.float32)
    lane_row = lane[:1]
    asked1, owned1 = asked[1:2], owned[1:2]
    ids = owned[2:3].astype(jnp.float32)
    rank = column_sum(jnp.where(down(ids) < across(ids), down(crowded), 0.0))
    rank_down = down(rank)
    hot_down = down(crowded) > 0.5
    my_rank = jnp.sum(jnp.where(lane_row == PEERS, rank, 0.0), 1, keepdims=True)
    count = jnp.sum(crowded, 1, keepdims=True)

    def pick(wanted, terms):
        wanted = jnp.where(wanted >= RANKS, wanted - RANKS, wanted)
        wanted = jnp.where(wanted < 0, wanted + RANKS, wanted)
        return column_sum(jnp.where(hot_down & (rank_down == across(wanted)), terms, 0.0))

    ahead = my_rank + lane_row
    behind = my_rank - lane_row
    asked_second = jnp.where(asked1 >= 0, asked1 >> 5, 0).astype(jnp.float32)
    both = (owned1 >= 0) & (asked1 >= 0)
    mine = jnp.where(both, owned1 & (BLOCKS - 1), BLOCKS).astype(jnp.float32)
    places = row.astype(jnp.float32)
    lend = pick(ahead, down(asked_second))
    source = pick(behind, places)
    found = pick(behind, jnp.ones((BLK, BLK), jnp.float32))
    mine = jnp.where((lane_row < RANKS) & (found > 0.5), pick(behind, down(mine)), float(BLOCKS))
    relay = pick(rank - relay_shift, places)
    rows = sort_rows(mine, places, lane)
    lend = jnp.where(lane_row == BLK - 1, count, lend)
    rows += [jnp.minimum(mine, BLOCKS - 1.0), lend, source, relay]
    out[...] = jnp.concatenate(rows, 0).astype(jnp.int32)


def with_norms(rows, extra):
    points, normals = rows[0:3], rows[3:6]
    square = points * points
    product = points * normals
    return jnp.concatenate(
        [
            rows[0:6],
            square[0:1] + square[1:2] + square[2:3] + extra,
            -(product[0:1] + product[1:2] + product[2:3]),
        ],
        0,
    )


def split(values):
    high = values.astype(jnp.bfloat16).astype(jnp.float32)
    rest = values - high
    middle = rest.astype(jnp.bfloat16).astype(jnp.float32)
    return high, middle, rest - middle


def other_features(rows):
    high, middle, low = split(with_norms(rows, softening))
    ones = jnp.where(lax.broadcasted_iota(jnp.int32, (8, BLK), 0) < 3, 1.0, 0.0)
    parts = [high, high, middle, middle, high, low, ones, jnp.zeros((8, BLK), jnp.float32)]
    return jnp.concatenate(parts, 0).T.astype(jnp.bfloat16)


def own_features(rows):
    pieces = split(with_norms(rows, 0.0))
    zero = jnp.zeros((1, BLK), jnp.float32)
    zeros3 = jnp.zeros((3, BLK), jnp.float32)
    columns = ([], [], [])
    for which in (0, 1, 0, 1, 2, 0):
        part = pieces[which]
        one = zero + 1.0 if which == 0 else zero
        columns[0].append(jnp.concatenate([part[3:6], zeros3, zero, zero], 0))
        columns[1].append(jnp.concatenate([zeros3, part[0:3], zero, one], 0))
        columns[2].append(jnp.concatenate([-2.0 * part[0:3], zeros3, one, zero], 0))
    tail = jnp.zeros((5, BLK), jnp.float32)
    blank = jnp.zeros((8, BLK), jnp.float32)
    for column, row in ((0, 7), (1, None), (2, 6)):
        if row is None:
            columns[column].append(blank)
        else:
            columns[column].append(
                jnp.concatenate([part[row : row + 1] for part in pieces] + [tail], 0)
            )
        columns[column].append(blank)
    return [jnp.concatenate(column, 0).astype(jnp.bfloat16) for column in columns]


def tile(rows, own):
    forms = jnp.dot(other_features(rows), own, preferred_element_type=jnp.float32)
    facing = jnp.maximum(forms[:, :BLK], 0.0) * jnp.maximum(forms[:, BLK : 2 * BLK], 0.0)
    distance_sq = forms[:, 2 * BLK :]
    bottom = math.pi * distance_sq * distance_sq
    inverse = pl.reciprocal(bottom, approx=True)
    inverse = inverse * (2.0 - bottom * inverse)
    return (facing * inverse).astype(jnp.bfloat16)


def fused_kernel(
    steps,
    target,
    pair_block,
    pair_local,
    emission,
    areas,
    material,
    reflect,
    positions,
    normals,
    out,
    fits,
    name_table,
    names,
    geometry,
    features,
    albedo,
    classes,
    scaled,
    total,
    running,
    send,
    last_send,
    near_send,
    near_recv,
    far_send,
    far_recv,
    asked_rows,
    table_rows,
    table,
    rest_rows,
    rest,
    tiles0,
    tiles1,
    last_tiles0,
    last_tiles1,
    recv00,
    recv01,
    recv10,
    recv11,
    last_recv00,
    last_recv01,
    last_recv10,
    last_recv11,
    lend_send,
    lend_recv0,
    lend_recv1,
    relay_send,
    relay_recv0,
    relay_recv1,
    shape_send,
    shape_recv,
    shape_relay,
    shape_came,
    rest_tiles,
    rest_values,
    send_sem,
    recv_sem,
    table_sem,
):
    tiles = (tiles0, tiles1)
    last_tiles = (last_tiles0, last_tiles1)
    recv = ((recv00, recv01), (recv10, recv11))
    last_recv = ((last_recv00, last_recv01), (last_recv10, last_recv11))
    lend_recv = (lend_recv0, lend_recv1)
    relay_recv = (relay_recv0, relay_recv1)
    grp, dev = lax.axis_index("grp"), lax.axis_index("dev")
    core = lax.rem(grp, 2)
    chip = (grp // 2) * 16 + dev
    peers = [peer(grp, dev, step) for step in ORDER]
    barrier = pltpu.get_barrier_semaphore()
    for other in peers[::-1]:
        pl.semaphore_signal(barrier, inc=1, device_id=other, device_id_type=MESH)

    def describe(kind, source, target, halves=True):
        return [
            pltpu.make_async_remote_copy(
                src_ref=source(place),
                dst_ref=target(place),
                send_sem=send_sem.at[kind],
                recv_sem=recv_sem.at[kind * 2 + (place // PLACES if halves else 0)],
                device_id=other,
                device_id_type=MESH,
            )
            for place, other in enumerate(peers)
        ]

    def all_of(kind, ref, half=0):
        return pltpu.make_async_remote_copy(
            src_ref=ref,
            dst_ref=ref,
            send_sem=send_sem.at[kind],
            recv_sem=recv_sem.at[kind * 2 + half],
            device_id=peers[0],
            device_id_type=MESH,
        )

    def start(copies, first=0, count=PEERS):
        for turn in range(2):

            @pl.when(core == turn)
            def _():
                for place in TURNS[turn][first : first + count]:
                    copies[place].start()

    def exchange(kind, source, target, halves=True):
        start(describe(kind, source, target, halves))

    def came(kind, ref, half, each):
        count = (PLACES if half == 0 else PLACES - 1) * each
        all_of(kind, ref.at[pl.ds(0, count)], half).wait_recv()

    def left(kind, ref, count):
        all_of(kind, ref.at[pl.ds(0, count)]).wait_send()

    def firsts(sweep, first, count):
        def source(place):
            return send.at[pl.ds(place * 2 + first, count)]

        def target(place):
            half = recv[sweep][place // PLACES]
            return half.at[pl.ds(place % PLACES * 2 + first, count)]

        return source, target

    def lasts(sweep):
        def target(place):
            return last_recv[sweep][place // PLACES].at[place % PLACES]

        return lambda place: last_send.at[place], target

    def at_places(act):
        def step(group, _):
            for inner in range(8):
                act(group * 8 + inner)
            return 0

        lax.fori_loop(0, DEVICES // 8, step, 0)

    def near_index(place, slot):
        return names[slot, place] & (BLOCKS - 1)

    def sent(row, place):
        return table[MISC + row, BACK[place]] & (BLOCKS - 1)

    def pack_near_values():
        def pack(place):
            send[place * 2] = scaled[near_index(place, 0)]

        at_places(pack)

    def pack_far_values():
        for place in range(DEVICES):
            send[place * 2 + 1] = scaled[sent(0, place)]

    def pack_last_values(sweep):
        for place in range(DEVICES):
            last_send[place] = scaled[sent(2, place)]
        last_recv[sweep][1][PLACES - 1] = last_send[PEERS]

    def keep_own(sweep):
        for slot in range(2):
            recv[sweep][1][PLACES * 2 - 2 + slot] = send[PEERS * 2 + slot]

    sides = [[place for place in range(PEERS) if ORDER[place][1] == side] for side in range(2)]

    def on_core(side, act):
        @pl.when(core == side)
        def _():
            act()

    def lend(sweep):
        for apart in range(RANKS):
            block = scaled[rest[5, apart] & (BLOCKS - 1)]
            for piece in range(PIECES):
                lend_send[apart * PIECES + piece] = block[piece * ROWS : (piece + 1) * ROWS]
        lend_recv[sweep][PEERS] = lend_send[chip]
        copies = describe(
            7 + sweep,
            lambda place: lend_send.at[(peers[place][0] // 2) * 16 + peers[place][1]],
            lambda place: lend_recv[sweep].at[place],
            False,
        )
        for side in range(2):
            on_core(side, lambda: [copies[place].start() for place in sides[side]] and None)

    def pass_on(sweep):
        copies = describe(
            9 + sweep,
            lambda place: relay_send.at[place],
            lambda place: relay_recv[sweep].at[chip],
            False,
        )

        @pl.when(core == 0)
        def _():
            all_of(7 + sweep, lend_recv[sweep].at[pl.ds(0, PEERS)]).wait_recv()
            for place in range(DEVICES):
                relay_send[place] = lend_recv[sweep][rest[7, BACK[place]] & (DEVICES - 1)]
            relay_recv[sweep][chip] = relay_send[PEERS]
            for place in range(PEERS):
                copies[place].start()

    z = lax.rem(dev, 4)
    is_relay = (core == 0) & (z == 0)
    not_relay = jnp.logical_not(is_relay)

    def lend_geometry():
        for apart in range(RANKS):
            shape_send[apart] = geometry[rest[5, apart] & (BLOCKS - 1)]
        shape_recv[PEERS] = shape_send[chip // PIECES]
        copies = describe(
            11,
            lambda place: shape_send.at[(peers[place][0] // 2) * 4 + peers[place][1] // 4],
            lambda place: shape_recv.at[place],
            False,
        )
        for side in range(2):
            for level in range(4):

                @pl.when((core == side) & (z == level))
                def _():
                    for place in sides[side]:
                        if (level + ORDER[place][3]) % 4 == 0:
                            copies[place].start()

    def pass_geometry_on():
        copies = describe(
            12,
            lambda place: shape_relay.at[place],
            lambda place: shape_came.at[chip // PIECES],
            False,
        )

        @pl.when(is_relay)
        def _():
            all_of(11, shape_recv.at[pl.ds(0, PEERS)]).wait_recv()
            for place in range(DEVICES):
                shape_relay[place] = shape_recv[rest[7, BACK[place]] & (DEVICES - 1)]
            shape_came[chip // PIECES] = shape_relay[PEERS]
            for place in range(PEERS):
                copies[place].start()

    def geometry_came():
        for condition, count in ((is_relay, RANKS - 1), (not_relay, RANKS)):

            @pl.when(condition)
            def _():
                all_of(12, shape_came.at[pl.ds(0, count)]).wait_recv()
                left(11, shape_send, count)

        @pl.when(is_relay)
        def _():
            left(12, shape_relay, PEERS)

    def passed_came(sweep):
        for side in range(2):
            pieces = relay_recv[sweep].at[pl.ds(0, len(sides[side]))]
            on_core(side, lambda: all_of(9 + sweep, pieces).wait_recv())

    def rest_left(sweep):
        for side in range(2):
            on_core(side, lambda: left(7 + sweep, lend_send, len(sides[side])))
        on_core(0, lambda: left(9 + sweep, relay_send, PEERS))

    code = pair_block[...] * BLOCKS + pair_local[...]
    name_table[...] = name_rows(grp, dev, steps[...], target[...], code)
    to_names = pltpu.make_async_copy(name_table, names, table_sem.at[2])
    to_names.start()

    for block in range(BLOCKS):
        lanes = pl.ds(block * BLK, BLK)
        geometry[block] = jnp.concatenate(
            [positions[:, lanes], normals[:, lanes], jnp.zeros((2, BLK), jnp.float32)], 0
        )
    to_names.wait()
    lane = lax.broadcasted_iota(jnp.int32, (2, BLK), 1)

    def pack_near(place):
        first, second = names[0, place], names[1, place]
        codes = jnp.where(lane == 0, first, jnp.where(lane == 1, second, 0)).astype(jnp.float32)
        near_send[place] = jnp.concatenate([geometry[near_index(place, 0)][:6], codes], 0)

    at_places(pack_near)
    near_recv[PEERS] = near_send[PEERS]
    pl.semaphore_wait(barrier, PEERS)
    exchange(0, lambda place: near_send.at[place], lambda place: near_recv.at[place], False)
    for block in range(BLOCKS):
        lanes = pl.ds(block * BLK, BLK)
        scaled[block] = (emission[:, lanes] * areas[:, lanes]).astype(jnp.bfloat16)
    pack_near_values()
    exchange(2, *firsts(0, 0, 1))

    by_band = jnp.concatenate([reflect[...], jnp.zeros_like(reflect[...])], 1).T[:BANDS]
    for which in range(classes.shape[0]):
        classes[which] = jnp.broadcast_to(by_band[:, which : which + 1], (BANDS, BLK))
    for block in range(BLOCKS):
        lanes = pl.ds(block * BLK, BLK)
        row = material[:, lanes]
        part = classes[0]
        for which in range(1, classes.shape[0]):
            part = jnp.where(row == which, classes[which], part)
        albedo[:, lanes] = part

    def build_features(block, _):
        for index, column in enumerate(own_features(geometry[block])):
            features[block, :, index * BLK : (index + 1) * BLK] = column
        return 0

    lax.fori_loop(0, BLOCKS, build_features, 0)

    all_of(0, near_recv.at[pl.ds(0, PEERS)]).wait_recv()

    def collect_asked(place):
        asked_rows[pl.ds(place, 1)] = near_recv[place, 6:7]

    at_places(collect_asked)
    asked = asked_rows[...].T[:8].astype(jnp.int32)
    route(asked, name_table[2:5], table_rows)
    to_table = pltpu.make_async_copy(table_rows, table, table_sem.at[0])
    to_table.start()
    to_table.wait()

    crowded_row = table_rows[MISC + 4 : MISC + 5].astype(jnp.float32)
    blank = jnp.zeros((3, BLK), jnp.float32)
    for place in range(DEVICES):
        rows = [geometry[sent(row, place)][:6] for row in (0, 2)]
        far_send[place] = jnp.concatenate(rows + [crowded_row, blank], 0)
    far_recv[PEERS] = far_send[PEERS]
    exchange(1, lambda place: far_send.at[place], lambda place: far_recv.at[place], False)
    pack_far_values()
    keep_own(0)
    exchange(3, *firsts(0, 1, 1))
    pack_last_values(0)
    last_copies = describe(4, *lasts(0))
    start(last_copies, 0, PLACES)

    def own_side(group, task):
        return features[table[group * 8 + 4, task] & (BLOCKS - 1)]

    def build(source, slot, half):
        def step(pair, _):
            for inner in range(2):
                place = pair * 2 + inner
                rows = source[half * PLACES + place][:6]
                tiles[half][place * 2 + slot] = tile(rows, own_side(half, slot * PLACES + place))
            return 0

        lax.fori_loop(0, PLACES // 2, step, 0)

    for half in range(HALVES):
        build(near_recv, 0, half)

    all_of(1, far_recv.at[pl.ds(0, PEERS)]).wait_recv()

    def collect_crowded(place):
        asked_rows[pl.ds(place, 1)] = far_recv[place, 12:13]

    at_places(collect_crowded)
    crowded = asked_rows[...].T[:1]
    shift = (chip // PIECES).astype(jnp.float32)
    route_rest(crowded, asked, name_table[2:5], shift, rest_rows)
    to_rest = pltpu.make_async_copy(rest_rows, rest, table_sem.at[1])
    to_rest.start()
    to_rest.wait()
    fits[0, 0] = rest[5, BLK - 1]
    lend_geometry()
    lend(0)
    start(last_copies, PLACES, PEERS - PLACES)

    for half in range(HALVES):
        build(far_recv, 1, half)
    pass_geometry_on()
    pass_on(0)

    for half in range(HALVES):

        def build_last(pair, _):
            for inner in range(2):
                place = pair * 2 + inner
                rows = far_recv[half * PLACES + place][6:12]
                last_tiles[half][place] = tile(rows, own_side(HALVES + half, place))
            return 0

        lax.fori_loop(0, PLACES // 2, build_last, 0)

    def build_rest(apart, _):
        own = features[rest[4, apart] & (BLOCKS - 1)]
        rest_tiles[apart] = tile(shape_came[apart][:6], own)
        return 0

    def accumulate(values_ref, tiles_ref, rows, base, first):
        tasks = values_ref.shape[0]

        def add(group, run):
            for inner in range(8):
                task = group * 8 + inner
                index = rows[base, task] & (tasks - 1)
                run = run * rows[base + 1, task].astype(jnp.float32) + jnp.dot(
                    values_ref[index], tiles_ref[index], preferred_element_type=jnp.float32
                )
                running[task] = run
            return run

        lax.fori_loop(0, tasks // 8, add, jnp.zeros((BANDS, BLK), jnp.float32))

        def fold(block, _):
            part = running[rows[base + 2, block] & (tasks - 1)]
            part = part * rows[base + 3, block].astype(jnp.float32)
            total[block] = part if first else total[block] + part
            return 0

        lax.fori_loop(0, BLOCKS, fold, 0)

    for sweep in range(SWEEPS):
        if sweep == 0:
            rounds = ((2, 1), (3, 1))
        else:
            rounds = ((5, 2),)
            lend(1)
            pack_near_values()
            pack_far_values()
            exchange(5, *firsts(1, 0, 2))
            keep_own(1)
            pack_last_values(1)
            pass_on(1)
            exchange(6, *lasts(1))

        for half in range(HALVES):
            for kind, each in rounds:
                came(kind, recv[sweep][half], half, each)
            accumulate(recv[sweep][half], tiles[half], table, half * 8, half == 0)
        for kind, each in rounds:
            left(kind, send, PEERS * each)

        if sweep == 0:
            geometry_came()
            lax.fori_loop(0, RANKS, build_rest, 0)
        passed_came(sweep)
        for apart in range(RANKS):
            for piece in range(PIECES):
                rest_values[apart, piece * ROWS : (piece + 1) * ROWS] = relay_recv[sweep][
                    apart * PIECES + piece
                ]
        accumulate(rest_values, rest_tiles, rest, 0, False)
        rest_left(sweep)
        if sweep == 0:
            left(0, near_send, PEERS)
            left(1, far_send, PEERS)

        for half in range(HALVES):
            came(4 + 2 * sweep, last_recv[sweep][half], half, 1)
            accumulate(
                last_recv[sweep][half], last_tiles[half], table, (HALVES + half) * 8, False
            )
        left(4 + 2 * sweep, last_send, PEERS)

        for block in range(BLOCKS):
            lanes = pl.ds(block * BLK, BLK)
            reflected = albedo[:, lanes] * total[block]
            if sweep + 1 < SWEEPS:
                current = emission[:, lanes] + reflected
                scaled[block] = (current * areas[:, lanes]).astype(jnp.bfloat16)
            else:
                out[:, lanes] = reflected


def fused(steps, target, pair_block, pair_local, emission, areas, material, reflect, positions, normals):
    smem = pl.BlockSpec(memory_space=pltpu.SMEM)
    vmem = pl.BlockSpec(memory_space=pltpu.VMEM)
    values = pltpu.VMEM((PLACES * 2, BANDS, BLK), jnp.bfloat16)
    last_values = pltpu.VMEM((PLACES, BANDS, BLK), jnp.bfloat16)
    tiles = pltpu.VMEM((PLACES * 2, BLK, BLK), jnp.bfloat16)
    last_tiles = pltpu.VMEM((PLACES, BLK, BLK), jnp.bfloat16)
    message = pltpu.VMEM((DEVICES, 16, BLK), jnp.float32)
    lent = pltpu.VMEM((DEVICES, ROWS, BLK), jnp.bfloat16)
    shapes = pltpu.VMEM((RANKS, 8, BLK), jnp.float32)
    all_shapes = pltpu.VMEM((DEVICES, 8, BLK), jnp.float32)
    passed = pltpu.VMEM((RELAYS, ROWS, BLK), jnp.bfloat16)
    return pl.pallas_call(
        fused_kernel,
        in_specs=[vmem] * 10,
        out_specs=[vmem, smem],
        out_shape=[
            jax.ShapeDtypeStruct(emission.shape, jnp.float32),
            jax.ShapeDtypeStruct((1, 1), jnp.int32),
        ],
        scratch_shapes=[
            pltpu.VMEM((8, BLK), jnp.int32),
            pltpu.SMEM((8, BLK), jnp.int32),
            pltpu.VMEM((BLOCKS, 8, BLK), jnp.float32),
            pltpu.VMEM((BLOCKS, FEATURES, 3 * BLK), jnp.bfloat16),
            pltpu.VMEM(emission.shape, jnp.float32),
            pltpu.VMEM((reflect.shape[0], BANDS, BLK), jnp.float32),
            pltpu.VMEM((BLOCKS, BANDS, BLK), jnp.bfloat16),
            pltpu.VMEM((BLOCKS, BANDS, BLK), jnp.float32),
            pltpu.VMEM((PLACES * 2, BANDS, BLK), jnp.float32),
            pltpu.VMEM((DEVICES * 2, BANDS, BLK), jnp.bfloat16),
            pltpu.VMEM((DEVICES, BANDS, BLK), jnp.bfloat16),
            all_shapes,
            all_shapes,
            message,
            message,
            pltpu.VMEM((DEVICES, BLK), jnp.float32),
            pltpu.VMEM((MISC + 8, BLK), jnp.int32),
            pltpu.SMEM((MISC + 8, BLK), jnp.int32),
            pltpu.VMEM((8, BLK), jnp.int32),
            pltpu.SMEM((8, BLK), jnp.int32),
        ]
        + [tiles] * HALVES
        + [last_tiles] * HALVES
        + [values] * (SWEEPS * HALVES)
        + [last_values] * (SWEEPS * HALVES)
        + [passed, lent, lent, lent, passed, passed]
        + [shapes, all_shapes, all_shapes, shapes]
        + [
            pltpu.VMEM((RANKS, BLK, BLK), jnp.bfloat16),
            pltpu.VMEM((RANKS, BANDS, BLK), jnp.bfloat16),
            pltpu.SemaphoreType.DMA((13,)),
            pltpu.SemaphoreType.DMA((26,)),
            pltpu.SemaphoreType.DMA((3,)),
        ],
        compiler_params=pltpu.CompilerParams(
            collective_id=0, has_side_effects=True, vmem_limit_bytes=62 << 20
        ),
        name="fused",
    )(
        steps,
        target,
        pair_block,
        pair_local,
        emission,
        areas,
        material,
        reflect,
        positions,
        normals,
    )


def on_device(
    emission, positions, normals, areas, material, reflect, pair_local, pair_device, pair_block
):
    steps = ORDER + [(0, 0, 0, 0)]
    steps = np.array([step + opposite(step) for step in steps], np.int32).T
    reflected, crowded = fused(
        jnp.asarray(steps),
        pair_device.reshape(1, -1),
        pair_block[None, :],
        pair_local[None, :],
        emission,
        areas[None, :],
        material[None, :],
        reflect.T,
        positions,
        normals,
    )
    return lax.cond(
        crowded[0, 0] <= RANKS,
        lambda: emission + reflected,
        lambda: general(
            emission,
            positions,
            normals,
            areas,
            material,
            reflect,
            pair_local,
            pair_device,
            pair_block,
        ),
    )


def solution(mesh):
    return jax.shard_map(
        on_device,
        mesh=mesh,
        in_specs=(
            P(None, AXES),
            P(None, AXES),
            P(None, AXES),
            P(AXES),
            P(AXES),
            P(),
            P(AXES),
            P(AXES, None),
            P(AXES),
        ),
        out_specs=P(None, AXES),
        check_vma=False,
    )
```

```python
import math

import jax
import jax.numpy as jnp
import numpy as np
from jax import lax
from jax.experimental import pallas as pl
from jax.experimental.pallas import tpu as pltpu
from jax.sharding import PartitionSpec as P

BLK = 128
SWEEPS = 2
AXES = ("grp", "dev")
DEVICES = 128
BLOCKS = 32
BANDS = 64
RANKS = 16
PIECES = 4
RELAYS = RANKS * PIECES
ROWS = 64 // PIECES
HALVES = 2
PLACES = DEVICES // HALVES
FEATURES = 64
MISC = 32
MESH = pl.DeviceIdType.MESH
softening = 0.5


def view_tile(near, far):
    distance_sq = softening
    facing_near = 0.0
    facing_far = 0.0
    for axis_index in range(3):
        offset = far[:, axis_index, None, :] - near[:, axis_index, :, None]
        distance_sq = distance_sq + offset * offset
        facing_near = facing_near + near[:, 3 + axis_index, :, None] * offset
        facing_far = facing_far - far[:, 3 + axis_index, None, :] * offset
    return (
        jnp.maximum(facing_near, 0.0)
        * jnp.maximum(facing_far, 0.0)
        / (math.pi * distance_sq * distance_sq)
    )


def general(
    emission, positions, normals, areas, material, reflect, pair_local, pair_device, pair_block
):
    band_count, patch_count = emission.shape
    local_blocks = patch_count // BLK
    device_count = lax.axis_size(("grp", "dev"))
    pair_count = pair_local.shape[0]
    capacity = max(2, (2 * pair_count + device_count - 1) // device_count)
    slot_total = device_count * capacity
    target = pair_device[:, 0]
    target_hot = (target[:, None] == jnp.arange(device_count, dtype=jnp.int32)[None, :]).astype(
        jnp.int32
    )
    earlier = jnp.cumsum(target_hot, 0) - target_hot
    slot_index = target * capacity + jnp.sum(earlier * target_hot, 1)
    wanted = jnp.zeros((slot_total,), jnp.int32).at[slot_index].set(pair_block)
    asked_for = lax.all_to_all(wanted, ("grp", "dev"), split_axis=0, concat_axis=0, tiled=True)
    geometry = jnp.concatenate([positions, normals, areas[None, :]], 0)
    geometry = geometry.reshape(7, local_blocks, BLK).transpose(1, 0, 2)
    lent_geometry = geometry[asked_for]
    served = lax.all_to_all(lent_geometry, ("grp", "dev"), split_axis=0, concat_axis=0, tiled=True)
    far_geometry = served[slot_index]
    near_geometry = geometry[pair_local]
    block_ids = jnp.arange(local_blocks, dtype=jnp.int32)
    local_hot = (pair_local[:, None] == block_ids[None, :]).astype(jnp.float32)
    asked_hot = (asked_for[:, None] == block_ids[None, :]).astype(jnp.float32)
    class_hot = (
        jnp.arange(reflect.shape[1], dtype=jnp.int32)[:, None] == material[None, :]
    ).astype(jnp.float32)
    albedo = jnp.dot(reflect, class_hot, precision=lax.Precision.HIGHEST)
    albedo = albedo.reshape(band_count, local_blocks, BLK).transpose(1, 0, 2)
    source = emission.reshape(band_count, local_blocks, BLK).transpose(1, 0, 2)
    area_blocks = geometry[:, 6, :]
    current = source
    for sweep_index in range(SWEEPS):
        scaled = (current * area_blocks[:, None, :]).astype(jnp.bfloat16)
        lent_values = scaled[asked_for]
        kernel = view_tile(near_geometry, far_geometry).astype(jnp.bfloat16)
        incoming = lax.all_to_all(
            lent_values, ("grp", "dev"), split_axis=0, concat_axis=0, tiled=True
        )
        to_near = jnp.einsum(
            "pnj,pij->pni", incoming[slot_index], kernel, preferred_element_type=jnp.float32
        )
        to_far = jnp.einsum(
            "pni,pij->pnj", scaled[pair_local], kernel, preferred_element_type=jnp.float32
        )
        replies = jnp.zeros((slot_total, band_count, BLK), jnp.float32).at[slot_index].set(to_far)
        returned = lax.all_to_all(replies, ("grp", "dev"), split_axis=0, concat_axis=0, tiled=True)
        gathered = jnp.einsum("pb,pnk->bnk", local_hot, to_near, precision=lax.Precision.HIGHEST)
        gathered = gathered + jnp.einsum(
            "sb,snk->bnk", asked_hot, returned, precision=lax.Precision.HIGHEST
        )
        current = source + albedo * gathered
    return current.transpose(1, 0, 2).reshape(band_count, patch_count)


def torus_order():
    seen = set()
    groups = []
    for dx in range(4):
        for dy in range(4):
            for dz in range(4):
                for core in range(2):
                    group = []
                    for x, y, z in ((dx, dy, dz), (dy, dz, dx), (dz, dx, dy)):
                        for step in ((x, core, y, z), (-x % 4, core, -y % 4, -z % 4)):
                            if step not in seen and any(step):
                                seen.add(step)
                                group.append(step)
                    if group:
                        groups.append(group)
    groups.sort(key=lambda group: sum(min(v, 4 - v) for v in group[0][:1] + group[0][2:]))
    return [step for group in groups for step in group]


ORDER = torus_order()
PEERS = len(ORDER)


def peer(grp, dev, step):
    x, core, y, z = step
    return (
        lax.rem(grp // 2 + x, 4) * 2 + lax.rem(lax.rem(grp, 2) + core, 2),
        lax.rem(dev // 4 + y, 4) * 4 + lax.rem(lax.rem(dev, 4) + z, 4),
    )


def opposite(step):
    x, core, y, z = step
    return (-x % 4, core, -y % 4, -z % 4)


BACK = [ORDER.index(opposite(step)) for step in ORDER] + [PEERS]


TURNS = [list(range(PEERS)), [ORDER.index((y, core, z, x)) for x, core, y, z in ORDER]]


def across(row):
    return jnp.broadcast_to(row, (BLK, BLK))


def down(row):
    return jnp.broadcast_to(row, (BLK, BLK)).T


def column_sum(terms):
    return jnp.sum(terms, 0, keepdims=True)


def sort_rows(mine, names, lane):
    lane_row = lane[:1]
    key = mine * BLK + lane_row
    rank = column_sum(jnp.where(down(key) < across(key), 1.0, 0.0))
    at_rank = down(rank) == lane
    order = column_sum(jnp.where(at_rank, names, 0.0))
    mine_down = down(mine)
    sorted_mine = column_sum(jnp.where(at_rank, mine_down, 0.0))
    before = pltpu.roll(jnp.broadcast_to(sorted_mine, (8, BLK)), 1, 1)[:1]
    keep = jnp.where((sorted_mine == before) & (lane_row > 0), 1.0, 0.0)
    upto = column_sum(jnp.where(mine_down <= lane, 1.0, 0.0))
    has = column_sum(jnp.where(mine_down == lane, 1.0, 0.0))
    return [order, keep, jnp.maximum(upto - 1.0, 0.0), jnp.minimum(has, 1.0)]


def iotas():
    row = lax.broadcasted_iota(jnp.int32, (BLK, BLK), 0)
    lane = lax.broadcasted_iota(jnp.int32, (BLK, BLK), 1)
    return row, lane


def name_rows(grp, dev, steps, target, code):
    row, lane = iotas()

    def ids(first):
        x, core, y, z = (steps[first + part : first + part + 1] for part in range(4))
        x, core = (x + grp // 2) & 3, (core + lax.rem(grp, 2)) & 1
        y, z = (y + dev // 4) & 3, (z + lax.rem(dev, 4)) & 3
        return ((x * 2 + core) * 16 + y * 4 + z).astype(jnp.float32)

    there, here = ids(0), ids(4)
    target, code = target.astype(jnp.float32), code.astype(jnp.float32)
    target_down, code_down = down(target), down(code)
    earlier = (target_down == across(target)) & (row < lane)
    second = jnp.max(jnp.where(earlier, 1.0, 0.0), 0, keepdims=True)
    second_down = down(second)

    def named(ids, which):
        found = (target_down == across(ids)) & (second_down == which)
        return jnp.max(jnp.where(found, code_down, -1.0), 0, keepdims=True)

    rows = [named(there, 0.0), named(there, 1.0), named(here, 0.0), named(here, 1.0), here]
    return jnp.concatenate(rows + [jnp.zeros((3, BLK), jnp.float32)], 0).astype(jnp.int32)


def route(asked, owned, out):
    row, lane = iotas()
    lane_row = lane[:1]
    lane = lane.astype(jnp.float32)
    asked0, asked1, owned0, owned1 = asked[0:1], asked[1:2], owned[0:1], owned[1:2]
    owned_mine = owned1 & (BLOCKS - 1)
    first_near = jnp.where(asked0 >= 0, asked0 >> 5, BLOCKS)
    first_far = jnp.where(owned0 >= 0, owned0 & (BLOCKS - 1), BLOCKS)
    second = jnp.where(asked1 >= 0, asked1 >> 5, jnp.where(owned1 >= 0, owned_mine, BLOCKS))

    def shifted(values, lanes):
        return pltpu.roll(jnp.broadcast_to(values, (8, BLK)), lanes % BLK, 1)[:1]

    low = lane_row < PLACES
    paired = ((row % PLACES) * 2 + row // PLACES).astype(jnp.float32)
    single = row.astype(jnp.float32)
    for half in range(HALVES):
        shift = -half * PLACES
        both = jnp.where(low, shifted(first_near, shift), shifted(first_far, shift + PLACES))
        last = jnp.where(low, shifted(second, shift), BLOCKS)
        for table, mine, names in ((half, both, paired), (HALVES + half, last, single)):
            mine = mine.astype(jnp.float32)
            rows = sort_rows(mine, names, lane)
            rows += [jnp.minimum(mine, BLOCKS - 1.0), jnp.zeros((3, BLK), jnp.float32)]
            out[table * 8 : table * 8 + 8] = jnp.concatenate(rows, 0).astype(jnp.int32)
    asked_first = jnp.where(asked0 >= 0, asked0 >> 5, 0)
    asked_second = jnp.where(asked1 >= 0, asked1 >> 5, 0)
    both = (owned1 >= 0) & (asked1 >= 0)
    crowded = jnp.max(jnp.where(both, 1.0, 0.0), 1, keepdims=True)
    out[MISC : MISC + 8] = jnp.concatenate(
        [
            asked_first,
            asked_second,
            jnp.where(owned1 >= 0, owned_mine, asked_second),
            (asked1 >= 0).astype(jnp.int32),
            jnp.broadcast_to(crowded, (1, BLK)).astype(jnp.int32),
            jnp.zeros((3, BLK), jnp.int32),
        ],
        0,
    )


def route_rest(crowded, asked, owned, relay_shift, out):
    row, lane = iotas()
    lane = lane.astype(jnp.float32)
    lane_row = lane[:1]
    asked1, owned1 = asked[1:2], owned[1:2]
    ids = owned[2:3].astype(jnp.float32)
    rank = column_sum(jnp.where(down(ids) < across(ids), down(crowded), 0.0))
    rank_down = down(rank)
    hot_down = down(crowded) > 0.5
    my_rank = jnp.sum(jnp.where(lane_row == PEERS, rank, 0.0), 1, keepdims=True)
    count = jnp.sum(crowded, 1, keepdims=True)

    def pick(wanted, terms):
        wanted = jnp.where(wanted >= RANKS, wanted - RANKS, wanted)
        wanted = jnp.where(wanted < 0, wanted + RANKS, wanted)
        return column_sum(jnp.where(hot_down & (rank_down == across(wanted)), terms, 0.0))

    ahead = my_rank + lane_row
    behind = my_rank - lane_row
    asked_second = jnp.where(asked1 >= 0, asked1 >> 5, 0).astype(jnp.float32)
    both = (owned1 >= 0) & (asked1 >= 0)
    mine = jnp.where(both, owned1 & (BLOCKS - 1), BLOCKS).astype(jnp.float32)
    places = row.astype(jnp.float32)
    lend = pick(ahead, down(asked_second))
    source = pick(behind, places)
    found = pick(behind, jnp.ones((BLK, BLK), jnp.float32))
    mine = jnp.where((lane_row < RANKS) & (found > 0.5), pick(behind, down(mine)), float(BLOCKS))
    relay = pick(rank - relay_shift, places)
    rows = sort_rows(mine, places, lane)
    lend = jnp.where(lane_row == BLK - 1, count, lend)
    rows += [jnp.minimum(mine, BLOCKS - 1.0), lend, source, relay]
    out[...] = jnp.concatenate(rows, 0).astype(jnp.int32)


def with_norms(rows, extra):
    points, normals = rows[0:3], rows[3:6]
    square = points * points
    product = points * normals
    return jnp.concatenate(
        [
            rows[0:6],
            square[0:1] + square[1:2] + square[2:3] + extra,
            -(product[0:1] + product[1:2] + product[2:3]),
        ],
        0,
    )


def split(values):
    high = values.astype(jnp.bfloat16).astype(jnp.float32)
    rest = values - high
    middle = rest.astype(jnp.bfloat16).astype(jnp.float32)
    return high, middle, rest - middle


def other_features(rows):
    high, middle, low = split(with_norms(rows, softening))
    ones = jnp.where(lax.broadcasted_iota(jnp.int32, (8, BLK), 0) < 3, 1.0, 0.0)
    parts = [high, high, middle, middle, high, low, ones, jnp.zeros((8, BLK), jnp.float32)]
    return jnp.concatenate(parts, 0).T.astype(jnp.bfloat16)


def own_features(rows):
    pieces = split(with_norms(rows, 0.0))
    zero = jnp.zeros((1, BLK), jnp.float32)
    zeros3 = jnp.zeros((3, BLK), jnp.float32)
    columns = ([], [], [])
    for which in (0, 1, 0, 1, 2, 0):
        part = pieces[which]
        one = zero + 1.0 if which == 0 else zero
        columns[0].append(jnp.concatenate([part[3:6], zeros3, zero, zero], 0))
        columns[1].append(jnp.concatenate([zeros3, part[0:3], zero, one], 0))
        columns[2].append(jnp.concatenate([-2.0 * part[0:3], zeros3, one, zero], 0))
    tail = jnp.zeros((5, BLK), jnp.float32)
    blank = jnp.zeros((8, BLK), jnp.float32)
    for column, row in ((0, 7), (1, None), (2, 6)):
        if row is None:
            columns[column].append(blank)
        else:
            columns[column].append(
                jnp.concatenate([part[row : row + 1] for part in pieces] + [tail], 0)
            )
        columns[column].append(blank)
    return [jnp.concatenate(column, 0).astype(jnp.bfloat16) for column in columns]


def tile(rows, own):
    forms = jnp.dot(other_features(rows), own, preferred_element_type=jnp.float32)
    facing = jnp.maximum(forms[:, :BLK], 0.0) * jnp.maximum(forms[:, BLK : 2 * BLK], 0.0)
    distance_sq = forms[:, 2 * BLK :]
    bottom = math.pi * distance_sq * distance_sq
    inverse = pl.reciprocal(bottom, approx=True)
    inverse = inverse * (2.0 - bottom * inverse)
    return (facing * inverse).astype(jnp.bfloat16)


def fused_kernel(
    steps,
    target,
    pair_block,
    pair_local,
    emission,
    areas,
    material,
    reflect,
    positions,
    normals,
    out,
    fits,
    name_table,
    names,
    geometry,
    features,
    albedo,
    classes,
    scaled,
    total,
    running,
    send,
    last_send,
    near_send,
    near_recv,
    far_send,
    far_recv,
    asked_rows,
    table_rows,
    table,
    rest_rows,
    rest,
    tiles0,
    tiles1,
    last_tiles0,
    last_tiles1,
    recv00,
    recv01,
    recv10,
    recv11,
    last_recv00,
    last_recv01,
    last_recv10,
    last_recv11,
    lend_send,
    lend_recv0,
    lend_recv1,
    relay_send,
    relay_recv0,
    relay_recv1,
    rest_tiles,
    rest_values,
    send_sem,
    recv_sem,
    table_sem,
):
    tiles = (tiles0, tiles1)
    last_tiles = (last_tiles0, last_tiles1)
    recv = ((recv00, recv01), (recv10, recv11))
    last_recv = ((last_recv00, last_recv01), (last_recv10, last_recv11))
    lend_recv = (lend_recv0, lend_recv1)
    relay_recv = (relay_recv0, relay_recv1)
    grp, dev = lax.axis_index("grp"), lax.axis_index("dev")
    core = lax.rem(grp, 2)
    chip = (grp // 2) * 16 + dev
    peers = [peer(grp, dev, step) for step in ORDER]
    barrier = pltpu.get_barrier_semaphore()
    for other in peers:
        pl.semaphore_signal(barrier, inc=1, device_id=other, device_id_type=MESH)

    def describe(kind, source, target, halves=True):
        return [
            pltpu.make_async_remote_copy(
                src_ref=source(place),
                dst_ref=target(place),
                send_sem=send_sem.at[kind],
                recv_sem=recv_sem.at[kind * 2 + (place // PLACES if halves else 0)],
                device_id=other,
                device_id_type=MESH,
            )
            for place, other in enumerate(peers)
        ]

    def all_of(kind, ref, half=0):
        return pltpu.make_async_remote_copy(
            src_ref=ref,
            dst_ref=ref,
            send_sem=send_sem.at[kind],
            recv_sem=recv_sem.at[kind * 2 + half],
            device_id=peers[0],
            device_id_type=MESH,
        )

    def start(copies, first=0, count=PEERS):
        for turn in range(2):

            @pl.when(core == turn)
            def _():
                for place in TURNS[turn][first : first + count]:
                    copies[place].start()

    def exchange(kind, source, target, halves=True):
        start(describe(kind, source, target, halves))

    def came(kind, ref, half, each):
        count = (PLACES if half == 0 else PLACES - 1) * each
        all_of(kind, ref.at[pl.ds(0, count)], half).wait_recv()

    def left(kind, ref, count):
        all_of(kind, ref.at[pl.ds(0, count)]).wait_send()

    def firsts(sweep, first, count):
        def source(place):
            return send.at[pl.ds(place * 2 + first, count)]

        def target(place):
            half = recv[sweep][place // PLACES]
            return half.at[pl.ds(place % PLACES * 2 + first, count)]

        return source, target

    def lasts(sweep):
        def target(place):
            return last_recv[sweep][place // PLACES].at[place % PLACES]

        return lambda place: last_send.at[place], target

    def at_places(act):
        def step(group, _):
            for inner in range(8):
                act(group * 8 + inner)
            return 0

        lax.fori_loop(0, DEVICES // 8, step, 0)

    def near_index(place, slot):
        return names[slot, place] & (BLOCKS - 1)

    def sent(row, place):
        return table[MISC + row, BACK[place]] & (BLOCKS - 1)

    def pack_near_values():
        def pack(place):
            send[place * 2] = scaled[near_index(place, 0)]

        at_places(pack)

    def pack_far_values():
        for place in range(DEVICES):
            send[place * 2 + 1] = scaled[sent(0, place)]

    def pack_last_values(sweep):
        for place in range(DEVICES):
            last_send[place] = scaled[sent(2, place)]
        last_recv[sweep][1][PLACES - 1] = last_send[PEERS]

    def keep_own(sweep):
        for slot in range(2):
            recv[sweep][1][PLACES * 2 - 2 + slot] = send[PEERS * 2 + slot]

    sides = [[place for place in range(PEERS) if ORDER[place][1] == side] for side in range(2)]

    def on_core(side, act):
        @pl.when(core == side)
        def _():
            act()

    def lend(sweep):
        for apart in range(RANKS):
            block = scaled[rest[5, apart] & (BLOCKS - 1)]
            for piece in range(PIECES):
                lend_send[apart * PIECES + piece] = block[piece * ROWS : (piece + 1) * ROWS]
        lend_recv[sweep][PEERS] = lend_send[chip]
        copies = describe(
            7 + sweep,
            lambda place: lend_send.at[(peers[place][0] // 2) * 16 + peers[place][1]],
            lambda place: lend_recv[sweep].at[place],
            False,
        )
        for side in range(2):
            on_core(side, lambda: [copies[place].start() for place in sides[side]] and None)

    def pass_on(sweep):
        copies = describe(
            9 + sweep,
            lambda place: relay_send.at[place],
            lambda place: relay_recv[sweep].at[chip],
            False,
        )

        @pl.when(core == 0)
        def _():
            all_of(7 + sweep, lend_recv[sweep].at[pl.ds(0, PEERS)]).wait_recv()
            for place in range(DEVICES):
                relay_send[place] = lend_recv[sweep][rest[7, BACK[place]] & (DEVICES - 1)]
            relay_recv[sweep][chip] = relay_send[PEERS]
            for place in range(PEERS):
                copies[place].start()

    def passed_came(sweep):
        for side in range(2):
            pieces = relay_recv[sweep].at[pl.ds(0, len(sides[side]))]
            on_core(side, lambda: all_of(9 + sweep, pieces).wait_recv())

    def rest_left(sweep):
        for side in range(2):
            on_core(side, lambda: left(7 + sweep, lend_send, len(sides[side])))
        on_core(0, lambda: left(9 + sweep, relay_send, PEERS))

    code = pair_block[...] * BLOCKS + pair_local[...]
    name_table[...] = name_rows(grp, dev, steps[...], target[...], code)
    to_names = pltpu.make_async_copy(name_table, names, table_sem.at[2])
    to_names.start()

    for block in range(BLOCKS):
        lanes = pl.ds(block * BLK, BLK)
        geometry[block] = jnp.concatenate(
            [positions[:, lanes], normals[:, lanes], jnp.zeros((2, BLK), jnp.float32)], 0
        )
    to_names.wait()
    lane = lax.broadcasted_iota(jnp.int32, (4, BLK), 1)

    def pack_near(place):
        first, second = names[0, place], names[1, place]
        codes = jnp.where(lane == 0, first, jnp.where(lane == 1, second, 0)).astype(jnp.float32)
        rows = [geometry[near_index(place, slot)][:6] for slot in range(2)]
        near_send[place] = jnp.concatenate(rows + [codes], 0)

    at_places(pack_near)
    near_recv[PEERS] = near_send[PEERS]
    pl.semaphore_wait(barrier, PEERS)
    exchange(0, lambda place: near_send.at[place], lambda place: near_recv.at[place], False)
    for block in range(BLOCKS):
        lanes = pl.ds(block * BLK, BLK)
        scaled[block] = (emission[:, lanes] * areas[:, lanes]).astype(jnp.bfloat16)
    pack_near_values()
    exchange(2, *firsts(0, 0, 1))

    by_band = jnp.concatenate([reflect[...], jnp.zeros_like(reflect[...])], 1).T[:BANDS]
    for which in range(classes.shape[0]):
        classes[which] = jnp.broadcast_to(by_band[:, which : which + 1], (BANDS, BLK))
    for block in range(BLOCKS):
        lanes = pl.ds(block * BLK, BLK)
        row = material[:, lanes]
        part = classes[0]
        for which in range(1, classes.shape[0]):
            part = jnp.where(row == which, classes[which], part)
        albedo[:, lanes] = part

    def build_features(block, _):
        for index, column in enumerate(own_features(geometry[block])):
            features[block, :, index * BLK : (index + 1) * BLK] = column
        return 0

    lax.fori_loop(0, BLOCKS, build_features, 0)

    all_of(0, near_recv.at[pl.ds(0, PEERS)]).wait_recv()

    def collect_asked(place):
        asked_rows[pl.ds(place, 1)] = near_recv[place, 12:13]

    at_places(collect_asked)
    asked = asked_rows[...].T[:8].astype(jnp.int32)
    route(asked, name_table[2:5], table_rows)
    to_table = pltpu.make_async_copy(table_rows, table, table_sem.at[0])
    to_table.start()
    to_table.wait()

    crowded_row = table_rows[MISC + 4 : MISC + 5].astype(jnp.float32)
    blank = jnp.zeros((3, BLK), jnp.float32)
    for place in range(DEVICES):
        rows = [geometry[sent(slot, place)][:6] for slot in range(2)]
        far_send[place] = jnp.concatenate(rows + [crowded_row, blank], 0)
    far_recv[PEERS] = far_send[PEERS]
    exchange(1, lambda place: far_send.at[place], lambda place: far_recv.at[place], False)
    pack_far_values()
    keep_own(0)
    exchange(3, *firsts(0, 1, 1))
    pack_last_values(0)
    last_copies = describe(4, *lasts(0))
    start(last_copies, 0, PLACES)

    def own_side(group, task):
        return features[table[group * 8 + 4, task] & (BLOCKS - 1)]

    def build(source, slot, half):
        def step(pair, _):
            for inner in range(2):
                place = pair * 2 + inner
                rows = source[half * PLACES + place][:6]
                tiles[half][place * 2 + slot] = tile(rows, own_side(half, slot * PLACES + place))
            return 0

        lax.fori_loop(0, PLACES // 2, step, 0)

    for half in range(HALVES):
        build(near_recv, 0, half)

    all_of(1, far_recv.at[pl.ds(0, PEERS)]).wait_recv()

    def collect_crowded(place):
        asked_rows[pl.ds(place, 1)] = far_recv[place, 12:13]

    at_places(collect_crowded)
    crowded = asked_rows[...].T[:1]
    shift = (chip // PIECES).astype(jnp.float32)
    route_rest(crowded, asked, name_table[2:5], shift, rest_rows)
    to_rest = pltpu.make_async_copy(rest_rows, rest, table_sem.at[1])
    to_rest.start()
    to_rest.wait()
    fits[0, 0] = rest[5, BLK - 1]
    lend(0)
    start(last_copies, PLACES, PEERS - PLACES)

    for half in range(HALVES):
        build(far_recv, 1, half)
    pass_on(0)

    for half in range(HALVES):

        def build_last(pair, _):
            for inner in range(2):
                place = pair * 2 + inner
                whole = half * PLACES + place
                near = table[MISC + 3, whole] > 0
                rows = jnp.where(near, near_recv[whole], far_recv[whole])[6:12]
                last_tiles[half][place] = tile(rows, own_side(HALVES + half, place))
            return 0

        lax.fori_loop(0, PLACES // 2, build_last, 0)

    def build_rest(apart, _):
        rows = far_recv[rest[6, apart] & (DEVICES - 1)][6:12]
        rest_tiles[apart] = tile(rows, features[rest[4, apart] & (BLOCKS - 1)])
        return 0

    lax.fori_loop(0, RANKS, build_rest, 0)

    def accumulate(values_ref, tiles_ref, rows, base, first):
        tasks = values_ref.shape[0]

        def add(group, run):
            for inner in range(8):
                task = group * 8 + inner
                index = rows[base, task] & (tasks - 1)
                run = run * rows[base + 1, task].astype(jnp.float32) + jnp.dot(
                    values_ref[index], tiles_ref[index], preferred_element_type=jnp.float32
                )
                running[task] = run
            return run

        lax.fori_loop(0, tasks // 8, add, jnp.zeros((BANDS, BLK), jnp.float32))

        def fold(block, _):
            part = running[rows[base + 2, block] & (tasks - 1)]
            part = part * rows[base + 3, block].astype(jnp.float32)
            total[block] = part if first else total[block] + part
            return 0

        lax.fori_loop(0, BLOCKS, fold, 0)

    for sweep in range(SWEEPS):
        if sweep == 0:
            rounds = ((2, 1), (3, 1))
        else:
            rounds = ((5, 2),)
            lend(1)
            pack_near_values()
            pack_far_values()
            exchange(5, *firsts(1, 0, 2))
            keep_own(1)
            pack_last_values(1)
            pass_on(1)
            exchange(6, *lasts(1))

        for half in range(HALVES):
            for kind, each in rounds:
                came(kind, recv[sweep][half], half, each)
            accumulate(recv[sweep][half], tiles[half], table, half * 8, half == 0)
        for kind, each in rounds:
            left(kind, send, PEERS * each)

        passed_came(sweep)
        for apart in range(RANKS):
            for piece in range(PIECES):
                rest_values[apart, piece * ROWS : (piece + 1) * ROWS] = relay_recv[sweep][
                    apart * PIECES + piece
                ]
        accumulate(rest_values, rest_tiles, rest, 0, False)
        rest_left(sweep)
        if sweep == 0:
            left(0, near_send, PEERS)
            left(1, far_send, PEERS)

        for half in range(HALVES):
            came(4 + 2 * sweep, last_recv[sweep][half], half, 1)
            accumulate(
                last_recv[sweep][half], last_tiles[half], table, (HALVES + half) * 8, False
            )
        left(4 + 2 * sweep, last_send, PEERS)

        for block in range(BLOCKS):
            lanes = pl.ds(block * BLK, BLK)
            reflected = albedo[:, lanes] * total[block]
            if sweep + 1 < SWEEPS:
                current = emission[:, lanes] + reflected
                scaled[block] = (current * areas[:, lanes]).astype(jnp.bfloat16)
            else:
                out[:, lanes] = reflected


def fused(steps, target, pair_block, pair_local, emission, areas, material, reflect, positions, normals):
    smem = pl.BlockSpec(memory_space=pltpu.SMEM)
    vmem = pl.BlockSpec(memory_space=pltpu.VMEM)
    values = pltpu.VMEM((PLACES * 2, BANDS, BLK), jnp.bfloat16)
    last_values = pltpu.VMEM((PLACES, BANDS, BLK), jnp.bfloat16)
    tiles = pltpu.VMEM((PLACES * 2, BLK, BLK), jnp.bfloat16)
    last_tiles = pltpu.VMEM((PLACES, BLK, BLK), jnp.bfloat16)
    message = pltpu.VMEM((DEVICES, 16, BLK), jnp.float32)
    lent = pltpu.VMEM((DEVICES, ROWS, BLK), jnp.bfloat16)
    passed = pltpu.VMEM((RELAYS, ROWS, BLK), jnp.bfloat16)
    return pl.pallas_call(
        fused_kernel,
        in_specs=[vmem] * 10,
        out_specs=[vmem, smem],
        out_shape=[
            jax.ShapeDtypeStruct(emission.shape, jnp.float32),
            jax.ShapeDtypeStruct((1, 1), jnp.int32),
        ],
        scratch_shapes=[
            pltpu.VMEM((8, BLK), jnp.int32),
            pltpu.SMEM((8, BLK), jnp.int32),
            pltpu.VMEM((BLOCKS, 8, BLK), jnp.float32),
            pltpu.VMEM((BLOCKS, FEATURES, 3 * BLK), jnp.bfloat16),
            pltpu.VMEM(emission.shape, jnp.float32),
            pltpu.VMEM((reflect.shape[0], BANDS, BLK), jnp.float32),
            pltpu.VMEM((BLOCKS, BANDS, BLK), jnp.bfloat16),
            pltpu.VMEM((BLOCKS, BANDS, BLK), jnp.float32),
            pltpu.VMEM((PLACES * 2, BANDS, BLK), jnp.float32),
            pltpu.VMEM((DEVICES * 2, BANDS, BLK), jnp.bfloat16),
            pltpu.VMEM((DEVICES, BANDS, BLK), jnp.bfloat16),
            message,
            message,
            message,
            message,
            pltpu.VMEM((DEVICES, BLK), jnp.float32),
            pltpu.VMEM((MISC + 8, BLK), jnp.int32),
            pltpu.SMEM((MISC + 8, BLK), jnp.int32),
            pltpu.VMEM((8, BLK), jnp.int32),
            pltpu.SMEM((8, BLK), jnp.int32),
        ]
        + [tiles] * HALVES
        + [last_tiles] * HALVES
        + [values] * (SWEEPS * HALVES)
        + [last_values] * (SWEEPS * HALVES)
        + [passed, lent, lent, lent, passed, passed]
        + [
            pltpu.VMEM((RANKS, BLK, BLK), jnp.bfloat16),
            pltpu.VMEM((RANKS, BANDS, BLK), jnp.bfloat16),
            pltpu.SemaphoreType.DMA((11,)),
            pltpu.SemaphoreType.DMA((22,)),
            pltpu.SemaphoreType.DMA((3,)),
        ],
        compiler_params=pltpu.CompilerParams(
            collective_id=0, has_side_effects=True, vmem_limit_bytes=62 << 20
        ),
        name="fused",
    )(
        steps,
        target,
        pair_block,
        pair_local,
        emission,
        areas,
        material,
        reflect,
        positions,
        normals,
    )


def on_device(
    emission, positions, normals, areas, material, reflect, pair_local, pair_device, pair_block
):
    steps = ORDER + [(0, 0, 0, 0)]
    steps = np.array([step + opposite(step) for step in steps], np.int32).T
    reflected, crowded = fused(
        jnp.asarray(steps),
        pair_device.reshape(1, -1),
        pair_block[None, :],
        pair_local[None, :],
        emission,
        areas[None, :],
        material[None, :],
        reflect.T,
        positions,
        normals,
    )
    return lax.cond(
        crowded[0, 0] <= RANKS,
        lambda: emission + reflected,
        lambda: general(
            emission,
            positions,
            normals,
            areas,
            material,
            reflect,
            pair_local,
            pair_device,
            pair_block,
        ),
    )


def solution(mesh):
    return jax.shard_map(
        on_device,
        mesh=mesh,
        in_specs=(
            P(None, AXES),
            P(None, AXES),
            P(None, AXES),
            P(AXES),
            P(AXES),
            P(),
            P(AXES),
            P(AXES, None),
            P(AXES),
        ),
        out_specs=P(None, AXES),
        check_vma=False,
    )
```
